32 devices in a mesh: lat: 16 (over z, y, core), lon: 2 (over x).
Axes of the slice: x: 2, y: 2, z: 4, core: 2. Of those that a mesh axis runs over, the one named last changes fastest.
Arguments:
- inputs: float32 [2, 64, 128, 641], P(None, 'lat', 'lon'), may hold values from -6 to 6
- noise_field: float32 [2, 64, 128, 8], P(None, 'lat', 'lon'), may hold values from -6 to 6
- basis_values: float32 [64, 7, 5, 9], P('lat'), may hold values from -1.2 to 1.2
- row_reach: int32 [64], P('lat'), may hold values from 1 to 4, as said below
- conv_weight: float32 [7, 649, 641], replicated, may hold values from -0.09375 to 0.09375
- conv_bias: float32 [641], replicated, may hold values from -1.5 to 1.5
- first_gain: float32 [641], replicated, may hold values from 0.25 to 1.75
- first_shift: float32 [641], replicated, may hold values from -1.5 to 1.5
- second_gain: float32 [641], replicated, may hold values from 0.25 to 1.75
- second_shift: float32 [641], replicated, may hold values from -1.5 to 1.5
- hidden_weight: float32 [641, 1282], replicated, may hold values from -0.25 to 0.25
- hidden_bias: float32 [1282], replicated, may hold values from -1.5 to 1.5
- output_weight: float32 [1282, 641], replicated, may hold values from -0.15625 to 0.15625
- output_bias: float32 [641], replicated, may hold values from -1.5 to 1.5
- cotangent: float32 [2, 64, 128, 641], P(None, 'lat', 'lon'), may hold values from -6 to 6
Outputs:
- block_output: float32 [2, 64, 128, 641], P(None, 'lat', 'lon')
- input_grad: float32 [2, 64, 128, 641], P(None, 'lat', 'lon')
- conv_weight_grad: float32 [7, 649, 641], replicated
- conv_bias_grad: float32 [641], replicated
- first_gain_grad: float32 [641], replicated
- first_shift_grad: float32 [641], replicated
- second_gain_grad: float32 [641], replicated
- second_shift_grad: float32 [641], replicated
- hidden_weight_grad: float32 [641, 1282], replicated
- hidden_bias_grad: float32 [1282], replicated
- output_weight_grad: float32 [1282, 641], replicated
- output_bias_grad: float32 [641], replicated
The draws below stay inside these ranges and needn't reach their ends.
Inputs may be any that keep to these rules, and one draw needn't show every extreme that they name: `row_reach`: some row has reach 4.
All inputs are finite; a program needn't handle non-finite values.
Results may differ from the reference program's by a relative error of at most 0.0003.
Values sent between devices are 32-bit elements; how exact they have to be, the bound alone decides.
No kernel may reach another device: no remote copies, remote signals or barrier semaphores. Data moves between devices by JAX's collectives and lax.ppermute only.
A program may use at most 192 MiB of HBM per device.

```python
import jax
import jax.numpy as jnp
from jax import lax

CHANNELS = 641
NOISE_CH = 8
HIDDEN_SIZE = 1282
NBASIS = 7
LAT_HALO = 2
LON_HALO = 4
SAMPLES = 2
NLAT = 64
NLON = 128


def draw_row_reach(key, part):
    key = jax.random.fold_in(key, 7)
    value_key, place_key = jax.random.split(key)
    values = jax.random.randint(value_key, (NLAT,), 1, LON_HALO + 1)
    chosen = jax.random.randint(place_key, (), 0, NLAT)
    return jnp.where(jnp.arange(NLAT) == chosen, LON_HALO, values).astype(jnp.int32)


def shard_levels(stream_key, extent, cuts, least, largest):
    level, own = 1.0, jax.random.fold_in(stream_key, 6)
    for dim, parts in cuts:
        heights = jnp.exp(jax.random.uniform(jax.random.fold_in(own, dim), (parts,), jnp.float32, least / len(cuts), largest / len(cuts)))
        level = level * jnp.repeat(heights, extent[dim] // parts).reshape([-1 if axis == dim else 1 for axis in range(len(extent))])
    return level


def noise(stream_key, extent, spread, limit, cuts=(), held_as=jnp.bfloat16):
    values = jax.random.normal(stream_key, extent, jnp.float32) * spread
    if len(cuts) > 0:
        values = shard_levels(stream_key, extent, cuts, -0.22, 0.18) * values
    return jnp.clip(values, min=-limit, max=limit).astype(held_as)


def setup_inputs(seed: int = 0) -> dict:
    keys = jax.random.split(jax.random.key(seed), 16)
    inputs = noise(keys[0], (SAMPLES, NLAT, NLON, CHANNELS), 1.0, 6.0, ((1, 16), (2, 2)), jnp.float32)
    noise_field = noise(keys[1], (SAMPLES, NLAT, NLON, NOISE_CH), 1.0, 6.0, ((1, 16), (2, 2)), jnp.float32)
    basis_values = noise(keys[2], (NLAT, NBASIS, 2 * LAT_HALO + 1, 2 * LON_HALO + 1), 0.2, 1.2, ((0, 16),), jnp.float32)
    row_reach = draw_row_reach(jax.random.fold_in(keys[15], 71), 0)
    conv_weight = noise(keys[4], (NBASIS, CHANNELS + NOISE_CH, CHANNELS), (NBASIS * (CHANNELS + NOISE_CH)) ** -0.5, 0.09375, (), jnp.float32)
    conv_bias = noise(keys[5], (CHANNELS,), 0.3, 1.5, (), jnp.float32)
    first_gain = jnp.clip(1.0 + 0.15 * jax.random.normal(keys[6], (CHANNELS,), jnp.float32), 0.25, 1.75)
    first_shift = noise(keys[7], (CHANNELS,), 0.3, 1.5, (), jnp.float32)
    second_gain = jnp.clip(1.0 + 0.15 * jax.random.normal(keys[8], (CHANNELS,), jnp.float32), 0.25, 1.75)
    second_shift = noise(keys[9], (CHANNELS,), 0.3, 1.5, (), jnp.float32)
    hidden_weight = noise(keys[10], (CHANNELS, HIDDEN_SIZE), CHANNELS ** -0.5, 0.25, (), jnp.float32)
    hidden_bias = noise(keys[11], (HIDDEN_SIZE,), 0.3, 1.5, (), jnp.float32)
    output_weight = noise(keys[12], (HIDDEN_SIZE, CHANNELS), HIDDEN_SIZE ** -0.5, 0.15625, (), jnp.float32)
    output_bias = noise(keys[13], (CHANNELS,), 0.3, 1.5, (), jnp.float32)
    cotangent = noise(keys[14], (SAMPLES, NLAT, NLON, CHANNELS), 1.0, 6.0, ((1, 16), (2, 2)), jnp.float32)
    return {"inputs": inputs, "noise_field": noise_field, "basis_values": basis_values, "row_reach": row_reach, "conv_weight": conv_weight, "conv_bias": conv_bias, "first_gain": first_gain, "first_shift": first_shift, "second_gain": second_gain, "second_shift": second_shift, "hidden_weight": hidden_weight, "hidden_bias": hidden_bias, "output_weight": output_weight, "output_bias": output_bias, "cotangent": cotangent}


@jax.custom_vjp
def low(v):
    return lax.optimization_barrier(v.astype(jnp.bfloat16)).astype(jnp.float32)

@jax.custom_vjp
def low_back(v):
    return v

def low_keep(v):
    return (low(v), None)

def low_pass(kept, grad):
    return (grad,)

def back_keep(v):
    return (v, None)

def back_low(kept, grad):
    return (low(grad),)
low.defvjp(low_keep, low_pass)
low_back.defvjp(back_keep, back_low)
HIGHEST = lax.Precision.HIGHEST
EPSILON = 1e-05

def layer_norm(field, gain, shift):
    average = lax.optimization_barrier(jnp.mean(field, axis=-1, keepdims=True))
    centered = field - average
    variance = lax.optimization_barrier(jnp.mean(centered * centered, axis=-1, keepdims=True))
    return centered * lax.rsqrt(variance + EPSILON) * gain + shift

def banded_table(basis_values, row_reach):
    offsets = jnp.arange(2 * LON_HALO + 1, dtype=jnp.int32) - LON_HALO
    allowed = (jnp.abs(offsets)[None, :] <= row_reach[:, None]).astype(jnp.float32)
    masked = basis_values * allowed[:, None, None, :]
    source = jnp.arange(NLON, dtype=jnp.int32)
    target = jnp.arange(NLON, dtype=jnp.int32)
    distance = (source[None, :, None] - target[None, None, :] - offsets[:, None, None]) % NLON
    onehot = (distance == 0).astype(jnp.float32)
    return jnp.einsum('hkdj,jvw->hkdvw', masked, onehot, precision=HIGHEST)

def forward(inputs, conv_weight, conv_bias, first_gain, first_shift, second_gain, second_shift, hidden_weight, hidden_bias, output_weight, output_bias, noise_field, basis_values, row_reach):
    banded = banded_table(basis_values, row_reach)
    normed = layer_norm(inputs, first_gain, first_shift)
    joined = jnp.concatenate([normed, noise_field], axis=-1)
    padded = jnp.pad(joined, ((0, 0), (LAT_HALO, LAT_HALO), (0, 0), (0, 0)))
    mixed = jnp.zeros(inputs.shape[:3] + (NBASIS, CHANNELS + NOISE_CH), jnp.float32)
    for offset in range(2 * LAT_HALO + 1):
        mixed = mixed + jnp.einsum('hkvw,bhvc->bhwkc', banded[:, :, offset], padded[:, offset:offset + NLAT], precision=HIGHEST)
    conv = jnp.einsum('bhwkc,kco->bhwo', mixed, conv_weight, precision=HIGHEST) + conv_bias
    middle = inputs + conv
    second = layer_norm(middle, second_gain, second_shift)
    active = jax.nn.gelu(jnp.einsum('bhwc,cu->bhwu', second, hidden_weight, precision=HIGHEST) + hidden_bias, approximate=False)
    return middle + jnp.einsum('bhwu,uc->bhwc', active, output_weight, precision=HIGHEST) + output_bias

def reference(inputs, noise_field, basis_values, row_reach, conv_weight, conv_bias, first_gain, first_shift, second_gain, second_shift, hidden_weight, hidden_bias, output_weight, output_bias, cotangent):

    def wrapped(field, conv_w, conv_b, gain_one, shift_one, gain_two, shift_two, hid_w, hid_b, out_w, out_b):
        return forward(field, conv_w, conv_b, gain_one, shift_one, gain_two, shift_two, hid_w, hid_b, out_w, out_b, noise_field, basis_values, row_reach)
    block_output, pullback = jax.vjp(wrapped, inputs, conv_weight, conv_bias, first_gain, first_shift, second_gain, second_shift, hidden_weight, hidden_bias, output_weight, output_bias)
    input_grad, conv_weight_grad, conv_bias_grad, first_gain_grad, first_shift_grad, second_gain_grad, second_shift_grad, hidden_weight_grad, hidden_bias_grad, output_weight_grad, output_bias_grad = pullback(cotangent)
    return (block_output, input_grad, conv_weight_grad, conv_bias_grad, first_gain_grad, first_shift_grad, second_gain_grad, second_shift_grad, hidden_weight_grad, hidden_bias_grad, output_weight_grad, output_bias_grad)
```

```python
from functools import partial

import jax
import jax.numpy as jnp
import numpy as np
from jax import lax
from jax.experimental import pallas as pl
from jax.experimental.pallas import tpu as pltpu
from jax.sharding import Mesh, PartitionSpec as P

LAT_HALO = 2
LON_HALO = 4
EPSILON = 1e-05
F32 = jnp.float32
BF16 = jnp.bfloat16
LAT = ("z", "y", "core")
LON = ("w", "x")
AXES = LAT + LON
LANES = 128
STEP = 256


def split(value):
    high = value.astype(BF16)
    return high, (value - high.astype(F32)).astype(BF16)


def left(value):
    high, low = split(value)
    return jnp.concatenate([high, high, low], axis=1)


def right(value):
    high, low = split(value)
    return jnp.concatenate([high, low, high], axis=0)


def right_t(value):
    high, low = split(value)
    return jnp.concatenate([high, low, high], axis=1)


def nn(a, b):
    return lax.dot_general(a, b, (((1,), (0,)), ((), ())), preferred_element_type=F32)


def nt(a, b):
    return lax.dot_general(a, b, (((1,), (1,)), ((), ())), preferred_element_type=F32)


def params(megabytes=30):
    return pltpu.CompilerParams(vmem_limit_bytes=megabytes * 1024 * 1024)


def cost(macs, moved):
    return pl.CostEstimate(flops=6 * macs // 50, bytes_accessed=moved // 50, transcendentals=0)


def full(shape):
    return pl.BlockSpec(shape, lambda *_: (0,) * len(shape), pipeline_mode=pl.Buffered(1))


def result(shape):
    return pl.BlockSpec(shape, lambda *_: (0,) * len(shape))


def round_up(value, to):
    return -(-value // to) * to


def normalize(field):
    average = jnp.mean(field, axis=-1, keepdims=True)
    centered = field - average
    variance = jnp.mean(centered * centered, axis=-1, keepdims=True)
    inverse = lax.rsqrt(variance + EPSILON)
    return centered * inverse, inverse


def norm_back(grad_norm, normalized, inverse):
    first_term = jnp.mean(grad_norm, axis=-1, keepdims=True)
    second_term = jnp.mean(grad_norm * normalized, axis=-1, keepdims=True)
    return inverse * (grad_norm - first_term - normalized * second_term)


def padded_t(value, size):
    return jnp.transpose(
        jnp.concatenate(
            [value, jnp.zeros((value.shape[0], size - value.shape[1]), value.dtype)], axis=1
        )
    )


class Sizes:
    def __init__(self, inputs, noise_field, conv_weight, hidden_weight):
        self.samples, self.rows, self.columns, self.width = inputs.shape
        self.joined = self.width + noise_field.shape[-1]
        self.basis = conv_weight.shape[0]
        self.hidden = hidden_weight.shape[1]
        self.pixels = self.samples * self.rows * self.columns
        self.main = self.width // LANES * LANES
        self.tiles = self.main // LANES
        self.extra = self.joined - self.main
        self.span = round_up(self.columns + 2 * LON_HALO, 16)
        self.taps = (2 * LAT_HALO + 1) * self.span
        self.depth = self.basis * self.main + LANES
        self.half = self.depth // 2
        self.wide = self.main + LANES
        self.high = round_up(self.width, 8)
        self.steps = self.hidden // self.main
        self.rest = self.hidden - self.steps * self.main
        self.parts = self.wide // LANES
        self.mlp_half = self.tiles * self.high + 8 * self.parts // 2


def hidden_steps(z, body):
    step = pl.program_id(0)
    pl.when(step < z.steps)(lambda: body(z.main, False))
    pl.when(step == z.steps)(lambda: body(LANES, True))


def only(z, value, last):
    if not last:
        return value
    valid = lax.broadcasted_iota(jnp.int32, (1, LANES), 1) < z.rest
    return jnp.where(valid, value.astype(F32), 0.0).astype(value.dtype)


def active_back_body(z, cot_ref, weight_ref, out_ref, lhs):
    main = z.main

    @pl.when(pl.program_id(0) == 0)
    def _():
        lhs[...] = left(cot_ref[:, :main])

    def body(width, last):
        product = nn(lhs[...], right(weight_ref[:main, :width]))
        out_ref[:, :width] = product + cot_ref[:, main : main + 1] * weight_ref[main : main + 1, :width]

    hidden_steps(z, body)


def active_back(z, cot, weight):
    return pl.pallas_call(
        partial(active_back_body, z),
        name="active_back",
        grid=(z.steps + 1,),
        in_specs=[
            full((z.pixels, z.width)),
            pl.BlockSpec((z.width, z.main), lambda i: (0, i)),
        ],
        out_specs=pl.BlockSpec((z.pixels, z.main), lambda i: (0, i)),
        out_shape=jax.ShapeDtypeStruct((z.pixels, z.hidden), F32),
        scratch_shapes=[pltpu.VMEM((z.pixels, 3 * z.main), BF16)],
        compiler_params=params(),
        cost_estimate=cost(z.pixels * z.width * z.hidden, 8 * z.width * z.hidden),
    )(cot, weight)


def band_rows(z, basis_values, row_reach):
    offsets = jnp.arange(2 * LON_HALO + 1, dtype=jnp.int32) - LON_HALO
    allowed = (jnp.abs(offsets)[None, :] <= row_reach[:, None]).astype(F32)
    masked = basis_values * allowed[:, None, None, :]
    masked = jnp.pad(masked, ((0, 0), (0, 0), (0, 0), (0, z.span - masked.shape[3])))
    return masked.reshape(z.rows, z.basis, z.taps)


def band(row, columns):
    spread = jnp.broadcast_to(row, (columns, row.shape[1]))
    return pltpu.roll(spread, 0, 1, stride=1, stride_axis=0)


def mix_body(z, info_ref, band_ref, own_ref, west_ref, east_ref, above_ref, below_ref, affine_ref, mixed_ref, other_ref, lhs, high, low):
    row = pl.program_id(0)
    gap = z.span - z.columns - 2 * LON_HALO

    def place(sample, at, value, present):
        channel = lax.broadcasted_iota(jnp.int32, (1, z.joined), 1)
        inside = channel < z.width
        mean = jnp.sum(jnp.where(inside, value, 0.0), axis=1, keepdims=True) / z.width
        centered = jnp.where(inside, value - mean, 0.0)
        variance = jnp.sum(centered * centered, axis=1, keepdims=True) / z.width
        normed = centered * lax.rsqrt(variance + EPSILON) * affine_ref[0:1, :] + affine_ref[1:2, :]
        value = jnp.where(inside, normed, value) * present
        value = jnp.concatenate([value, jnp.zeros((value.shape[0], z.wide - z.joined), F32)], axis=1)
        value = jnp.concatenate([value, jnp.zeros((gap, z.wide), F32)], axis=0)
        high_part, low_part = split(value)
        rows, lanes = slice(at * z.span, (at + 1) * z.span), slice(sample * z.wide, (sample + 1) * z.wide)
        high[rows, lanes] = high_part
        low[rows, lanes] = low_part

    @pl.when(row == 0)
    def _():
        has_above = (info_ref[1] != 0).astype(F32)
        has_below = (info_ref[2] != 0).astype(F32)
        for b in range(z.samples):
            for i in range(LAT_HALO):
                place(b, i, above_ref[b, i], has_above)
                place(b, i + z.rows + LAT_HALO, below_ref[b, i], has_below)
            for i in range(z.rows):
                value = jnp.concatenate([west_ref[b, i], own_ref[b, i], east_ref[b, i]], axis=0)
                place(b, i + LAT_HALO, value, 1.0)

    for k in range(z.basis):
        value = band(band_ref[0, k : k + 1, :], z.columns)
        lhs[k * z.columns : (k + 1) * z.columns, :] = value.astype(BF16)

    rows = pl.ds(pl.multiple_of(row * z.span, 16), z.taps)
    top, rest = high[rows, :], low[rows, :]
    product = nn(lhs[:, : 3 * z.taps], jnp.concatenate([top, rest, top], axis=0))
    for b in range(z.samples):
        tail = jnp.zeros((z.columns, LANES), F32)
        for k in range(z.basis):
            part = product[k * z.columns : (k + 1) * z.columns, b * z.wide : (b + 1) * z.wide]
            mixed_ref[b, :, k * z.main : (k + 1) * z.main] = part[:, : z.main]
            last = part[:, z.main :]
            tail = tail + (last if k == 0 else pltpu.roll(last, z.extra * k, 1))
        mixed_ref[b, :, z.basis * z.main :] = tail

    @pl.when(info_ref[0] == 0)
    def _():
        other_ref[...] = mixed_ref[:, :, z.half :]

    @pl.when(info_ref[0] != 0)
    def _():
        other_ref[...] = mixed_ref[:, :, : z.half]


def mix(z, info, bands, own, west, east, above, below, affine):
    height = (z.rows + 2 * LAT_HALO) * z.span
    high = lax.reduce_precision(bands, 8, 7)
    lanes = round_up(3 * z.taps, LANES)
    stacked = jnp.concatenate([high, high, bands - high], axis=-1)
    stacked = jnp.pad(stacked, ((0, 0), (0, 0), (0, lanes - 3 * z.taps)))
    mixed, other = pl.pallas_call(
        partial(mix_body, z),
        name="mix",
        grid_spec=pltpu.PrefetchScalarGridSpec(
            num_scalar_prefetch=1,
            grid=(z.rows,),
            in_specs=[
                pl.BlockSpec((1, z.basis, lanes), lambda r, *_: (r, 0, 0)),
                full(own.shape),
                full(west.shape),
                full(east.shape),
                full(above.shape),
                full(below.shape),
                full(affine.shape),
            ],
            out_specs=[
                pl.BlockSpec((z.samples, z.columns, z.depth), lambda r, *_: (0, r, 0)),
                pl.BlockSpec((z.samples, z.columns, z.half), lambda r, *_: (0, r, 0)),
            ],
            scratch_shapes=[
                pltpu.VMEM((z.basis * z.columns, lanes), BF16),
                pltpu.VMEM((height, z.samples * z.wide), BF16),
                pltpu.VMEM((height, z.samples * z.wide), BF16),
            ],
        ),
        out_shape=[
            jax.ShapeDtypeStruct((z.samples, z.rows * z.columns, z.depth), F32),
            jax.ShapeDtypeStruct((z.samples, z.rows * z.columns, z.half), F32),
        ],
        compiler_params=params(34),
        cost_estimate=cost(z.pixels * z.basis * z.taps * z.joined, 8 * z.pixels * z.depth),
    )(info, stacked, own, west, east, above, below, affine)
    return mixed.reshape(z.pixels, z.depth), other.reshape(z.pixels, z.half)


def conv_body(z, mixed_ref, tail_ref, weight_ref, base_ref, affine_ref, out_ref, tail_weight):
    step = pl.program_id(0)

    @pl.when(step == 0)
    def _():
        out_ref[...] = base_ref[...] + affine_ref[3:4, :]
        tail_weight[...] = jnp.zeros_like(tail_weight)

    out_ref[...] += nt(left(mixed_ref[...]), right_t(weight_ref[0, :, : z.main]))
    last = weight_ref[0, :, z.main :]
    last = jnp.concatenate([last, jnp.zeros((last.shape[0], LANES - z.extra), F32)], axis=1)
    tail_weight[...] += pltpu.roll(last, z.extra * step, 1)

    @pl.when(step == z.basis - 1)
    def _():
        out_ref[...] += nt(left(tail_ref[...]), right_t(tail_weight[...]))


def conv(z, mixed, weight, base, affine):
    return pl.pallas_call(
        partial(conv_body, z),
        name="conv",
        grid=(z.basis,),
        in_specs=[
            pl.BlockSpec((z.pixels, z.main), lambda k: (0, k)),
            pl.BlockSpec((z.pixels, LANES), lambda k: (0, z.basis * z.tiles)),
            pl.BlockSpec((1, z.width, z.joined), lambda k: (k, 0, 0)),
            full((z.pixels, z.width)),
            full(affine.shape),
        ],
        out_specs=result((z.pixels, z.width)),
        out_shape=jax.ShapeDtypeStruct((z.pixels, z.width), F32),
        scratch_shapes=[pltpu.VMEM((z.width, LANES), F32)],
        compiler_params=params(52),
        cost_estimate=cost(z.pixels * z.depth * z.width, 4 * z.depth * (z.width + z.pixels)),
    )(mixed, mixed, weight, base, affine)


def mlp_body(
    z,
    info_ref,
    middle_ref,
    cot_ref,
    d_active_ref,
    weight_ref,
    bias_ref,
    affine_ref,
    kept_ref,
    sent_ref,
    active_high_ref,
    active_low_ref,
    d_pre_high_ref,
    d_pre_low_ref,
    d_bias_ref,
    second_ref,
    second_lhs,
    second_t,
    cot_t,
):
    step = pl.program_id(0)
    main = z.main

    @pl.when(step == 0)
    def _():
        norm, _ = normalize(middle_ref[...])
        second = norm * affine_ref[0:1, :] + affine_ref[1:2, :]
        second_ref[...] = second
        second_lhs[...] = left(second[:, :main])
        second_t[...] = left(padded_t(second, z.wide)[: z.high])
        cot_t[...] = left(padded_t(cot_ref[...], z.wide)[: z.high])

    def store(out_ref, value, last):
        if not last:
            for i in range(z.tiles):
                out_ref[step, i * z.high : (i + 1) * z.high, :] = value[:, i * LANES : (i + 1) * LANES]
            return
        fill = jnp.zeros((z.wide - z.high, LANES), F32)
        value = jnp.transpose(jnp.concatenate([value, fill], axis=0))[:8]
        for i in range(z.parts):
            half, place = i // (z.parts // 2), i % (z.parts // 2)
            rows = slice(z.tiles * z.high + 8 * place, z.tiles * z.high + 8 * place + 8)
            out_ref[half, rows, :] = value[:, i * LANES : (i + 1) * LANES]

    def body(width, last):
        weight = only(z, weight_ref[:, :width], last)
        bias = only(z, bias_ref[:, :width], last)
        d_active = only(z, d_active_ref[:, :width], last)
        pre = nn(second_lhs[...], right(weight[:main]))
        pre = pre + second_ref[:, main : main + 1] * weight[main : main + 1] + bias
        cdf = 0.5 * (1.0 + lax.erf(pre * np.float32(0.5**0.5)))
        pdf = jnp.exp(pre * pre * -0.5) * np.float32(1.0 / np.sqrt(2.0 * np.pi))
        active = only(z, pre * cdf, last)
        d_pre = d_active * (cdf + pre * pdf)
        high, low = split(active)
        active_high_ref[:, :width] = high
        active_low_ref[:, :width] = low
        output_grad = nn(cot_t[...], jnp.concatenate([high, low, high], axis=0))
        high, low = split(d_pre)
        d_pre_high_ref[:, :width] = high
        d_pre_low_ref[:, :width] = low
        d_bias_ref[:, :width] = jnp.sum(d_pre, axis=0, keepdims=True)
        hidden_grad = nn(second_t[...], jnp.concatenate([high, low, high], axis=0))

        @pl.when(info_ref[0] == 0)
        def _():
            store(kept_ref, output_grad, last)
            store(sent_ref, hidden_grad, last)

        @pl.when(info_ref[0] != 0)
        def _():
            store(sent_ref, output_grad, last)
            store(kept_ref, hidden_grad, last)

    hidden_steps(z, body)


def mlp(z, info, middle, cot, d_active, weight, bias, affine):
    flat = (2, z.mlp_half, LANES)
    hidden = pl.BlockSpec((z.pixels, z.main), lambda i, *_: (0, i))
    wide = jax.ShapeDtypeStruct((z.pixels, z.hidden), BF16)
    return pl.pallas_call(
        partial(mlp_body, z),
        name="mlp",
        grid_spec=pltpu.PrefetchScalarGridSpec(
            num_scalar_prefetch=1,
            grid=(z.steps + 1,),
            in_specs=[
                full((z.pixels, z.width)),
                full((z.pixels, z.width)),
                hidden,
                pl.BlockSpec((z.width, z.main), lambda i, *_: (0, i)),
                pl.BlockSpec((1, z.main), lambda i, *_: (0, i)),
                full(affine.shape),
            ],
            out_specs=[
                full(flat),
                full(flat),
                hidden,
                hidden,
                hidden,
                hidden,
                pl.BlockSpec((1, z.main), lambda i, *_: (0, i)),
            ],
            scratch_shapes=[
                pltpu.VMEM((z.pixels, z.width), F32),
                pltpu.VMEM((z.pixels, 3 * z.main), BF16),
                pltpu.VMEM((z.high, 3 * z.pixels), BF16),
                pltpu.VMEM((z.high, 3 * z.pixels), BF16),
            ],
        ),
        out_shape=[
            jax.ShapeDtypeStruct(flat, F32),
            jax.ShapeDtypeStruct(flat, F32),
            wide,
            wide,
            wide,
            wide,
            jax.ShapeDtypeStruct((1, z.hidden), F32),
        ],
        compiler_params=params(44),
        cost_estimate=cost(3 * z.pixels * z.width * z.hidden, 12 * z.width * z.hidden),
    )(info, middle, cot, d_active, weight, bias, affine)


def middle_back_body(z, high_ref, low_ref, weight_ref, middle_ref, cot_ref, affine_ref, out_ref, out_t_ref, sums_ref, d_second):
    step = pl.program_id(0)

    @pl.when(step == 0)
    def _():
        d_second[...] = jnp.zeros_like(d_second)

    def body(width, last):
        high = only(z, high_ref[:, :width], last)
        low = only(z, low_ref[:, :width], last)
        weight = right_t(only(z, weight_ref[:, :width], last))
        d_second[...] += nt(jnp.concatenate([high, high, low], axis=1), weight)

    hidden_steps(z, body)

    @pl.when(step == z.steps)
    def _():
        norm, inverse = normalize(middle_ref[...])
        grad = d_second[...]
        sums_ref[0:1, :] = jnp.sum(grad * norm, axis=0, keepdims=True)
        sums_ref[1:2, :] = jnp.sum(grad, axis=0, keepdims=True)
        cot = cot_ref[...]
        sums_ref[3:4, :] = jnp.sum(cot, axis=0, keepdims=True)
        d_middle = cot + norm_back(grad * affine_ref[0:1, :], norm, inverse)
        sums_ref[2:3, :] = jnp.sum(d_middle, axis=0, keepdims=True)
        out_ref[...] = d_middle
        out_t_ref[...] = padded_t(d_middle, z.wide)[: z.high]


def middle_back(z, high, low, weight, middle, cot, affine):
    hidden = pl.BlockSpec((z.pixels, z.main), lambda i: (0, i))
    return pl.pallas_call(
        partial(middle_back_body, z),
        name="middle_back",
        grid=(z.steps + 1,),
        in_specs=[
            hidden,
            hidden,
            pl.BlockSpec((z.width, z.main), lambda i: (0, i)),
            full((z.pixels, z.width)),
            full((z.pixels, z.width)),
            full(affine.shape),
        ],
        out_specs=[
            full((z.pixels, z.width)),
            full((z.high, z.pixels)),
            full((4, z.width)),
        ],
        out_shape=[
            jax.ShapeDtypeStruct((z.pixels, z.width), F32),
            jax.ShapeDtypeStruct((z.high, z.pixels), F32),
            jax.ShapeDtypeStruct((4, z.width), F32),
        ],
        scratch_shapes=[pltpu.VMEM((z.pixels, z.width), F32)],
        compiler_params=params(),
        cost_estimate=cost(z.pixels * z.width * z.hidden, 8 * z.width * z.hidden),
    )(high, low, weight, middle, cot, affine)


def output_body(z, high_ref, low_ref, weight_ref, middle_ref, affine_ref, out_ref):
    @pl.when(pl.program_id(0) == 0)
    def _():
        out_ref[...] = middle_ref[...] + affine_ref[2:3, :]

    def body(width, last):
        high = only(z, high_ref[:, :width], last)
        low = only(z, low_ref[:, :width], last)
        weight = right_t(only(z, weight_ref[:, :width], last))
        out_ref[...] += nt(jnp.concatenate([high, high, low], axis=1), weight)

    hidden_steps(z, body)


def output(z, high, low, weight, middle, affine):
    hidden = pl.BlockSpec((z.pixels, z.main), lambda i: (0, i))
    return pl.pallas_call(
        partial(output_body, z),
        name="output",
        grid=(z.steps + 1,),
        in_specs=[
            hidden,
            hidden,
            pl.BlockSpec((z.width, z.main), lambda i: (0, i)),
            full((z.pixels, z.width)),
            full(affine.shape),
        ],
        out_specs=full((z.pixels, z.width)),
        out_shape=jax.ShapeDtypeStruct((z.pixels, z.width), F32),
        compiler_params=params(),
        cost_estimate=cost(z.pixels * z.width * z.hidden, 8 * z.width * z.hidden),
    )(high, low, weight, middle, affine)


def conv_grad_body(z, info_ref, own_ref, far_ref, own_t_ref, far_t_ref, sent_ref, kept_ref, lhs):
    step = pl.program_id(0)
    half = pl.num_programs(0) // 2
    tiles = own_ref.shape[1] // LANES

    @pl.when(step == 0)
    def _():
        lhs[...] = left(jnp.concatenate([own_t_ref[...], far_t_ref[...]], axis=1))
        for ref in (sent_ref, kept_ref):
            used = half * tiles * z.high
            ref[used:, :] = jnp.zeros((ref.shape[0] - used, LANES), F32)

    value = nn(lhs[...], right(jnp.concatenate([own_ref[...], far_ref[...]], axis=0)))

    def store(ref, at):
        for i in range(tiles):
            rows = pl.ds(pl.multiple_of((at * tiles + i) * z.high, 8), z.high)
            ref[rows, :] = value[:, i * LANES : (i + 1) * LANES]

    pl.when(step < half)(lambda: store(sent_ref, step))
    pl.when(step >= half)(lambda: store(kept_ref, step - half))


def conv_grad(z, info, first, count, mixed, far_mixed, own_t, far_t):
    tiles = 2 if count % 2 == 0 else 3
    start, steps, whole = first // tiles, count // tiles, z.half // LANES // tiles
    flat = round_up(count * z.high, 32)

    def at(i, c):
        kept = i // steps
        return start + jnp.where(kept == 1, c[1], 1 - c[1]) * steps + i % steps

    return pl.pallas_call(
        partial(conv_grad_body, z),
        name="conv_grad",
        grid_spec=pltpu.PrefetchScalarGridSpec(
            num_scalar_prefetch=1,
            grid=(2 * steps,),
            in_specs=[
                pl.BlockSpec((z.pixels, tiles * LANES), lambda i, c: (0, c[0] * whole + at(i, c))),
                pl.BlockSpec((z.pixels, tiles * LANES), lambda i, c: (0, at(i, c))),
                full((z.high, z.pixels)),
                full((z.high, z.pixels)),
            ],
            out_specs=[full((flat, LANES)), full((flat, LANES))],
            scratch_shapes=[pltpu.VMEM((z.high, 6 * z.pixels), BF16)],
        ),
        out_shape=[jax.ShapeDtypeStruct((flat, LANES), F32)] * 2,
        compiler_params=params(50),
        cost_estimate=cost(4 * z.pixels * z.width * count * LANES, 12 * z.pixels * count * LANES),
    )(info, mixed, far_mixed, own_t, far_t)


def mix_back_body(z, first, last, weight_ref, dm_ref, band_ref, out_ref, lhs, high, low):
    step = pl.program_id(0)
    columns, main, span = z.columns, z.main, last - first
    depth = z.basis * columns

    @pl.when(step == 0)
    def _():
        lhs[...] = left(dm_ref[:, :main])
        out_ref[...] = jnp.zeros_like(out_ref)
        fill = jnp.zeros((z.rows, high.shape[1] - depth, high.shape[2]), BF16)
        high[:, depth:, :] = fill
        low[:, depth:, :] = fill

    @pl.when(step < z.basis)
    def _():
        value = nn(lhs[...], right(weight_ref[0, :main, : last - first]))
        value = value + dm_ref[:, main : main + 1] * weight_ref[0, main : main + 1, : last - first]
        value_high, value_low = split(value)
        place = pl.ds(pl.multiple_of(step * columns, 16), columns)
        for b in range(z.samples):
            for r in range(z.rows):
                i = (b * z.rows + r) * columns
                lane = b * round_up(span, LANES)
                high[r, place, lane : lane + span] = value_high[i : i + columns]
                low[r, place, lane : lane + span] = value_low[i : i + columns]

    @pl.when(step >= z.basis)
    def _():
        row = step - z.basis
        spread = [band(band_ref[0, k : k + 1, :], columns) for k in range(z.basis)]
        spread.append(jnp.zeros((high.shape[1] - depth, band_ref.shape[2]), F32))
        spread = jnp.transpose(jnp.concatenate(spread, axis=0))[: z.taps]
        place = pl.ds(pl.multiple_of(row * z.span, 8), z.taps)
        rhs = jnp.concatenate([high[row], low[row], high[row]], axis=0)
        value = nn(left(spread), rhs)
        for b in range(z.samples):
            lane = b * round_up(span, LANES)
            out_ref[b, place, :] += value[:, lane : lane + span]


def mix_back(z, weight, d_middle, bands, first, last):
    lanes = round_up(z.taps, LANES)
    bands = jnp.pad(bands, ((0, 0), (0, 0), (0, lanes - z.taps)))
    height = (z.rows + 2 * LAT_HALO) * z.span
    end = z.basis - 1
    span = last - first
    depth = round_up(z.basis * z.columns, LANES)
    return pl.pallas_call(
        partial(mix_back_body, z, first, last),
        name="mix_back",
        grid=(z.basis + z.rows,),
        in_specs=[
            pl.BlockSpec((1, z.width, STEP), lambda i: (jnp.minimum(i, end), 0, first // STEP)),
            full((z.pixels, z.width)),
            pl.BlockSpec((1, z.basis, lanes), lambda i: (jnp.maximum(i - z.basis, 0), 0, 0)),
        ],
        out_specs=result((z.samples, height, span)),
        out_shape=jax.ShapeDtypeStruct((z.samples, height, span), F32),
        scratch_shapes=[
            pltpu.VMEM((z.pixels, 3 * z.main), BF16),
            pltpu.VMEM((z.rows, depth, z.samples * round_up(span, LANES)), BF16),
            pltpu.VMEM((z.rows, depth, z.samples * round_up(span, LANES)), BF16),
        ],
        compiler_params=params(50),
        cost_estimate=cost(
            z.pixels * z.depth * span + z.pixels * z.basis * z.taps * span,
            4 * z.depth * z.width,
        ),
    )(weight, d_middle, bands)


def conv_place_body(z, first, count, info_ref, *refs):
    pieces, (out_ref, held, narrow, sems) = refs[:4], refs[-4:]
    main_tiles = z.basis * z.tiles
    with_extra = first + 2 * count == z.half // LANES
    used = count * z.high

    def get(i):
        return pltpu.make_async_copy(pieces[i].at[pl.ds(0, used), :], held.at[i], sems.at[i])

    def tile(i, t):
        return (info_ref[i] // 2) * (z.half // LANES) + first + (info_ref[i] % 2) * count + t

    def put(i, t):
        at = tile(i, t)
        lanes = pl.ds(pl.multiple_of(at % z.tiles * LANES, LANES), LANES)
        return pltpu.make_async_copy(
            held.at[i, pl.ds(t * z.high, z.width), :],
            out_ref.at[at // z.tiles, :, lanes],
            sems.at[4 + i * count + t],
        )

    def put_extra(k):
        return pltpu.make_async_copy(
            narrow.at[k], out_ref.at[k, :, pl.ds(z.main, z.extra)], sems.at[4 + 4 * count + k]
        )

    for i in range(4):
        get(i).start()
    for i in range(4):
        get(i).wait()
        for t in range(count):
            is_main = tile(i, t) < main_tiles

            @pl.when(is_main)
            def _():
                put(i, t).start()

            if with_extra and t == count - 1:

                @pl.when(jnp.logical_not(is_main))
                def _():
                    for k in range(z.basis):
                        value = held[i, t * z.high : (t + 1) * z.high, :]
                        value = value if k == 0 else pltpu.roll(value, LANES - z.extra * k, 1)
                        narrow[k] = value[: z.width, : z.extra]
                        put_extra(k).start()

    if with_extra:
        for k in range(z.basis):
            put_extra(k).wait()
    for i in range(4):
        for t in range(count):

            @pl.when(tile(i, t) < main_tiles)
            def _():
                put(i, t).wait()


def conv_place(z, places, first, count, pieces, onto):
    anywhere = pl.BlockSpec(memory_space=pl.ANY)
    operands = [places, *pieces]
    aliases = {}
    if onto is not None:
        operands.append(onto)
        aliases = {5: 0}
    return pl.pallas_call(
        partial(conv_place_body, z, first, count),
        name="conv_place",
        grid_spec=pltpu.PrefetchScalarGridSpec(
            num_scalar_prefetch=1,
            grid=(),
            in_specs=[anywhere] * (len(operands) - 1),
            out_specs=anywhere,
            scratch_shapes=[
                pltpu.VMEM((4, count * z.high, LANES), F32),
                pltpu.VMEM((z.basis, z.width, z.extra), F32),
                pltpu.SemaphoreType.DMA((4 + 4 * count + z.basis,)),
            ],
        ),
        out_shape=jax.ShapeDtypeStruct((z.basis, z.width, z.joined), F32),
        input_output_aliases=aliases,
        compiler_params=params(16),
        cost_estimate=cost(0, 20 * count * z.main * LANES),
    )(*operands)


def mlp_place_body(z, info_ref, own_ref, far_ref, output_ref, hidden_ref, held, narrow, sems):
    main_tiles = 2 * z.tiles

    def place(refs):
        gets = []
        for i, ref in enumerate(refs):
            quarter = z.mlp_half // 2
            for q, at in enumerate((0, 2, 1, 3) if i == 0 else (0, 1, 2, 3)):
                gets.append(
                    pltpu.make_async_copy(
                        ref.at[pl.ds(at * quarter, quarter), :],
                        held.at[i, q // 2, pl.ds(q % 2 * quarter, quarter), :],
                        sems.at[4 * i + q],
                    )
                )
                gets[-1].start()
        puts = []
        for i, out_ref in enumerate((output_ref, hidden_ref)):
            for t in range(main_tiles):
                half = t // z.tiles
                if t % z.tiles == 0:
                    gets[4 * i + 2 * half].wait()
                    gets[4 * i + 2 * half + 1].wait()
                puts.append(
                    pltpu.make_async_copy(
                        held.at[i, half, pl.ds(t % z.tiles * z.high, z.width), :],
                        out_ref.at[:, pl.ds(t * LANES, LANES)],
                        sems.at[8 + i * main_tiles + t],
                    )
                )
                puts[-1].start()
            start = z.tiles * z.high
            parts = [
                held[i, half, start + 8 * j : start + 8 * j + 8, :] for half in range(2) for j in range(z.parts // 2)
            ]
            value = jnp.concatenate([jnp.concatenate(parts, axis=1)] * (LANES // 8), axis=0)
            narrow[i] = jnp.transpose(value)[: z.width, : z.rest]
            puts.append(
                pltpu.make_async_copy(
                    narrow.at[i],
                    out_ref.at[:, pl.ds(main_tiles * LANES, z.rest)],
                    sems.at[8 + 2 * main_tiles + i],
                )
            )
            puts[-1].start()
        for c in puts:
            c.wait()

    pl.when(info_ref[0] == 0)(lambda: place((own_ref, far_ref)))
    pl.when(info_ref[0] != 0)(lambda: place((far_ref, own_ref)))


def mlp_place(z, info, own, far):
    shape = jax.ShapeDtypeStruct((z.width, z.hidden), F32)
    anywhere = pl.BlockSpec(memory_space=pl.ANY)
    return pl.pallas_call(
        partial(mlp_place_body, z),
        name="mlp_place",
        grid_spec=pltpu.PrefetchScalarGridSpec(
            num_scalar_prefetch=1,
            grid=(),
            in_specs=[anywhere, anywhere],
            out_specs=[anywhere, anywhere],
            scratch_shapes=[
                pltpu.VMEM((2, 2, z.mlp_half, LANES), F32),
                pltpu.VMEM((2, z.width, z.rest), F32),
                pltpu.SemaphoreType.DMA((4 * z.tiles + 10,)),
            ],
        ),
        out_shape=[shape, shape],
        compiler_params=params(16),
        cost_estimate=cost(0, 16 * z.hidden * z.width),
    )(info, own, far)


def axis_size(axes):
    size = 1
    for axis in axes:
        size *= lax.axis_size(axis)
    return size


def pairs(lats, lons, target):
    found = []
    for lat in range(lats):
        for lon in range(lons):
            to_lat, to_lon = target(lat, lon)
            found.append((lat * lons + lon, to_lat * lons + to_lon))
    return found


class GridSum:
    def __init__(self):
        lats, lons = axis_size(LAT), axis_size(LON)
        lat, lon = lax.axis_index(LAT), lax.axis_index(LON)
        over = partial(pairs, lats, lons)
        self.core = lat % 2
        self.cores = over(lambda a, o: (a ^ 1, o))
        self.first = over(lambda a, o: (a ^ 2, o) if a % 2 else (a, o ^ 1))
        self.second = over(lambda a, o: (a, o ^ 1) if a % 2 else (a ^ 2, o))
        self.third = over(lambda a, o: (a ^ 4, o))
        lon_bit, lat_bit = lon % 2, lat // 2 % 2
        self.first_bit = jnp.where(self.core == 0, lon_bit, lat_bit)
        self.second_bit = jnp.where(self.core == 0, lat_bit, lon_bit)
        self.third_bit = lat // 4 % 2
        far_bit = jnp.where(self.core == 0, lat_bit, lon_bit)
        mine, other = 2 * self.core, 2 * (1 - self.core)
        self.places = jnp.stack(
            [mine + self.first_bit, mine + 1 - self.first_bit, other + far_bit, other + 1 - far_bit]
        ).astype(jnp.int32)
        self.others = []
        bit = 8
        while bit < lats:
            self.others.append(over(lambda a, o, bit=bit: (a ^ bit, o)))
            bit *= 2
        bit = 2
        while bit < lons:
            self.others.append(over(lambda a, o, bit=bit: (a, o ^ bit)))
            bit *= 2

    def swap(self, value, where):
        return lax.ppermute(value, AXES, where)

    def all(self, value, where):
        return value + self.swap(value, where)


class Order:
    def __init__(self):
        self.last = ()
        self.held = True

    def use(self, value):
        if not self.held:
            return value
        value, self.last = lax.optimization_barrier((value, self.last))
        return value

    def mark(self, value):
        if self.held:
            self.last = (value,)
        return value

    def wait(self, value):
        return self.mark(self.use(value))

    def run(self, function, *values):
        return self.mark(function(*self.use(values)))


class Chunk:
    def __init__(self, total, order, name, sent, kept):
        self.total, self.order, self.name = total, order, name
        self.value = kept
        self.far = self.swap("scatter_first", order.mark(sent), total.first)

    def swap(self, step, value, where):
        with jax.named_scope(f"{self.name}_{step}"):
            return self.total.swap(value, where)

    def halve(self, step, where, bit):
        def part(which):
            def add(a, b):
                size = a.shape[0] // 2
                a = lax.dynamic_slice_in_dim(a, which * size, size, 0)
                return a + lax.dynamic_slice_in_dim(b, which * size, size, 0)

            return add

        sent = self.order.run(part(1 - bit), self.value, self.far)
        self.value = part(bit)(self.value, self.far)
        self.far = self.swap(step, sent, where)

    def send(self, step, where):
        self.far = self.swap(step, self.value, where)

    def add(self):
        self.value = self.order.run(lambda a, b: a + b, self.value, self.far)

    def join(self, bit):
        def both(value, far):
            own = (jnp.arange(2) == bit)[:, None, None]
            return jnp.where(own, value[None], far[None]).reshape(-1, LANES)

        self.value = self.order.run(both, self.value, self.far)

    def scatter_second(self):
        self.halve("scatter_second", self.total.second, self.total.second_bit)

    def across_first(self):
        self.halve("across_first", self.total.third, self.total.third_bit)

    def across_second(self):
        self.add()
        for where in self.total.others[:-1]:
            self.value = self.total.all(self.value, where)
        self.send("across_second", self.total.others[-1])

    def across_third(self):
        self.add()
        self.send("across_third", self.total.third)

    def gather_second(self):
        self.join(self.total.third_bit)
        self.send("gather_second", self.total.second)

    def gather_first(self):
        self.join(self.total.second_bit)
        self.send("gather_first", self.total.first)
        self.near = self.swap("near_core", self.value, self.total.cores)

    def gather_core(self):
        self.far = self.order.mark(self.order.use(self.far))
        self.last = self.swap("gather_core", self.far, self.total.cores)

    def gather_plane(self):
        self.join(self.total.third_bit)
        self.value = lax.all_gather(self.value, ("y", "x"), axis=0, tiled=True)

    def pieces(self):
        return self.value, self.far, self.near, self.last


def after(value, *others):
    return lax.optimization_barrier((value, others))[0]


def rows_of(vector):
    size = round_up(vector.shape[0], LANES)
    return jnp.pad(vector, (0, size - vector.shape[0])).reshape(-1, LANES)


def moved(value, axis, steps, cycle):
    count = axis_size(axis)
    if cycle:
        where = [(i, (i + steps) % count) for i in range(count)]
    else:
        where = [(i, i + steps) for i in range(max(0, -steps), min(count, count - steps))]
    return lax.ppermute(value, axis, where)


def edges(low, high, dim):
    if axis_size(LON) == 2:
        both = moved(jnp.concatenate([high, low], axis=dim), LON, 1, True)
        size = high.shape[dim]
        return (
            lax.slice_in_dim(both, 0, size, axis=dim),
            lax.slice_in_dim(both, size, None, axis=dim),
        )
    return moved(high, LON, 1, True), moved(low, LON, -1, True)


def local(
    inputs,
    noise_field,
    basis_values,
    row_reach,
    conv_weight,
    conv_bias,
    first_gain,
    first_shift,
    second_gain,
    second_shift,
    hidden_weight,
    hidden_bias,
    output_weight,
    output_bias,
    cotangent,
):
    z = Sizes(inputs, noise_field, conv_weight, hidden_weight)
    total = GridSum()
    lat, lats = lax.axis_index(LAT), axis_size(LAT)
    info = jnp.stack([total.core, (lat > 0).astype(jnp.int32), (lat < lats - 1).astype(jnp.int32)])
    rows, columns, width = z.rows, z.columns, z.width
    flat = (z.pixels, width)
    cot = cotangent.reshape(flat)
    conv_weight = jnp.transpose(conv_weight, (0, 2, 1))
    output_weight = jnp.transpose(output_weight)

    own = jnp.concatenate([inputs, noise_field], axis=-1)
    west, east = edges(own[:, :, :LON_HALO], own[:, :, columns - LON_HALO :], 2)
    above = moved(
        jnp.concatenate([part[:, rows - LAT_HALO :] for part in (west, own, east)], axis=2), LAT, 1, False
    )
    below = moved(
        jnp.concatenate([part[:, :LAT_HALO] for part in (west, own, east)], axis=2), LAT, -1, False
    )
    d_active = active_back(z, cot, output_weight)
    bands = band_rows(z, basis_values, row_reach)
    none = jnp.zeros_like(conv_bias)
    affine = jnp.stack([second_gain, second_shift, output_bias, conv_bias, none, none, none, none])
    first_affine = jnp.pad(jnp.stack([first_gain, first_shift]), ((0, 6), (0, z.joined - width)))
    above, below = after((above, below), d_active)
    mixed, other = mix(z, info, bands, own, west, east, above, below, first_affine)
    far_mixed = total.swap(other, total.cores)
    middle = conv(z, mixed, conv_weight, inputs.reshape(flat), affine)
    kept, sent, active_high, active_low, d_pre_high, d_pre_low, d_hidden_bias = mlp(
        z, info, middle, cot, d_active, hidden_weight, hidden_bias[None], affine
    )
    order = Order()
    arrived = total.swap(sent, total.cores)
    d_middle, d_middle_t, sums = order.run(
        partial(middle_back, z), d_pre_high, d_pre_low, hidden_weight, middle, cot, affine
    )
    far_t = total.swap(d_middle_t, total.cores)

    bit = total.first_bit
    pick = lambda which: lambda a, b: (
        lax.dynamic_index_in_dim(a, which, 0, keepdims=False) + lax.dynamic_index_in_dim(b, which, 0, keepdims=False)
    )
    m = Chunk(total, order, "m", order.run(pick(1 - bit), kept, arrived), pick(bit)(kept, arrived))
    keep = jnp.stack([total.core, bit])
    half_tiles = z.half // LANES
    late = half_tiles // 6
    early = half_tiles // 2 - late
    operands = mixed, far_mixed, d_middle_t, far_t
    grad = lambda first, count: order.run(
        lambda *v: conv_grad(z, keep, first, count, *v), *operands
    )
    parts = []

    def back_part(first):
        last = min(first + STEP, z.joined)
        back = partial(mix_back, z)
        parts.append(order.run(lambda *v: back(*v, first, last), conv_weight, d_middle, bands))

    a = Chunk(total, order, "a", *grad(2 * late, early))
    m.scatter_second()
    b = Chunk(total, order, "b", *grad(0, late))
    back_part(0)
    m.across_first()
    back_part(STEP)
    a.scatter_second()
    m.across_second()
    for first in range(2 * STEP, z.joined, STEP):
        back_part(first)
    d_padded = jnp.concatenate(parts, axis=2)
    d_padded = d_padded.reshape(z.samples, -1, z.span, z.joined)[:, :, : columns + 2 * LON_HALO]
    rims = order.wait((d_padded[:, :LAT_HALO], d_padded[:, rows + LAT_HALO :]))
    from_below = moved(rims[0], LAT, -1, False)
    from_above = moved(rims[1], LAT, 1, False)
    b.scatter_second()
    a.across_first()
    block_output = order.run(
        partial(output, z), active_high, active_low, output_weight, middle, affine
    )
    m.across_third()
    from_above, from_below = order.wait((from_above, from_below))
    inner = d_padded[:, LAT_HALO : rows + LAT_HALO]
    inner = inner + jnp.pad(from_above, ((0, 0), (0, rows - LAT_HALO), (0, 0), (0, 0)))
    inner = inner + jnp.pad(from_below, ((0, 0), (rows - LAT_HALO, 0), (0, 0), (0, 0)))
    low, high = order.wait((inner[:, :, :LON_HALO], inner[:, :, columns + LON_HALO :]))
    from_west, from_east = edges(low, high, 2)
    b.across_first()
    a.across_second()
    m.gather_plane()
    from_west, from_east = order.wait((from_west, from_east))
    d_joined = inner[:, :, LON_HALO : columns + LON_HALO]
    d_joined = d_joined + jnp.pad(from_west, ((0, 0), (0, 0), (0, columns - LON_HALO), (0, 0)))
    d_joined = d_joined + jnp.pad(from_east, ((0, 0), (0, 0), (columns - LON_HALO, 0), (0, 0)))
    d_normed = d_joined[..., :width]
    first_norm, first_inverse = normalize(order.use(inputs))
    axes = (0, 1, 2)
    first_gain_grad = jnp.sum(d_normed * first_norm, axis=axes)
    first_shift_grad = jnp.sum(d_normed, axis=axes)

    vectors = [sums[2], first_gain_grad, first_shift_grad, sums[0], sums[1], d_hidden_bias[0], sums[3]]
    sizes = [v.shape[0] for v in vectors]
    vectors = [rows_of(v) for v in vectors]
    counts = [v.shape[0] for v in vectors]
    vectors = jnp.concatenate(vectors, axis=0)
    vectors = jnp.pad(vectors, ((0, round_up(sum(counts), 16) - sum(counts)), (0, 0)))
    vectors = order.wait(vectors)

    def turn(where):
        with jax.named_scope("vectors"):
            return order.run(lambda v, f: v + f, vectors, total.swap(vectors, where))

    vectors = turn(total.cores)
    b.across_second()
    input_grad = d_middle.reshape(inputs.shape) + norm_back(d_normed * first_gain, first_norm, first_inverse)
    input_grad = order.wait(input_grad)
    vectors = turn(total.first)
    a.across_third()
    vectors = turn(total.second)
    b.across_third()
    vectors = turn(total.third)
    a.gather_second()
    for where in total.others:
        vectors = turn(where)
    found, start = [], 0
    for size, count in zip(sizes, counts):
        found.append(vectors[start : start + count].reshape(-1)[:size])
        start += count
    b.gather_second()
    a.gather_first()
    found = order.wait(found)
    b.gather_first()
    m.value = order.wait(m.value)
    m_far = total.swap(m.value, total.cores)
    a.gather_core()
    output_weight_grad, hidden_weight_grad = order.run(lambda *v: mlp_place(z, info, *v), m.value, m_far)
    conv_weight_grad = order.run(lambda *v: conv_place(z, total.places, 2 * late, early, v, None), *a.pieces())
    b.gather_core()
    conv_weight_grad = conv_place(z, total.places, 0, late, b.pieces(), conv_weight_grad)
    conv_weight_grad = jnp.transpose(conv_weight_grad, (0, 2, 1))
    output_weight_grad = jnp.transpose(output_weight_grad)
    conv_bias_grad, first_gain_grad, first_shift_grad, second_gain_grad, second_shift_grad = found[:5]
    hidden_bias_grad, output_bias_grad = found[5:]
    return (
        block_output.reshape(inputs.shape),
        input_grad,
        conv_weight_grad,
        conv_bias_grad,
        first_gain_grad,
        first_shift_grad,
        second_gain_grad,
        second_shift_grad,
        hidden_weight_grad,
        hidden_bias_grad,
        output_weight_grad,
        output_bias_grad,
    )


def solution(mesh):
    lats, lons = mesh.shape["lat"], mesh.shape["lon"]
    fine = Mesh(mesh.devices.reshape(lats // 4, 2, 2, lons // 2, 2), AXES)
    grid = P(None, LAT, LON, None)
    weights = (P(),) * 10
    in_specs = (grid, grid, P(LAT, None, None, None), P(LAT)) + weights + (grid,)
    out_specs = (grid, grid) + weights
    return jax.shard_map(local, mesh=fine, in_specs=in_specs, out_specs=out_specs, check_vma=False)
```

```python
from functools import partial

import jax
import jax.numpy as jnp
import numpy as np
from jax import lax
from jax.experimental import pallas as pl
from jax.experimental.pallas import tpu as pltpu
from jax.sharding import Mesh, PartitionSpec as P

LAT_HALO = 2
LON_HALO = 4
EPSILON = 1e-05
F32 = jnp.float32
BF16 = jnp.bfloat16
LAT = ("z", "y", "core")
LON = ("w", "x")
AXES = LAT + LON
LANES = 128
STEP = 256


def split(value):
    high = value.astype(BF16)
    return high, (value - high.astype(F32)).astype(BF16)


def left(value):
    high, low = split(value)
    return jnp.concatenate([high, high, low], axis=1)


def right(value):
    high, low = split(value)
    return jnp.concatenate([high, low, high], axis=0)


def right_t(value):
    high, low = split(value)
    return jnp.concatenate([high, low, high], axis=1)


def nn(a, b):
    return lax.dot_general(a, b, (((1,), (0,)), ((), ())), preferred_element_type=F32)


def nt(a, b):
    return lax.dot_general(a, b, (((1,), (1,)), ((), ())), preferred_element_type=F32)


def params(megabytes=30):
    return pltpu.CompilerParams(vmem_limit_bytes=megabytes * 1024 * 1024)


def cost(macs, moved):
    return pl.CostEstimate(flops=12 * macs, bytes_accessed=moved, transcendentals=0)


def full(shape):
    return pl.BlockSpec(shape, lambda *_: (0,) * len(shape), pipeline_mode=pl.Buffered(1))


def result(shape):
    return pl.BlockSpec(shape, lambda *_: (0,) * len(shape))


def row(ref):
    return ref[...].reshape(1, ref.shape[0])


def round_up(value, to):
    return -(-value // to) * to


def normalize(field):
    average = jnp.mean(field, axis=-1, keepdims=True)
    centered = field - average
    variance = jnp.mean(centered * centered, axis=-1, keepdims=True)
    inverse = lax.rsqrt(variance + EPSILON)
    return centered * inverse, inverse


def norm_back(grad_norm, normalized, inverse):
    first_term = jnp.mean(grad_norm, axis=-1, keepdims=True)
    second_term = jnp.mean(grad_norm * normalized, axis=-1, keepdims=True)
    return inverse * (grad_norm - first_term - normalized * second_term)


def padded_t(value, size):
    return jnp.transpose(
        jnp.concatenate(
            [value, jnp.zeros((value.shape[0], size - value.shape[1]), value.dtype)], axis=1
        )
    )


class Sizes:
    def __init__(self, inputs, noise_field, conv_weight, hidden_weight):
        self.samples, self.rows, self.columns, self.width = inputs.shape
        self.joined = self.width + noise_field.shape[-1]
        self.basis = conv_weight.shape[0]
        self.hidden = hidden_weight.shape[1]
        self.pixels = self.samples * self.rows * self.columns
        self.main = self.width // LANES * LANES
        self.tiles = self.main // LANES
        self.extra = self.joined - self.main
        self.span = round_up(self.columns + 2 * LON_HALO, 16)
        self.taps = (2 * LAT_HALO + 1) * self.span
        self.depth = self.basis * self.main + LANES
        self.half = self.depth // 2
        self.wide = self.main + LANES
        self.high = round_up(self.width, 8)
        self.steps = self.hidden // self.main
        self.rest = self.hidden - self.steps * self.main
        self.parts = self.wide // LANES
        self.mlp_half = self.tiles * self.high + 8 * self.parts // 2


def hidden_steps(z, body):
    step = pl.program_id(0)
    pl.when(step < z.steps)(lambda: body(z.main, False))
    pl.when(step == z.steps)(lambda: body(LANES, True))


def only(z, value, last):
    if not last:
        return value
    valid = lax.broadcasted_iota(jnp.int32, (1, LANES), 1) < z.rest
    return jnp.where(valid, value.astype(F32), 0.0).astype(value.dtype)


def active_back_body(z, cot_ref, weight_ref, out_ref, lhs):
    main = z.main

    @pl.when(pl.program_id(0) == 0)
    def _():
        lhs[...] = left(cot_ref[:, :main])

    def body(width, last):
        product = nn(lhs[...], right(weight_ref[:main, :width]))
        out_ref[:, :width] = product + cot_ref[:, main : main + 1] * weight_ref[main : main + 1, :width]

    hidden_steps(z, body)


def active_back(z, cot, weight):
    return pl.pallas_call(
        partial(active_back_body, z),
        name="active_back",
        grid=(z.steps + 1,),
        in_specs=[
            full((z.pixels, z.width)),
            pl.BlockSpec((z.width, z.main), lambda i: (0, i)),
        ],
        out_specs=pl.BlockSpec((z.pixels, z.main), lambda i: (0, i)),
        out_shape=jax.ShapeDtypeStruct((z.pixels, z.hidden), F32),
        scratch_shapes=[pltpu.VMEM((z.pixels, 3 * z.main), BF16)],
        compiler_params=params(),
        cost_estimate=cost(z.pixels * z.width * z.hidden, 8 * z.width * z.hidden),
    )(cot, weight)


def band_rows(z, basis_values, row_reach):
    offsets = jnp.arange(2 * LON_HALO + 1, dtype=jnp.int32) - LON_HALO
    allowed = (jnp.abs(offsets)[None, :] <= row_reach[:, None]).astype(F32)
    masked = basis_values * allowed[:, None, None, :]
    masked = jnp.pad(masked, ((0, 0), (0, 0), (0, 0), (0, z.span - masked.shape[3])))
    return masked.reshape(z.rows, z.basis, z.taps)


def band(row, columns):
    spread = jnp.broadcast_to(row, (columns, row.shape[1]))
    return pltpu.roll(spread, 0, 1, stride=1, stride_axis=0)


def cut_body(z, inputs_ref, noise_ref, top_ref, bottom_ref, top_sides_ref, bottom_sides_ref, sides_ref):
    for b in range(z.samples):
        for i in range(z.rows):
            value = jnp.concatenate([inputs_ref[b, i], jnp.transpose(noise_ref[b, i])], axis=1)
            side = jnp.concatenate([value[z.columns - LON_HALO :], value[:LON_HALO]], axis=0)
            sides_ref[b, i] = side
            if i < LAT_HALO:
                top_ref[b, i] = value
                top_sides_ref[b, i] = side
            if i >= z.rows - LAT_HALO:
                bottom_ref[b, i - z.rows + LAT_HALO] = value
                bottom_sides_ref[b, i - z.rows + LAT_HALO] = side


def cut(z, inputs, noise):
    shape = lambda rows, columns: jax.ShapeDtypeStruct((z.samples, rows, columns, z.joined), F32)
    rim, side = shape(LAT_HALO, z.columns), shape(LAT_HALO, 2 * LON_HALO)
    return pl.pallas_call(
        partial(cut_body, z),
        name="cut",
        out_shape=[rim, rim, side, side, shape(z.rows, 2 * LON_HALO)],
        compiler_params=params(16),
    )(inputs, noise)


def mix_body(z, info_ref, band_ref, inputs_ref, noise_ref, above_ref, below_ref, above_sides_ref, below_sides_ref, sides_ref, gain_ref, shift_ref, mixed_ref, other_ref, lhs, high, low):
    at_row = pl.program_id(0)
    gap = z.span - z.columns - 2 * LON_HALO

    def place(sample, at, value, sides, present, gain, shift):
        value = jnp.concatenate([sides[:LON_HALO], value, sides[LON_HALO:]], axis=0)
        channel = lax.broadcasted_iota(jnp.int32, (1, z.joined), 1)
        inside = channel < z.width
        mean = jnp.sum(jnp.where(inside, value, 0.0), axis=1, keepdims=True) / z.width
        centered = jnp.where(inside, value - mean, 0.0)
        variance = jnp.sum(centered * centered, axis=1, keepdims=True) / z.width
        normed = centered * lax.rsqrt(variance + EPSILON) * gain + shift
        value = jnp.where(inside, normed, value) * present
        value = jnp.concatenate([value, jnp.zeros((value.shape[0], z.wide - z.joined), F32)], axis=1)
        value = jnp.concatenate([value, jnp.zeros((gap, z.wide), F32)], axis=0)
        high_part, low_part = split(value)
        rows, lanes = slice(at * z.span, (at + 1) * z.span), slice(sample * z.wide, (sample + 1) * z.wide)
        high[rows, lanes] = high_part
        low[rows, lanes] = low_part

    @pl.when(at_row == 0)
    def _():
        fill = jnp.zeros((1, z.joined - z.width), F32)
        gain = jnp.concatenate([row(gain_ref), fill], axis=1)
        shift = jnp.concatenate([row(shift_ref), fill], axis=1)
        has_above = (info_ref[1] != 0).astype(F32)
        has_below = (info_ref[2] != 0).astype(F32)
        for b in range(z.samples):
            for i in range(LAT_HALO):
                place(b, i, above_ref[b, i], above_sides_ref[b, i], has_above, gain, shift)
                place(b, i + z.rows + LAT_HALO, below_ref[b, i], below_sides_ref[b, i], has_below, gain, shift)
            for i in range(z.rows):
                value = jnp.concatenate([inputs_ref[b, i], jnp.transpose(noise_ref[b, i])], axis=1)
                place(b, i + LAT_HALO, value, sides_ref[b, i], 1.0, gain, shift)

    for k in range(z.basis):
        value = band(band_ref[0, k : k + 1, :], z.columns)
        lhs[k * z.columns : (k + 1) * z.columns, :] = value.astype(BF16)

    rows = pl.ds(pl.multiple_of(at_row * z.span, 16), z.taps)
    top, rest = high[rows, :], low[rows, :]
    product = nn(lhs[:, : 3 * z.taps], jnp.concatenate([top, rest, top], axis=0))
    for b in range(z.samples):
        tail = jnp.zeros((z.columns, LANES), F32)
        for k in range(z.basis):
            part = product[k * z.columns : (k + 1) * z.columns, b * z.wide : (b + 1) * z.wide]
            mixed_ref[b, :, k * z.main : (k + 1) * z.main] = part[:, : z.main]
            last = part[:, z.main :]
            tail = tail + (last if k == 0 else pltpu.roll(last, z.extra * k, 1))
        mixed_ref[b, :, z.basis * z.main :] = tail

    @pl.when(info_ref[0] == 0)
    def _():
        other_ref[...] = mixed_ref[:, :, z.half :]

    @pl.when(info_ref[0] != 0)
    def _():
        other_ref[...] = mixed_ref[:, :, : z.half]


def mix(z, info, bands, inputs, noise, above, below, sides, gain, shift):
    height = (z.rows + 2 * LAT_HALO) * z.span
    high = lax.reduce_precision(bands, 8, 7)
    lanes = round_up(3 * z.taps, LANES)
    stacked = jnp.concatenate([high, high, bands - high], axis=-1)
    stacked = jnp.pad(stacked, ((0, 0), (0, 0), (0, lanes - 3 * z.taps)))
    arrays = [inputs, noise, above, below, *sides, gain, shift]
    mixed, other = pl.pallas_call(
        partial(mix_body, z),
        name="mix",
        grid_spec=pltpu.PrefetchScalarGridSpec(
            num_scalar_prefetch=1,
            grid=(z.rows,),
            in_specs=[
                pl.BlockSpec((1, z.basis, lanes), lambda r, *_: (r, 0, 0)),
                *(full(a.shape) for a in arrays),
            ],
            out_specs=[
                pl.BlockSpec((z.samples, z.columns, z.depth), lambda r, *_: (0, r, 0)),
                pl.BlockSpec((z.samples, z.columns, z.half), lambda r, *_: (0, r, 0)),
            ],
            scratch_shapes=[
                pltpu.VMEM((z.basis * z.columns, lanes), BF16),
                pltpu.VMEM((height, z.samples * z.wide), BF16),
                pltpu.VMEM((height, z.samples * z.wide), BF16),
            ],
        ),
        out_shape=[
            pltpu.HBM((z.samples, z.rows * z.columns, z.depth), F32),
            pltpu.HBM((z.samples, z.rows * z.columns, z.half), F32),
        ],
        compiler_params=params(34),
        cost_estimate=cost(z.pixels * z.basis * z.taps * z.joined, 8 * z.pixels * z.depth),
    )(info, stacked, *arrays)
    return mixed.reshape(z.pixels, z.depth), other.reshape(z.pixels, z.half)


def conv_body(z, mixed_ref, tail_ref, weight_ref, base_ref, bias_ref, out_ref, tail_weight):
    step = pl.program_id(0)

    @pl.when(step == 0)
    def _():
        out_ref[...] = base_ref[...] + row(bias_ref)
        tail_weight[...] = jnp.zeros_like(tail_weight)

    out_ref[...] += nt(left(mixed_ref[...]), right_t(weight_ref[0, :, : z.main]))
    last = weight_ref[0, :, z.main :]
    last = jnp.concatenate([last, jnp.zeros((last.shape[0], LANES - z.extra), F32)], axis=1)
    tail_weight[...] += pltpu.roll(last, z.extra * step, 1)

    @pl.when(step == z.basis - 1)
    def _():
        out_ref[...] += nt(left(tail_ref[...]), right_t(tail_weight[...]))


def conv(z, mixed, weight, base, bias):
    return pl.pallas_call(
        partial(conv_body, z),
        name="conv",
        grid=(z.basis,),
        in_specs=[
            pl.BlockSpec((z.pixels, z.main), lambda k: (0, k)),
            pl.BlockSpec((z.pixels, LANES), lambda k: (0, z.basis * z.tiles)),
            pl.BlockSpec((1, z.width, z.joined), lambda k: (k, 0, 0)),
            full((z.pixels, z.width)),
            full(bias.shape),
        ],
        out_specs=result((z.pixels, z.width)),
        out_shape=jax.ShapeDtypeStruct((z.pixels, z.width), F32),
        scratch_shapes=[pltpu.VMEM((z.width, LANES), F32)],
        compiler_params=params(44),
        cost_estimate=cost(z.pixels * z.depth * z.width, 4 * z.depth * (z.width + z.pixels)),
    )(mixed, mixed, weight, base, bias)


def mlp_body(
    z,
    info_ref,
    middle_ref,
    cot_ref,
    d_active_ref,
    weight_ref,
    bias_ref,
    gain_ref,
    shift_ref,
    kept_ref,
    sent_ref,
    active_high_ref,
    active_low_ref,
    d_pre_high_ref,
    d_pre_low_ref,
    d_bias_ref,
    second_ref,
    second_lhs,
    second_t,
    cot_t,
):
    step = pl.program_id(0)
    main = z.main

    @pl.when(step == 0)
    def _():
        norm, _ = normalize(middle_ref[...])
        second = norm * row(gain_ref) + row(shift_ref)
        second_ref[...] = second
        second_lhs[...] = left(second[:, :main])
        second_t[...] = left(padded_t(second, z.wide)[: z.high])
        cot_t[...] = left(padded_t(cot_ref[...], z.wide)[: z.high])

    def store(out_ref, value, last):
        if not last:
            for i in range(z.tiles):
                out_ref[step, i * z.high : (i + 1) * z.high, :] = value[:, i * LANES : (i + 1) * LANES]
            return
        fill = jnp.zeros((z.wide - z.high, LANES), F32)
        value = jnp.transpose(jnp.concatenate([value, fill], axis=0))[:8]
        for i in range(z.parts):
            half, place = i // (z.parts // 2), i % (z.parts // 2)
            rows = slice(z.tiles * z.high + 8 * place, z.tiles * z.high + 8 * place + 8)
            out_ref[half, rows, :] = value[:, i * LANES : (i + 1) * LANES]

    def body(width, last):
        weight = only(z, weight_ref[:, :width], last)
        start = z.steps * main if last else pl.multiple_of(step * main, LANES)
        bias = bias_ref[pl.ds(start, z.rest if last else width)]
        bias = bias.reshape(1, bias.shape[0])
        if last:
            bias = jnp.concatenate([bias, jnp.zeros((1, width - z.rest), F32)], axis=1)
        d_active = only(z, d_active_ref[:, :width], last)
        pre = nn(second_lhs[...], right(weight[:main]))
        pre = pre + second_ref[:, main : main + 1] * weight[main : main + 1] + bias
        cdf = 0.5 * (1.0 + lax.erf(pre * np.float32(0.5**0.5)))
        pdf = jnp.exp(pre * pre * -0.5) * np.float32(1.0 / np.sqrt(2.0 * np.pi))
        active = only(z, pre * cdf, last)
        d_pre = d_active * (cdf + pre * pdf)
        high, low = split(active)
        active_high_ref[:, :width] = high
        active_low_ref[:, :width] = low
        output_grad = nn(cot_t[...], jnp.concatenate([high, low, high], axis=0))
        high, low = split(d_pre)
        d_pre_high_ref[:, :width] = high
        d_pre_low_ref[:, :width] = low
        d_bias_ref[:, :width] = jnp.sum(d_pre, axis=0, keepdims=True)
        hidden_grad = nn(second_t[...], jnp.concatenate([high, low, high], axis=0))

        @pl.when(info_ref[0] == 0)
        def _():
            store(kept_ref, output_grad, last)
            store(sent_ref, hidden_grad, last)

        @pl.when(info_ref[0] != 0)
        def _():
            store(sent_ref, output_grad, last)
            store(kept_ref, hidden_grad, last)

    hidden_steps(z, body)


def mlp(z, info, middle, cot, d_active, weight, bias, gain, shift):
    flat = (2, z.mlp_half, LANES)
    hidden = pl.BlockSpec((z.pixels, z.main), lambda i, *_: (0, i))
    wide = pltpu.HBM((z.pixels, z.hidden), BF16)
    return pl.pallas_call(
        partial(mlp_body, z),
        name="mlp",
        grid_spec=pltpu.PrefetchScalarGridSpec(
            num_scalar_prefetch=1,
            grid=(z.steps + 1,),
            in_specs=[
                full((z.pixels, z.width)),
                full((z.pixels, z.width)),
                hidden,
                pl.BlockSpec((z.width, z.main), lambda i, *_: (0, i)),
                full(bias.shape),
                full(gain.shape),
                full(shift.shape),
            ],
            out_specs=[
                full(flat),
                full(flat),
                hidden,
                hidden,
                hidden,
                hidden,
                pl.BlockSpec((1, z.main), lambda i, *_: (0, i)),
            ],
            scratch_shapes=[
                pltpu.VMEM((z.pixels, z.width), F32),
                pltpu.VMEM((z.pixels, 3 * z.main), BF16),
                pltpu.VMEM((z.high, 3 * z.pixels), BF16),
                pltpu.VMEM((z.high, 3 * z.pixels), BF16),
            ],
        ),
        out_shape=[
            jax.ShapeDtypeStruct(flat, F32),
            jax.ShapeDtypeStruct(flat, F32),
            wide,
            wide,
            wide,
            wide,
            jax.ShapeDtypeStruct((1, z.hidden), F32),
        ],
        compiler_params=params(44),
        cost_estimate=cost(3 * z.pixels * z.width * z.hidden, 12 * z.width * z.hidden),
    )(info, middle, cot, d_active, weight, bias, gain, shift)


def middle_back_body(z, high_ref, low_ref, weight_ref, middle_ref, cot_ref, gain_ref, out_ref, out_t_ref, sums_ref, d_second):
    step = pl.program_id(0)

    @pl.when(step == 0)
    def _():
        d_second[...] = jnp.zeros_like(d_second)

    def body(width, last):
        high = only(z, high_ref[:, :width], last)
        low = only(z, low_ref[:, :width], last)
        weight = right_t(only(z, weight_ref[:, :width], last))
        d_second[...] += nt(jnp.concatenate([high, high, low], axis=1), weight)

    hidden_steps(z, body)

    @pl.when(step == z.steps)
    def _():
        norm, inverse = normalize(middle_ref[...])
        grad = d_second[...]
        sums_ref[0:1, :] = jnp.sum(grad * norm, axis=0, keepdims=True)
        sums_ref[1:2, :] = jnp.sum(grad, axis=0, keepdims=True)
        cot = cot_ref[...]
        sums_ref[3:4, :] = jnp.sum(cot, axis=0, keepdims=True)
        d_middle = cot + norm_back(grad * row(gain_ref), norm, inverse)
        sums_ref[2:3, :] = jnp.sum(d_middle, axis=0, keepdims=True)
        out_ref[...] = d_middle
        out_t_ref[...] = padded_t(d_middle, z.wide)[: z.high]


def middle_back(z, high, low, weight, middle, cot, gain):
    hidden = pl.BlockSpec((z.pixels, z.main), lambda i: (0, i))
    return pl.pallas_call(
        partial(middle_back_body, z),
        name="middle_back",
        grid=(z.steps + 1,),
        in_specs=[
            hidden,
            hidden,
            pl.BlockSpec((z.width, z.main), lambda i: (0, i)),
            full((z.pixels, z.width)),
            full((z.pixels, z.width)),
            full(gain.shape),
        ],
        out_specs=[
            full((z.pixels, z.width)),
            full((z.high, z.pixels)),
            full((4, z.width)),
        ],
        out_shape=[
            jax.ShapeDtypeStruct((z.pixels, z.width), F32),
            jax.ShapeDtypeStruct((z.high, z.pixels), F32),
            jax.ShapeDtypeStruct((4, z.width), F32),
        ],
        scratch_shapes=[pltpu.VMEM((z.pixels, z.width), F32)],
        compiler_params=params(58),
        cost_estimate=cost(z.pixels * z.width * z.hidden, 8 * z.width * z.hidden),
    )(high, low, weight, middle, cot, gain)


def output_body(z, high_ref, low_ref, weight_ref, middle_ref, bias_ref, out_ref):
    @pl.when(pl.program_id(0) == 0)
    def _():
        out_ref[...] = middle_ref[...] + row(bias_ref)

    def body(width, last):
        high = only(z, high_ref[:, :width], last)
        low = only(z, low_ref[:, :width], last)
        weight = right_t(only(z, weight_ref[:, :width], last))
        out_ref[...] += nt(jnp.concatenate([high, high, low], axis=1), weight)

    hidden_steps(z, body)


def output(z, high, low, weight, middle, bias):
    hidden = pl.BlockSpec((z.pixels, z.main), lambda i: (0, i))
    return pl.pallas_call(
        partial(output_body, z),
        name="output",
        grid=(z.steps + 1,),
        in_specs=[
            hidden,
            hidden,
            pl.BlockSpec((z.width, z.main), lambda i: (0, i)),
            full((z.pixels, z.width)),
            full(bias.shape),
        ],
        out_specs=full((z.pixels, z.width)),
        out_shape=jax.ShapeDtypeStruct((z.pixels, z.width), F32),
        compiler_params=params(58),
        cost_estimate=cost(z.pixels * z.width * z.hidden, 8 * z.width * z.hidden),
    )(high, low, weight, middle, bias)


def conv_grad_body(z, info_ref, own_ref, far_ref, own_t_ref, far_t_ref, out_ref, lhs):
    step = pl.program_id(0)
    tiles = own_ref.shape[1] // LANES

    @pl.when(step == 0)
    def _():
        lhs[...] = left(jnp.concatenate([own_t_ref[...], far_t_ref[...]], axis=1))
        used = pl.num_programs(0) * tiles * z.high
        out_ref[used:, :] = jnp.zeros((out_ref.shape[0] - used, LANES), F32)

    value = nn(lhs[...], right(jnp.concatenate([own_ref[...], far_ref[...]], axis=0)))
    for i in range(tiles):
        rows = pl.ds(pl.multiple_of((step * tiles + i) * z.high, 8), z.high)
        out_ref[rows, :] = value[:, i * LANES : (i + 1) * LANES]


def conv_grad(z, info, mixed, far_mixed, own_t, far_t):
    count = z.half // LANES // 2
    tiles = 3
    steps = count // tiles
    flat = round_up(count * z.high, 32)
    return pl.pallas_call(
        partial(conv_grad_body, z),
        name="conv_grad",
        grid_spec=pltpu.PrefetchScalarGridSpec(
            num_scalar_prefetch=1,
            grid=(steps,),
            in_specs=[
                pl.BlockSpec((z.pixels, tiles * LANES), lambda i, c: (0, (2 * c[0] + c[1]) * steps + i)),
                pl.BlockSpec((z.pixels, tiles * LANES), lambda i, c: (0, c[1] * steps + i)),
                full((z.high, z.pixels)),
                full((z.high, z.pixels)),
            ],
            out_specs=full((flat, LANES)),
            scratch_shapes=[pltpu.VMEM((z.high, 6 * z.pixels), BF16)],
        ),
        out_shape=jax.ShapeDtypeStruct((flat, LANES), F32),
        compiler_params=params(50),
        cost_estimate=cost(2 * z.pixels * z.width * count * LANES, 12 * z.pixels * count * LANES),
    )(info, mixed, far_mixed, own_t, far_t)


def mixed_back_body(z, weight_ref, dm_ref, high_ref, low_ref, lhs):
    columns, main = z.columns, z.main

    @pl.when(pl.program_id(0) == 0)
    def _():
        lhs[...] = left(dm_ref[:, :main])

    value = nn(lhs[...], right(weight_ref[0, :main, :]))
    value = value + dm_ref[:, main : main + 1] * weight_ref[0, main : main + 1, :]
    value_high, value_low = split(value)
    for b in range(z.samples):
        for r in range(z.rows):
            i = (b * z.rows + r) * columns
            lane = b * z.wide
            high_ref[r, :, lane : lane + z.joined] = value_high[i : i + columns]
            low_ref[r, :, lane : lane + z.joined] = value_low[i : i + columns]


def mixed_back(z, weight, d_middle):
    out = pl.BlockSpec((z.rows, z.columns, z.samples * z.wide), lambda i: (0, i, 0))
    shape = pltpu.HBM((z.rows, z.basis * z.columns, z.samples * z.wide), BF16)
    return pl.pallas_call(
        partial(mixed_back_body, z),
        name="mixed_back",
        grid=(z.basis,),
        in_specs=[
            pl.BlockSpec((1, z.width, z.joined), lambda i: (i, 0, 0)),
            full((z.pixels, z.width)),
        ],
        out_specs=[out, out],
        out_shape=[shape, shape],
        scratch_shapes=[pltpu.VMEM((z.pixels, 3 * z.main), BF16)],
        compiler_params=params(56),
        cost_estimate=cost(z.pixels * z.depth * z.width, 4 * z.depth * z.width),
    )(weight, d_middle)


def outer_columns(z, value):
    return jnp.concatenate([value[z.columns + LON_HALO : z.columns + 2 * LON_HALO], value[:LON_HALO]], axis=0)


def band_back_body(z, high_ref, low_ref, band_ref, out_ref, top_ref, bottom_ref, sides_ref):
    row_at = pl.program_id(0)
    columns = z.columns

    @pl.when(row_at == 0)
    def _():
        out_ref[...] = jnp.zeros_like(out_ref)

    spread = [band(band_ref[0, k : k + 1, :], columns) for k in range(z.basis)]
    spread = jnp.transpose(jnp.concatenate(spread, axis=0))[: z.taps]
    high, low = split(spread)
    top, rest = high_ref[0], low_ref[0]
    value = nn(high, top) + nn(high, rest) + nn(low, top)
    place = pl.ds(pl.multiple_of(row_at * z.span, 8), z.taps)
    for b in range(z.samples):
        out_ref[b, place, :] += value[:, b * z.wide : b * z.wide + z.joined]

    @pl.when(row_at == z.rows - 1)
    def _():
        for b in range(z.samples):
            for r in range(z.rows + 2 * LAT_HALO):
                value = out_ref[b, r * z.span : r * z.span + columns + 2 * LON_HALO, :]
                if r < LAT_HALO:
                    top_ref[b, r] = value
                elif r < z.rows + LAT_HALO:
                    sides_ref[b, r - LAT_HALO] = outer_columns(z, value)
                else:
                    bottom_ref[b, r - z.rows - LAT_HALO] = value


def band_back(z, high, low, bands):
    lanes = round_up(z.taps, LANES)
    bands = jnp.pad(bands, ((0, 0), (0, 0), (0, lanes - z.taps)))
    height = (z.rows + 2 * LAT_HALO) * z.span
    rim = (z.samples, LAT_HALO, z.columns + 2 * LON_HALO, z.joined)
    shapes = [(z.samples, height, z.joined), rim, rim, (z.samples, z.rows, 2 * LON_HALO, z.joined)]
    part = pl.BlockSpec((1,) + high.shape[1:], lambda i: (i, 0, 0))
    return pl.pallas_call(
        partial(band_back_body, z),
        name="band_back",
        grid=(z.rows,),
        in_specs=[part, part, pl.BlockSpec((1, z.basis, lanes), lambda i: (i, 0, 0))],
        out_specs=[full(shape) for shape in shapes],
        out_shape=[jax.ShapeDtypeStruct(shape, F32) for shape in shapes],
        compiler_params=params(56),
        cost_estimate=cost(z.pixels * z.basis * z.taps * z.joined, 8 * z.pixels * z.depth),
    )(high, low, bands)


def edge_body(z, sides_ref, above_ref, below_ref, out_ref):
    for b in range(z.samples):
        for r in range(z.rows):
            value = sides_ref[b, r]
            if r < LAT_HALO:
                value = value + outer_columns(z, above_ref[b, r])
            if r >= z.rows - LAT_HALO:
                value = value + outer_columns(z, below_ref[b, r - z.rows + LAT_HALO])
            out_ref[b, r] = value


def edge(z, sides, above, below):
    return pl.pallas_call(
        partial(edge_body, z),
        name="edge",
        out_shape=jax.ShapeDtypeStruct(sides.shape, F32),
        compiler_params=params(16),
        cost_estimate=cost(2**30, 2**24),
    )(sides, above, below)


def finish_body(
    z, padded_ref, above_ref, below_ref, sides_ref, inputs_ref, d_middle_ref, gain_ref, sums_ref, d_bias_ref, out_ref, vectors_ref, own
):
    sample = pl.program_id(0)

    @pl.when(sample == 0)
    def _():
        own[...] = jnp.zeros_like(own)

    for r in range(z.rows):
        start = (r + LAT_HALO) * z.span
        value = padded_ref[0, start : start + z.columns + 2 * LON_HALO, :]
        if r < LAT_HALO:
            value = value + above_ref[0, r]
        if r >= z.rows - LAT_HALO:
            value = value + below_ref[0, r - z.rows + LAT_HALO]
        middle = value[2 * LON_HALO : z.columns]
        low = value[LON_HALO : 2 * LON_HALO] + sides_ref[0, r, :LON_HALO]
        high = value[z.columns : z.columns + LON_HALO] + sides_ref[0, r, LON_HALO:]
        grad = jnp.concatenate([low, middle, high], axis=0)[:, : z.width]
        norm, inverse = normalize(inputs_ref[0, r])
        own[0:1, :] += jnp.sum(grad * norm, axis=0, keepdims=True)
        own[1:2, :] += jnp.sum(grad, axis=0, keepdims=True)
        grad = norm_back(grad * row(gain_ref), norm, inverse)
        out_ref[0, r] = d_middle_ref[0, r] + grad

    @pl.when(sample == pl.num_programs(0) - 1)
    def _():
        vectors_ref[...] = jnp.zeros_like(vectors_ref)
        row = 0
        rows = [(sums_ref, 2), (own, 0), (own, 1), (sums_ref, 0), (sums_ref, 1), (d_bias_ref, 0), (sums_ref, 3)]
        for ref, at in rows:
            size = ref.shape[1]
            for i in range(0, size, LANES):
                end = min(i + LANES, size)
                vectors_ref[row : row + 1, : end - i] = ref[at : at + 1, i:end]
                row += 1


def finish(z, padded, above, below, sides, inputs, d_middle, gain, sums, d_bias):
    shape = (z.samples, z.rows, z.columns, z.width)
    count = round_up(6 * pl.cdiv(z.width, LANES) + pl.cdiv(z.hidden, LANES), 16)

    def part(array):
        size = array.shape[1:]
        return pl.BlockSpec((1,) + size, lambda b: (b,) + (0,) * len(size))

    d_middle = d_middle.reshape(shape)
    arrays = [padded, above, below, sides, inputs, d_middle]
    return pl.pallas_call(
        partial(finish_body, z),
        name="finish",
        grid=(z.samples,),
        in_specs=[part(a) for a in arrays] + [full(gain.shape), full(sums.shape), full(d_bias.shape)],
        out_specs=[part(inputs), full((count, LANES))],
        out_shape=[jax.ShapeDtypeStruct(shape, F32), jax.ShapeDtypeStruct((count, LANES), F32)],
        scratch_shapes=[pltpu.VMEM((8, z.width), F32)],
        compiler_params=params(60),
        cost_estimate=cost(2**30, 2**24),
    )(*arrays, gain, sums, d_bias)


def conv_place_body(z, which, first, count, info_ref, *refs):
    number = len(which)
    pieces, (out_ref, held, narrow, sems) = refs[:number], refs[-4:]
    main_tiles = z.basis * z.tiles
    with_extra = first + 2 * count == z.half // LANES
    used = count * z.high

    def get(i):
        return pltpu.make_async_copy(pieces[i].at[pl.ds(0, used), :], held.at[i], sems.at[i])

    def tile(i, t):
        return (info_ref[which[i]] // 2) * (z.half // LANES) + first + (info_ref[which[i]] % 2) * count + t

    def put(i, t):
        at = tile(i, t)
        lanes = pl.ds(pl.multiple_of(at % z.tiles * LANES, LANES), LANES)
        return pltpu.make_async_copy(
            held.at[i, pl.ds(t * z.high, z.width), :],
            out_ref.at[at // z.tiles, :, lanes],
            sems.at[number + i * count + t],
        )

    def put_extra(k):
        return pltpu.make_async_copy(
            narrow.at[k], out_ref.at[k, :, pl.ds(z.main, z.extra)], sems.at[number * (1 + count) + k]
        )

    for i in range(number):
        get(i).start()
    for i in range(number):
        get(i).wait()
        for t in range(count):
            is_main = tile(i, t) < main_tiles

            @pl.when(is_main)
            def _():
                put(i, t).start()

            if with_extra and t == count - 1:

                @pl.when(jnp.logical_not(is_main))
                def _():
                    for k in range(z.basis):
                        value = held[i, t * z.high : (t + 1) * z.high, :]
                        value = value if k == 0 else pltpu.roll(value, LANES - z.extra * k, 1)
                        narrow[k] = value[: z.width, : z.extra]
                        put_extra(k).start()

    for i in range(number):
        if with_extra:

            @pl.when(tile(i, count - 1) >= main_tiles)
            def _():
                for k in range(z.basis):
                    put_extra(k).wait()

        for t in range(count):

            @pl.when(tile(i, t) < main_tiles)
            def _():
                put(i, t).wait()


def conv_place(z, places, which, first, count, pieces, onto):
    anywhere = pl.BlockSpec(memory_space=pl.ANY)
    operands = [places, *pieces]
    aliases = {}
    if onto is not None:
        operands.append(onto)
        aliases = {1 + len(which): 0}
    return pl.pallas_call(
        partial(conv_place_body, z, which, first, count),
        name="conv_place",
        grid_spec=pltpu.PrefetchScalarGridSpec(
            num_scalar_prefetch=1,
            grid=(),
            in_specs=[anywhere] * (len(operands) - 1),
            out_specs=anywhere,
            scratch_shapes=[
                pltpu.VMEM((len(which), count * z.high, LANES), F32),
                pltpu.VMEM((z.basis, z.width, z.extra), F32),
                pltpu.SemaphoreType.DMA((len(which) * (1 + count) + z.basis,)),
            ],
        ),
        out_shape=jax.ShapeDtypeStruct((z.basis, z.width, z.joined), F32),
        input_output_aliases=aliases,
        compiler_params=params(16),
        cost_estimate=cost(2**30, 2**24),
    )(*operands)


def mlp_place_body(z, info_ref, own_ref, far_ref, output_ref, hidden_ref, held, narrow, sems):
    main_tiles = 2 * z.tiles

    def place(refs):
        gets = []
        for i, ref in enumerate(refs):
            for half in range(2):
                rows = pl.ds(half * z.mlp_half, z.mlp_half)
                gets.append(pltpu.make_async_copy(ref.at[rows, :], held.at[i, half], sems.at[2 * i + half]))
                gets[-1].start()
        puts = []
        for i, out_ref in enumerate((output_ref, hidden_ref)):
            for t in range(main_tiles):
                half = t // z.tiles
                if t % z.tiles == 0:
                    gets[2 * i + half].wait()
                puts.append(
                    pltpu.make_async_copy(
                        held.at[i, half, pl.ds(t % z.tiles * z.high, z.width), :],
                        out_ref.at[:, pl.ds(t * LANES, LANES)],
                        sems.at[8 + i * main_tiles + t],
                    )
                )
                puts[-1].start()
            start = z.tiles * z.high
            parts = [
                held[i, half, start + 8 * j : start + 8 * j + 8, :] for half in range(2) for j in range(z.parts // 2)
            ]
            value = jnp.concatenate([jnp.concatenate(parts, axis=1)] * (LANES // 8), axis=0)
            narrow[i] = jnp.transpose(value)[: z.width, : z.rest]
            puts.append(
                pltpu.make_async_copy(
                    narrow.at[i],
                    out_ref.at[:, pl.ds(main_tiles * LANES, z.rest)],
                    sems.at[8 + 2 * main_tiles + i],
                )
            )
            puts[-1].start()
        for c in puts:
            c.wait()

    pl.when(info_ref[0] == 0)(lambda: place((own_ref, far_ref)))
    pl.when(info_ref[0] != 0)(lambda: place((far_ref, own_ref)))


def mlp_place(z, info, own, far):
    shape = jax.ShapeDtypeStruct((z.width, z.hidden), F32)
    anywhere = pl.BlockSpec(memory_space=pl.ANY)
    return pl.pallas_call(
        partial(mlp_place_body, z),
        name="mlp_place",
        grid_spec=pltpu.PrefetchScalarGridSpec(
            num_scalar_prefetch=1,
            grid=(),
            in_specs=[anywhere, anywhere],
            out_specs=[anywhere, anywhere],
            scratch_shapes=[
                pltpu.VMEM((2, 2, z.mlp_half, LANES), F32),
                pltpu.VMEM((2, z.width, z.rest), F32),
                pltpu.SemaphoreType.DMA((4 * z.tiles + 10,)),
            ],
        ),
        out_shape=[shape, shape],
        compiler_params=params(16),
        cost_estimate=cost(2**30, 2**24),
    )(info, own, far)


def axis_size(axes):
    size = 1
    for axis in axes:
        size *= lax.axis_size(axis)
    return size


def pairs(lats, lons, target):
    found = []
    for lat in range(lats):
        for lon in range(lons):
            to_lat, to_lon = target(lat, lon)
            found.append((lat * lons + lon, to_lat * lons + to_lon))
    return found


class GridSum:
    def __init__(self):
        lats, lons = axis_size(LAT), axis_size(LON)
        lat, lon = lax.axis_index(LAT), lax.axis_index(LON)
        over = partial(pairs, lats, lons)
        self.core = lat % 2
        self.cores = over(lambda a, o: (a ^ 1, o))
        self.first = over(lambda a, o: (a ^ 2, o) if a % 2 else (a, o ^ 1))
        self.second = over(lambda a, o: (a, o ^ 1) if a % 2 else (a ^ 2, o))
        self.third = over(lambda a, o: (a ^ 4, o))
        lon_bit, lat_bit = lon % 2, lat // 2 % 2
        self.first_bit = jnp.where(self.core == 0, lon_bit, lat_bit)
        self.second_bit = jnp.where(self.core == 0, lat_bit, lon_bit)
        self.third_bit = lat // 4 % 2
        far_bit = jnp.where(self.core == 0, lat_bit, lon_bit)
        mine, other = 2 * self.core, 2 * (1 - self.core)
        self.places = jnp.stack(
            [mine + self.first_bit, mine + 1 - self.first_bit, other + far_bit, other + 1 - far_bit]
        ).astype(jnp.int32)
        self.others = []
        bit = 8
        while bit < lats:
            self.others.append(over(lambda a, o, bit=bit: (a ^ bit, o)))
            bit *= 2
        bit = 2
        while bit < lons:
            self.others.append(over(lambda a, o, bit=bit: (a, o ^ bit)))
            bit *= 2

    def swap(self, value, where):
        return lax.ppermute(value, AXES, where)

    def all(self, value, where):
        return value + self.swap(value, where)


class Order:
    def __init__(self):
        self.last = ()
        self.held = True

    def use(self, value):
        if not self.held:
            return value
        value, self.last = lax.optimization_barrier((value, self.last))
        return value

    def mark(self, value):
        if self.held:
            self.last = (value,)
        return value

    def wait(self, value):
        return self.mark(self.use(value))

    def run(self, function, *values):
        return self.mark(function(*self.use(values)))


def sum_rows(size, index, arrays, vectors):
    count = 0 if vectors is None else vectors.shape[0]

    def body(index_ref, *refs):
        out_ref = refs[-1]
        total = refs[0][...]
        for ref in refs[1 : len(arrays)]:
            total = total + ref[...]
        out_ref[:size, :] = total
        if vectors is not None:
            out_ref[size:, :] = refs[len(arrays)][...]

    more = [] if vectors is None else [vectors]
    blocks = [pl.BlockSpec((size, LANES), lambda g, p, i=i: (p[i], 0)) for i in range(len(arrays))]
    return pl.pallas_call(
        body,
        name="sum_rows",
        grid_spec=pltpu.PrefetchScalarGridSpec(
            num_scalar_prefetch=1,
            grid=(1,),
            in_specs=blocks + [full(v.shape) for v in more],
            out_specs=full((size + count, LANES)),
        ),
        out_shape=jax.ShapeDtypeStruct((size + count, LANES), F32),
        compiler_params=params(16),
        cost_estimate=cost(2**30, 2**24),
    )(index, *arrays, *more)


def join_rows(size, bit, value, far):
    rows = value.shape[0] + size

    def body(bit_ref, value_ref, far_ref, out_ref):
        at = bit_ref[0]
        out_ref[pl.ds(pl.multiple_of(at * size, 8), size), :] = value_ref[:size, :]
        out_ref[pl.ds(pl.multiple_of((1 - at) * size, 8), size), :] = far_ref[:size, :]
        if rows > 2 * size:
            out_ref[2 * size :, :] = value_ref[size:, :] + far_ref[size:, :]

    return pl.pallas_call(
        body,
        name="join_rows",
        grid_spec=pltpu.PrefetchScalarGridSpec(
            num_scalar_prefetch=1,
            grid=(1,),
            in_specs=[full(value.shape), full(far.shape)],
            out_specs=full((rows, LANES)),
        ),
        out_shape=jax.ShapeDtypeStruct((rows, LANES), F32),
        compiler_params=params(16),
        cost_estimate=cost(2**30, 2**24),
    )(bit.reshape(1).astype(jnp.int32), value, far)


def add_rows(value, far, start=0):
    def body(value_ref, far_ref, out_ref):
        out_ref[...] = value_ref[...] + far_ref[start:, :]

    return pl.pallas_call(
        body,
        name="add_rows",
        out_shape=jax.ShapeDtypeStruct(value.shape, F32),
        compiler_params=params(16),
        cost_estimate=cost(2**30, 2**24),
    )(value, far)


class Chunk:
    def __init__(self, total, order, name, sent, kept):
        self.total, self.order, self.name = total, order, name
        self.terms, self.size = [(kept, 0)], sent.shape[0]
        self.vectors = None
        self.send("scatter_first", order.wait(sent), total.first)

    def send(self, step, value, where):
        with jax.named_scope(f"{self.name}_{step}"):
            self.value, self.far = value, self.total.swap(value, where)

    def take(self, index):
        arrays = [value for value, _ in self.terms]
        at = jnp.stack([jnp.asarray(index(at), jnp.int32) for _, at in self.terms])
        return self.order.run(partial(sum_rows, self.size), at, arrays, None)

    def halve(self, step, where, bit):
        self.terms.append((self.far, 0))
        self.size //= 2
        sent = self.take(lambda at: 2 * at + 1 - bit)
        self.terms = [(value, 2 * at + bit) for value, at in self.terms]
        self.send(step, sent, where)

    def join(self, bit):
        self.value = self.order.run(partial(join_rows, self.size), bit, self.value, self.far)
        self.size *= 2

    def scatter_second(self):
        self.halve("scatter_second", self.total.second, self.total.second_bit)

    def across_first(self):
        self.halve("across_first", self.total.third, self.total.third_bit)

    def across_second(self):
        self.terms.append((self.far, 0))
        self.value = self.take(lambda at: at)
        for where in self.total.others[:-1]:
            self.send("across", self.value, where)
            self.value = self.order.run(add_rows, self.value, self.far)
        self.send("across_second", self.value, self.total.others[-1])

    def across_third(self):
        both = [self.value, self.far]
        value = self.order.run(partial(sum_rows, self.size), jnp.zeros((2,), jnp.int32), both, self.vectors)
        self.send("across_third", value, self.total.third)

    def gather_second(self):
        self.join(self.total.third_bit)
        self.send("gather_second", self.value, self.total.second)

    def gather_first(self):
        self.join(self.total.second_bit)
        self.send("gather_first", self.value, self.total.first)
        with jax.named_scope(f"{self.name}_near_core"):
            self.near = self.total.swap(self.value, self.total.cores)

    def gather_whole(self):
        self.join(self.total.first_bit)
        with jax.named_scope(f"{self.name}_near_core"):
            self.near = self.total.swap(self.value, self.total.cores)

    def gather_core(self):
        self.far = self.order.wait(self.far)
        with jax.named_scope(f"{self.name}_gather_core"):
            self.last = self.total.swap(self.far, self.total.cores)

    def pieces(self):
        return self.value, self.far, self.near, self.last


def after(value, *others):
    return lax.optimization_barrier((value, others))[0]


def rows_of(vector):
    size = round_up(vector.shape[0], LANES)
    return jnp.pad(vector, (0, size - vector.shape[0])).reshape(-1, LANES)


def moved(value, axis, steps, cycle):
    count = axis_size(axis)
    if cycle:
        where = [(i, (i + steps) % count) for i in range(count)]
    else:
        where = [(i, i + steps) for i in range(max(0, -steps), min(count, count - steps))]
    return lax.ppermute(value, axis, where)


def edges(sides, down):
    lats, lons = axis_size(LAT), axis_size(LON)

    def shifted(value, steps):
        where = [
            (lat * lons + lon, (lat + down) * lons + (lon + steps) % lons)
            for lat in range(max(0, -down), min(lats, lats - down))
            for lon in range(lons)
        ]
        return lax.ppermute(value, AXES, where)

    if lons == 2:
        return shifted(sides, 1)
    return jnp.concatenate([shifted(sides[:, :, :LON_HALO], 1), shifted(sides[:, :, LON_HALO:], -1)], axis=2)


def local(
    inputs,
    noise_field,
    basis_values,
    row_reach,
    conv_weight,
    conv_bias,
    first_gain,
    first_shift,
    second_gain,
    second_shift,
    hidden_weight,
    hidden_bias,
    output_weight,
    output_bias,
    cotangent,
):
    z = Sizes(inputs, noise_field, conv_weight, hidden_weight)
    total = GridSum()
    lat, lats = lax.axis_index(LAT), axis_size(LAT)
    info = jnp.stack([total.core, (lat > 0).astype(jnp.int32), (lat < lats - 1).astype(jnp.int32)])
    rows, columns, width = z.rows, z.columns, z.width
    flat = (z.pixels, width)
    cot = cotangent.reshape(flat)
    conv_weight = jnp.transpose(conv_weight, (0, 2, 1))
    output_weight = jnp.transpose(output_weight)

    noise = jnp.transpose(noise_field, (0, 1, 3, 2))
    top, bottom, top_sides, bottom_sides, sides = cut(z, inputs, noise)
    below, above = moved(top, LAT, -1, False), moved(bottom, LAT, 1, False)
    sides = [edges(bottom_sides, 1), edges(top_sides, -1), edges(sides, 0)]
    d_active = active_back(z, cot, output_weight)
    bands = band_rows(z, basis_values, row_reach)
    above, below, sides = after((above, below, sides), d_active)
    mixed, other = mix(z, info, bands, inputs, noise, above, below, sides, first_gain, first_shift)
    far_mixed = total.swap(other, total.cores)
    middle = conv(z, mixed, conv_weight, inputs.reshape(flat), conv_bias)
    kept, sent, active_high, active_low, d_pre_high, d_pre_low, d_hidden_bias = mlp(
        z, info, middle, cot, d_active, hidden_weight, hidden_bias, second_gain, second_shift
    )
    order = Order()
    arrived = total.swap(sent, total.cores)

    d_middle, d_middle_t, sums = order.run(
        partial(middle_back, z), d_pre_high, d_pre_low, hidden_weight, middle, cot, second_gain
    )
    far_t = total.swap(d_middle_t, total.cores)

    bit = total.first_bit
    kept, arrived = kept.reshape(-1, LANES), arrived.reshape(-1, LANES)
    add_half = lambda k, r, w: sum_rows(z.mlp_half, jnp.stack([w, w]).astype(jnp.int32), [k, r], None)
    m = Chunk(total, order, "m", order.run(add_half, kept, arrived, 1 - bit), None)
    m.terms = [(kept, bit), (arrived, bit)]
    half = lambda which: order.run(
        lambda *v: conv_grad(z, jnp.stack([total.core, which]), *v), mixed, far_mixed, d_middle_t, far_t
    )
    sent = half(1 - bit)
    m.scatter_second()
    c = Chunk(total, order, "c", sent, None)
    c.terms = [(half(bit), 0)]
    d_mixed = order.run(partial(mixed_back, z), conv_weight, d_middle)
    m.across_first()
    c.scatter_second()
    m.across_second()
    d_padded, top, bottom, sides = order.run(partial(band_back, z), *d_mixed, bands)
    c.across_first()
    m.across_third()
    top, bottom = order.wait((top, bottom))
    from_below = moved(top, LAT, -1, False)
    from_above = moved(bottom, LAT, 1, False)
    block_output = order.run(
        partial(output, z), active_high, active_low, output_weight, middle, output_bias
    )
    c.across_second()
    outer = order.run(partial(edge, z), sides, from_above, from_below)
    from_sides = edges(outer, 0)
    input_grad, vectors = order.run(
        partial(finish, z), d_padded, from_above, from_below, from_sides, inputs, d_middle, first_gain, sums, d_hidden_bias
    )

    m.gather_second()
    c.vectors = vectors
    c.across_third()
    m.gather_first()
    c.gather_second()
    m.gather_whole()
    output_weight_grad, hidden_weight_grad = order.run(lambda *v: mlp_place(z, info, *v), m.value, m.near)
    c.gather_first()
    place = partial(conv_place, z, total.places)
    count = z.half // LANES // 2
    conv_weight_grad = order.run(lambda *v: place((0, 2), 0, count, v, None), c.value, c.near)
    c.gather_core()
    sums_at = [total.cores] + total.others
    place_far = lambda *v: place((1,), 0, count, v[:1], v[1])
    place_last = lambda *v: place((3,), 0, count, v[:1], v[1])
    vectors = order.run(lambda v, f: add_rows(v, f, c.size), c.value[c.size :], c.far)
    far_vectors = total.swap(vectors, sums_at[0])
    conv_weight_grad = order.run(place_far, c.far, conv_weight_grad)
    vectors = order.run(add_rows, vectors, far_vectors)
    far_vectors = total.swap(vectors, sums_at[1])
    conv_weight_grad = order.run(place_last, c.last, conv_weight_grad)
    vectors = order.run(add_rows, vectors, far_vectors)
    for where in sums_at[2:]:
        vectors = order.run(add_rows, vectors, total.swap(vectors, where))
    found, start = [], 0
    for size in (width,) * 5 + (z.hidden, width):
        count = pl.cdiv(size, LANES)
        found.append(vectors[start : start + count].reshape(-1)[:size])
        start += count
    conv_weight_grad = jnp.transpose(conv_weight_grad, (0, 2, 1))
    output_weight_grad = jnp.transpose(output_weight_grad)
    conv_bias_grad, first_gain_grad, first_shift_grad, second_gain_grad, second_shift_grad = found[:5]
    hidden_bias_grad, output_bias_grad = found[5:]
    return (
        block_output.reshape(inputs.shape),
        input_grad,
        conv_weight_grad,
        conv_bias_grad,
        first_gain_grad,
        first_shift_grad,
        second_gain_grad,
        second_shift_grad,
        hidden_weight_grad,
        hidden_bias_grad,
        output_weight_grad,
        output_bias_grad,
    )


def solution(mesh):
    lats, lons = mesh.shape["lat"], mesh.shape["lon"]
    fine = Mesh(mesh.devices.reshape(lats // 4, 2, 2, lons // 2, 2), AXES)
    grid = P(None, LAT, LON, None)
    weights = (P(),) * 10
    in_specs = (grid, grid, P(LAT, None, None, None), P(LAT)) + weights + (grid,)
    out_specs = (grid, grid) + weights
    return jax.shard_map(local, mesh=fine, in_specs=in_specs, out_specs=out_specs, check_vma=False)
```

```python
from functools import partial

import jax
import jax.numpy as jnp
import numpy as np
from jax import lax
from jax.experimental import pallas as pl
from jax.experimental.pallas import tpu as pltpu
from jax.sharding import Mesh, PartitionSpec as P

LAT_HALO = 2
LON_HALO = 4
EPSILON = 1e-05
F32 = jnp.float32
BF16 = jnp.bfloat16
LAT = ("z", "y", "core")
LON = ("w", "x")
AXES = LAT + LON
LANES = 128
STEP = 256


def split(value):
    high = value.astype(BF16)
    return high, (value - high.astype(F32)).astype(BF16)


def left(value):
    high, low = split(value)
    return jnp.concatenate([high, high, low], axis=1)


def right(value):
    high, low = split(value)
    return jnp.concatenate([high, low, high], axis=0)


def right_t(value):
    high, low = split(value)
    return jnp.concatenate([high, low, high], axis=1)


def nn(a, b):
    return lax.dot_general(a, b, (((1,), (0,)), ((), ())), preferred_element_type=F32)


def nt(a, b):
    return lax.dot_general(a, b, (((1,), (1,)), ((), ())), preferred_element_type=F32)


def params(megabytes=30):
    return pltpu.CompilerParams(vmem_limit_bytes=megabytes * 1024 * 1024)


def cost(macs, moved):
    return pl.CostEstimate(flops=12 * macs, bytes_accessed=moved, transcendentals=0)


def full(shape):
    return pl.BlockSpec(shape, lambda *_: (0,) * len(shape), pipeline_mode=pl.Buffered(1))


def result(shape):
    return pl.BlockSpec(shape, lambda *_: (0,) * len(shape))


def row(ref):
    return ref[...].reshape(1, ref.shape[0])


def round_up(value, to):
    return -(-value // to) * to


def normalize(field):
    average = jnp.mean(field, axis=-1, keepdims=True)
    centered = field - average
    variance = jnp.mean(centered * centered, axis=-1, keepdims=True)
    inverse = lax.rsqrt(variance + EPSILON)
    return centered * inverse, inverse


def norm_back(grad_norm, normalized, inverse):
    first_term = jnp.mean(grad_norm, axis=-1, keepdims=True)
    second_term = jnp.mean(grad_norm * normalized, axis=-1, keepdims=True)
    return inverse * (grad_norm - first_term - normalized * second_term)


def padded_t(value, size):
    return jnp.transpose(
        jnp.concatenate(
            [value, jnp.zeros((value.shape[0], size - value.shape[1]), value.dtype)], axis=1
        )
    )


class Sizes:
    def __init__(self, inputs, noise_field, conv_weight, hidden_weight):
        self.samples, self.rows, self.columns, self.width = inputs.shape
        self.joined = self.width + noise_field.shape[-1]
        self.basis = conv_weight.shape[0]
        self.hidden = hidden_weight.shape[1]
        self.pixels = self.samples * self.rows * self.columns
        self.main = self.width // LANES * LANES
        self.tiles = self.main // LANES
        self.extra = self.joined - self.main
        self.span = round_up(self.columns + 2 * LON_HALO, 16)
        self.taps = (2 * LAT_HALO + 1) * self.span
        self.depth = self.basis * self.main + LANES
        self.half = self.depth // 2
        self.wide = self.main + LANES
        self.high = round_up(self.width, 8)
        self.steps = self.hidden // self.main
        self.rest = self.hidden - self.steps * self.main
        self.parts = self.wide // LANES
        self.mlp_half = self.tiles * self.high + 8 * self.parts // 2


def hidden_steps(z, body):
    step = pl.program_id(0)
    pl.when(step < z.steps)(lambda: body(z.main, False))
    pl.when(step == z.steps)(lambda: body(LANES, True))


def only(z, value, last):
    if not last:
        return value
    valid = lax.broadcasted_iota(jnp.int32, (1, LANES), 1) < z.rest
    return jnp.where(valid, value.astype(F32), 0.0).astype(value.dtype)


def active_back_body(z, cot_ref, weight_ref, out_ref, lhs):
    main = z.main

    @pl.when(pl.program_id(0) == 0)
    def _():
        lhs[...] = left(cot_ref[:, :main])

    def body(width, last):
        product = nn(lhs[...], right(weight_ref[:main, :width]))
        out_ref[:, :width] = product + cot_ref[:, main : main + 1] * weight_ref[main : main + 1, :width]

    hidden_steps(z, body)


def active_back(z, cot, weight):
    return pl.pallas_call(
        partial(active_back_body, z),
        name="active_back",
        grid=(z.steps + 1,),
        in_specs=[
            full((z.pixels, z.width)),
            pl.BlockSpec((z.width, z.main), lambda i: (0, i)),
        ],
        out_specs=pl.BlockSpec((z.pixels, z.main), lambda i: (0, i)),
        out_shape=pltpu.HBM((z.pixels, z.hidden), F32),
        scratch_shapes=[pltpu.VMEM((z.pixels, 3 * z.main), BF16)],
        compiler_params=params(60),
        cost_estimate=cost(z.pixels * z.width * z.hidden, 8 * z.width * z.hidden),
    )(cot, weight)


def band_rows_body(z, reach_ref, basis_ref, stacked_ref, plain_ref):
    width = 2 * LON_HALO + 1
    height = 2 * LAT_HALO + 1
    offset = lax.broadcasted_iota(jnp.int32, (1, height * width), 1) % width - LON_HALO
    row_at = lax.broadcasted_iota(jnp.int32, (z.rows, 1), 0)
    reach = jnp.zeros((z.rows, 1), jnp.int32)
    for r in range(z.rows):
        reach = jnp.where(row_at == r, reach_ref[r], reach)
    values = [
        jnp.where(
            jnp.abs(offset) <= reach, jnp.concatenate([basis_ref[k, a] for a in range(height)], axis=1), 0.0
        )
        for k in range(z.basis)
    ]
    values = jnp.concatenate(values, axis=0)
    source = lax.broadcasted_iota(jnp.int32, (values.shape[1], z.taps), 0)
    target = lax.broadcasted_iota(jnp.int32, (values.shape[1], z.taps), 1)
    place = source // width * z.span + source % width
    onehot = (place == target).astype(BF16)
    high = values.astype(BF16)
    rest = values - high.astype(F32)
    low = rest.astype(BF16)
    last = (rest - low.astype(F32)).astype(BF16)
    high, low, last = nn(high, onehot), nn(low, onehot), nn(last, onehot)
    rest = low + last
    fill = jnp.zeros((values.shape[0], stacked_ref.shape[2] - 3 * z.taps), F32)
    stacked = jnp.concatenate([high, high, rest, fill], axis=1)
    fill = jnp.zeros((values.shape[0], plain_ref.shape[2] - z.taps), F32)
    plain = jnp.concatenate([high + rest, fill], axis=1)
    for r in range(z.rows):
        for k in range(z.basis):
            at = k * z.rows + r
            stacked_ref[r, k : k + 1, :] = stacked[at : at + 1]
            plain_ref[r, k : k + 1, :] = plain[at : at + 1]


def band_rows(z, basis_values, row_reach):
    flat = jnp.transpose(basis_values, (1, 2, 0, 3))
    shapes = [(z.rows, z.basis, round_up(3 * z.taps, LANES)), (z.rows, z.basis, round_up(z.taps, LANES))]
    return pl.pallas_call(
        partial(band_rows_body, z),
        name="band_rows",
        grid_spec=pltpu.PrefetchScalarGridSpec(
            num_scalar_prefetch=1,
            grid=(1,),
            in_specs=[full(flat.shape)],
            out_specs=[full(shape) for shape in shapes],
        ),
        out_shape=[jax.ShapeDtypeStruct(shape, F32) for shape in shapes],
        compiler_params=params(16),
    )(row_reach, flat)


def band(row, columns):
    spread = jnp.broadcast_to(row, (columns, row.shape[1]))
    return pltpu.roll(spread, 0, 1, stride=1, stride_axis=0)


def cut_body(z, inputs_ref, noise_ref, top_ref, bottom_ref, top_sides_ref, bottom_sides_ref, sides_ref):
    for b in range(z.samples):
        for i in range(z.rows):
            value = jnp.concatenate([inputs_ref[b, i], jnp.transpose(noise_ref[b, i])], axis=1)
            side = jnp.concatenate([value[z.columns - LON_HALO :], value[:LON_HALO]], axis=0)
            sides_ref[b, i] = side
            if i < LAT_HALO:
                top_ref[b, i] = value
                top_sides_ref[b, i] = side
            if i >= z.rows - LAT_HALO:
                bottom_ref[b, i - z.rows + LAT_HALO] = value
                bottom_sides_ref[b, i - z.rows + LAT_HALO] = side


def cut(z, inputs, noise):
    shape = lambda rows, columns: jax.ShapeDtypeStruct((z.samples, rows, columns, z.joined), F32)
    rim, side = shape(LAT_HALO, z.columns), shape(LAT_HALO, 2 * LON_HALO)
    return pl.pallas_call(
        partial(cut_body, z),
        name="cut",
        out_shape=[rim, rim, side, side, shape(z.rows, 2 * LON_HALO)],
        compiler_params=params(60),
    )(inputs, noise)


def mix_body(z, info_ref, band_ref, inputs_ref, noise_ref, above_ref, below_ref, above_sides_ref, below_sides_ref, sides_ref, gain_ref, shift_ref, mixed_ref, other_ref, lhs, high, low):
    at_row = pl.program_id(0)
    gap = z.span - z.columns - 2 * LON_HALO

    def place(sample, at, value, sides, present, gain, shift):
        value = jnp.concatenate([sides[:LON_HALO], value, sides[LON_HALO:]], axis=0)
        channel = lax.broadcasted_iota(jnp.int32, (1, z.joined), 1)
        inside = channel < z.width
        mean = jnp.sum(jnp.where(inside, value, 0.0), axis=1, keepdims=True) / z.width
        centered = jnp.where(inside, value - mean, 0.0)
        variance = jnp.sum(centered * centered, axis=1, keepdims=True) / z.width
        normed = centered * lax.rsqrt(variance + EPSILON) * gain + shift
        value = jnp.where(inside, normed, value) * present
        value = jnp.concatenate([value, jnp.zeros((value.shape[0], z.wide - z.joined), F32)], axis=1)
        value = jnp.concatenate([value, jnp.zeros((gap, z.wide), F32)], axis=0)
        high_part, low_part = split(value)
        rows, lanes = slice(at * z.span, (at + 1) * z.span), slice(sample * z.wide, (sample + 1) * z.wide)
        high[rows, lanes] = high_part
        low[rows, lanes] = low_part

    @pl.when(at_row == 0)
    def _():
        fill = jnp.zeros((1, z.joined - z.width), F32)
        gain = jnp.concatenate([row(gain_ref), fill], axis=1)
        shift = jnp.concatenate([row(shift_ref), fill], axis=1)
        has_above = (info_ref[1] != 0).astype(F32)
        has_below = (info_ref[2] != 0).astype(F32)
        for b in range(z.samples):
            for i in range(LAT_HALO):
                place(b, i, above_ref[b, i], above_sides_ref[b, i], has_above, gain, shift)
                place(b, i + z.rows + LAT_HALO, below_ref[b, i], below_sides_ref[b, i], has_below, gain, shift)
            for i in range(z.rows):
                value = jnp.concatenate([inputs_ref[b, i], jnp.transpose(noise_ref[b, i])], axis=1)
                place(b, i + LAT_HALO, value, sides_ref[b, i], 1.0, gain, shift)

    for k in range(z.basis):
        value = band(band_ref[0, k : k + 1, :], z.columns)
        lhs[k * z.columns : (k + 1) * z.columns, :] = value.astype(BF16)

    rows = pl.ds(pl.multiple_of(at_row * z.span, 16), z.taps)
    top, rest = high[rows, :], low[rows, :]
    product = nn(lhs[:, : 3 * z.taps], jnp.concatenate([top, rest, top], axis=0))
    for b in range(z.samples):
        tail = jnp.zeros((z.columns, LANES), F32)
        for k in range(z.basis):
            part = product[k * z.columns : (k + 1) * z.columns, b * z.wide : (b + 1) * z.wide]
            mixed_ref[b, :, k * z.main : (k + 1) * z.main] = part[:, : z.main]
            last = part[:, z.main :]
            tail = tail + (last if k == 0 else pltpu.roll(last, z.extra * k, 1))
        mixed_ref[b, :, z.basis * z.main :] = tail

    @pl.when(info_ref[0] == 0)
    def _():
        other_ref[...] = mixed_ref[:, :, z.half :]

    @pl.when(info_ref[0] != 0)
    def _():
        other_ref[...] = mixed_ref[:, :, : z.half]


def mix(z, info, bands, inputs, noise, above, below, sides, gain, shift):
    height = (z.rows + 2 * LAT_HALO) * z.span
    lanes = bands.shape[2]
    arrays = [inputs, noise, above, below, *sides, gain, shift]
    mixed, other = pl.pallas_call(
        partial(mix_body, z),
        name="mix",
        grid_spec=pltpu.PrefetchScalarGridSpec(
            num_scalar_prefetch=1,
            grid=(z.rows,),
            in_specs=[
                pl.BlockSpec((1, z.basis, lanes), lambda r, *_: (r, 0, 0)),
                *(full(a.shape) for a in arrays),
            ],
            out_specs=[
                pl.BlockSpec((z.samples, z.columns, z.depth), lambda r, *_: (0, r, 0)),
                pl.BlockSpec((z.samples, z.columns, z.half), lambda r, *_: (0, r, 0)),
            ],
            scratch_shapes=[
                pltpu.VMEM((z.basis * z.columns, lanes), BF16),
                pltpu.VMEM((height, z.samples * z.wide), BF16),
                pltpu.VMEM((height, z.samples * z.wide), BF16),
            ],
        ),
        out_shape=[
            pltpu.HBM((z.samples, z.rows * z.columns, z.depth), F32),
            pltpu.HBM((z.samples, z.rows * z.columns, z.half), F32),
        ],
        compiler_params=params(34),
        cost_estimate=cost(z.pixels * z.basis * z.taps * z.joined, 8 * z.pixels * z.depth),
    )(info, bands, *arrays)
    return mixed.reshape(z.pixels, z.depth), other.reshape(z.pixels, z.half)


def conv_body(z, mixed_ref, tail_ref, weight_ref, base_ref, bias_ref, out_ref, tail_weight):
    step = pl.program_id(0)

    @pl.when(step == 0)
    def _():
        out_ref[...] = base_ref[...] + row(bias_ref)
        tail_weight[...] = jnp.zeros_like(tail_weight)

    out_ref[...] += nt(left(mixed_ref[...]), right_t(weight_ref[0, :, : z.main]))
    last = weight_ref[0, :, z.main :]
    last = jnp.concatenate([last, jnp.zeros((last.shape[0], LANES - z.extra), F32)], axis=1)
    tail_weight[...] += pltpu.roll(last, z.extra * step, 1)

    @pl.when(step == z.basis - 1)
    def _():
        out_ref[...] += nt(left(tail_ref[...]), right_t(tail_weight[...]))


def conv(z, mixed, weight, base, bias):
    return pl.pallas_call(
        partial(conv_body, z),
        name="conv",
        grid=(z.basis,),
        in_specs=[
            pl.BlockSpec((z.pixels, z.main), lambda k: (0, k)),
            pl.BlockSpec((z.pixels, LANES), lambda k: (0, z.basis * z.tiles)),
            pl.BlockSpec((1, z.width, z.joined), lambda k: (k, 0, 0)),
            full((z.pixels, z.width)),
            full(bias.shape),
        ],
        out_specs=result((z.pixels, z.width)),
        out_shape=jax.ShapeDtypeStruct((z.pixels, z.width), F32),
        scratch_shapes=[pltpu.VMEM((z.width, LANES), F32)],
        compiler_params=params(44),
        cost_estimate=cost(z.pixels * z.depth * z.width, 4 * z.depth * (z.width + z.pixels)),
    )(mixed, mixed, weight, base, bias)


def mlp_body(
    z,
    info_ref,
    middle_ref,
    cot_ref,
    d_active_ref,
    weight_ref,
    bias_ref,
    gain_ref,
    shift_ref,
    kept_ref,
    sent_ref,
    active_high_ref,
    active_low_ref,
    d_pre_high_ref,
    d_pre_low_ref,
    d_bias_ref,
    second_ref,
    second_lhs,
    second_t,
    cot_t,
    tail,
):
    step = pl.program_id(0)
    main = z.main

    @pl.when(step == 0)
    def _():
        norm, _ = normalize(middle_ref[...])
        second = norm * row(gain_ref) + row(shift_ref)
        second_ref[...] = second
        second_lhs[...] = left(second[:, :main])
        second_t[...] = left(padded_t(second, z.wide)[: z.high])
        cot_t[...] = left(padded_t(cot_ref[...], z.wide)[: z.high])

    def store(out_ref, which, value, last):
        if not last:
            for i in range(z.tiles):
                out_ref[0, i * z.high : (i + 1) * z.high, :] = value[:, i * LANES : (i + 1) * LANES]
            out_ref[0, z.tiles * z.high :, :] = tail[which, step - 1]
            return
        fill = jnp.zeros((z.wide - z.high, LANES), F32)
        value = jnp.transpose(jnp.concatenate([value, fill], axis=0))[:8]
        for i in range(z.parts):
            half, place = i // (z.parts // 2), i % (z.parts // 2)
            tail[which, half, 8 * place : 8 * place + 8, :] = value[:, i * LANES : (i + 1) * LANES]

    def body(width, last):
        weight = only(z, weight_ref[:, :width], last)
        start = z.steps * main if last else pl.multiple_of((step - 1) * main, LANES)
        bias = bias_ref[pl.ds(start, z.rest if last else width)]
        bias = bias.reshape(1, bias.shape[0])
        if last:
            bias = jnp.concatenate([bias, jnp.zeros((1, width - z.rest), F32)], axis=1)
        d_active = only(z, d_active_ref[:, :width], last)
        pre = nn(second_lhs[...], right(weight[:main]))
        pre = pre + second_ref[:, main : main + 1] * weight[main : main + 1] + bias
        cdf = 0.5 * (1.0 + lax.erf(pre * np.float32(0.5**0.5)))
        pdf = jnp.exp(pre * pre * -0.5) * np.float32(1.0 / np.sqrt(2.0 * np.pi))
        active = only(z, pre * cdf, last)
        d_pre = d_active * (cdf + pre * pdf)
        high, low = split(active)
        active_high_ref[:, :width] = high
        active_low_ref[:, :width] = low
        output_grad = nn(cot_t[...], jnp.concatenate([high, low, high], axis=0))
        high, low = split(d_pre)
        d_pre_high_ref[:, :width] = high
        d_pre_low_ref[:, :width] = low
        d_bias_ref[:, :width] = jnp.sum(d_pre, axis=0, keepdims=True)
        hidden_grad = nn(second_t[...], jnp.concatenate([high, low, high], axis=0))

        @pl.when(info_ref[0] == 0)
        def _():
            store(kept_ref, 0, output_grad, last)
            store(sent_ref, 1, hidden_grad, last)

        @pl.when(info_ref[0] != 0)
        def _():
            store(sent_ref, 0, output_grad, last)
            store(kept_ref, 1, hidden_grad, last)

    pl.when(step == 0)(lambda: body(LANES, True))
    pl.when(step > 0)(lambda: body(z.main, False))


def mlp(z, info, middle, cot, d_active, weight, bias, gain, shift):
    flat = (2, z.mlp_half, LANES)
    at = lambda i: jnp.where(i == 0, z.steps, i - 1)
    hidden = pl.BlockSpec((z.pixels, z.main), lambda i, *_: (0, at(i)))
    half = pl.BlockSpec((1, z.mlp_half, LANES), lambda i, *_: (jnp.maximum(i - 1, 0), 0, 0))
    wide = pltpu.HBM((z.pixels, z.hidden), BF16)
    return pl.pallas_call(
        partial(mlp_body, z),
        name="mlp",
        grid_spec=pltpu.PrefetchScalarGridSpec(
            num_scalar_prefetch=1,
            grid=(z.steps + 1,),
            in_specs=[
                full((z.pixels, z.width)),
                full((z.pixels, z.width)),
                hidden,
                pl.BlockSpec((z.width, z.main), lambda i, *_: (0, at(i))),
                full(bias.shape),
                full(gain.shape),
                full(shift.shape),
            ],
            out_specs=[
                half,
                half,
                hidden,
                hidden,
                hidden,
                hidden,
                pl.BlockSpec((1, z.main), lambda i, *_: (0, at(i))),
            ],
            scratch_shapes=[
                pltpu.VMEM((z.pixels, z.width), F32),
                pltpu.VMEM((z.pixels, 3 * z.main), BF16),
                pltpu.VMEM((z.high, 3 * z.pixels), BF16),
                pltpu.VMEM((z.high, 3 * z.pixels), BF16),
                pltpu.VMEM((2, z.steps, 8 * z.parts // 2, LANES), F32),
            ],
        ),
        out_shape=[
            pltpu.HBM(flat, F32),
            pltpu.HBM(flat, F32),
            wide,
            wide,
            wide,
            wide,
            jax.ShapeDtypeStruct((1, z.hidden), F32),
        ],
        compiler_params=params(44),
        cost_estimate=cost(3 * z.pixels * z.width * z.hidden, 12 * z.width * z.hidden),
    )(info, middle, cot, d_active, weight, bias, gain, shift)


def middle_back_body(z, high_ref, low_ref, weight_ref, middle_ref, cot_ref, gain_ref, out_ref, out_t_ref, sums_ref, d_second):
    step = pl.program_id(0)

    @pl.when(step == 0)
    def _():
        d_second[...] = jnp.zeros_like(d_second)

    def body(width, last):
        high = only(z, high_ref[:, :width], last)
        low = only(z, low_ref[:, :width], last)
        weight = right_t(only(z, weight_ref[:, :width], last))
        d_second[...] += nt(jnp.concatenate([high, high, low], axis=1), weight)

    hidden_steps(z, body)

    @pl.when(step == z.steps)
    def _():
        norm, inverse = normalize(middle_ref[...])
        grad = d_second[...]
        sums_ref[0:1, :] = jnp.sum(grad * norm, axis=0, keepdims=True)
        sums_ref[1:2, :] = jnp.sum(grad, axis=0, keepdims=True)
        cot = cot_ref[...]
        sums_ref[3:4, :] = jnp.sum(cot, axis=0, keepdims=True)
        d_middle = cot + norm_back(grad * row(gain_ref), norm, inverse)
        sums_ref[2:3, :] = jnp.sum(d_middle, axis=0, keepdims=True)
        out_ref[...] = d_middle
        out_t_ref[...] = padded_t(d_middle, z.wide)[: z.high]


def middle_back(z, high, low, weight, middle, cot, gain):
    hidden = pl.BlockSpec((z.pixels, z.main), lambda i: (0, i))
    return pl.pallas_call(
        partial(middle_back_body, z),
        name="middle_back",
        grid=(z.steps + 1,),
        in_specs=[
            hidden,
            hidden,
            pl.BlockSpec((z.width, z.main), lambda i: (0, i)),
            full((z.pixels, z.width)),
            full((z.pixels, z.width)),
            full(gain.shape),
        ],
        out_specs=[
            full((z.pixels, z.width)),
            full((z.high, z.pixels)),
            full((4, z.width)),
        ],
        out_shape=[
            jax.ShapeDtypeStruct((z.pixels, z.width), F32),
            jax.ShapeDtypeStruct((z.high, z.pixels), F32),
            jax.ShapeDtypeStruct((4, z.width), F32),
        ],
        scratch_shapes=[pltpu.VMEM((z.pixels, z.width), F32)],
        compiler_params=params(58),
        cost_estimate=cost(z.pixels * z.width * z.hidden, 8 * z.width * z.hidden),
    )(high, low, weight, middle, cot, gain)


def output_body(z, high_ref, low_ref, weight_ref, middle_ref, bias_ref, out_ref):
    @pl.when(pl.program_id(0) == 0)
    def _():
        out_ref[...] = middle_ref[...] + row(bias_ref)

    def body(width, last):
        high = only(z, high_ref[:, :width], last)
        low = only(z, low_ref[:, :width], last)
        weight = right_t(only(z, weight_ref[:, :width], last))
        out_ref[...] += nt(jnp.concatenate([high, high, low], axis=1), weight)

    hidden_steps(z, body)


def output(z, high, low, weight, middle, bias):
    hidden = pl.BlockSpec((z.pixels, z.main), lambda i: (0, i))
    return pl.pallas_call(
        partial(output_body, z),
        name="output",
        grid=(z.steps + 1,),
        in_specs=[
            hidden,
            hidden,
            pl.BlockSpec((z.width, z.main), lambda i: (0, i)),
            full((z.pixels, z.width)),
            full(bias.shape),
        ],
        out_specs=full((z.pixels, z.width)),
        out_shape=jax.ShapeDtypeStruct((z.pixels, z.width), F32),
        compiler_params=params(58),
        cost_estimate=cost(z.pixels * z.width * z.hidden, 8 * z.width * z.hidden),
    )(high, low, weight, middle, bias)


def conv_grad_body(z, info_ref, own_ref, far_ref, own_t_ref, far_t_ref, out_ref, lhs):
    step = pl.program_id(0)
    tiles = own_ref.shape[1] // LANES

    @pl.when(step == 0)
    def _():
        lhs[...] = left(jnp.concatenate([own_t_ref[...], far_t_ref[...]], axis=1))
        used = pl.num_programs(0) * tiles * z.high
        out_ref[used:, :] = jnp.zeros((out_ref.shape[0] - used, LANES), F32)

    value = nn(lhs[...], right(jnp.concatenate([own_ref[...], far_ref[...]], axis=0)))
    for i in range(tiles):
        rows = pl.ds(pl.multiple_of((step * tiles + i) * z.high, 8), z.high)
        out_ref[rows, :] = value[:, i * LANES : (i + 1) * LANES]


def conv_grad(z, info, mixed, far_mixed, own_t, far_t):
    count = z.half // LANES // 2
    tiles = 3
    steps = count // tiles
    flat = round_up(count * z.high, 32)
    return pl.pallas_call(
        partial(conv_grad_body, z),
        name="conv_grad",
        grid_spec=pltpu.PrefetchScalarGridSpec(
            num_scalar_prefetch=1,
            grid=(steps,),
            in_specs=[
                pl.BlockSpec((z.pixels, tiles * LANES), lambda i, c: (0, (2 * c[0] + c[1]) * steps + i)),
                pl.BlockSpec((z.pixels, tiles * LANES), lambda i, c: (0, c[1] * steps + i)),
                full((z.high, z.pixels)),
                full((z.high, z.pixels)),
            ],
            out_specs=full((flat, LANES)),
            scratch_shapes=[pltpu.VMEM((z.high, 6 * z.pixels), BF16)],
        ),
        out_shape=jax.ShapeDtypeStruct((flat, LANES), F32),
        compiler_params=params(50),
        cost_estimate=cost(2 * z.pixels * z.width * count * LANES, 12 * z.pixels * count * LANES),
    )(info, mixed, far_mixed, own_t, far_t)


def mixed_back_body(z, weight_ref, dm_ref, high_ref, low_ref, lhs):
    columns, main = z.columns, z.main

    @pl.when(pl.program_id(0) == 0)
    def _():
        lhs[...] = left(dm_ref[:, :main])

    value = nn(lhs[...], right(weight_ref[0, :main, :]))
    value = value + dm_ref[:, main : main + 1] * weight_ref[0, main : main + 1, :]
    value_high, value_low = split(value)
    for b in range(z.samples):
        for r in range(z.rows):
            i = (b * z.rows + r) * columns
            lane = b * z.wide
            high_ref[r, :, lane : lane + z.joined] = value_high[i : i + columns]
            low_ref[r, :, lane : lane + z.joined] = value_low[i : i + columns]


def mixed_back(z, weight, d_middle):
    out = pl.BlockSpec((z.rows, z.columns, z.samples * z.wide), lambda i: (0, i, 0))
    shape = pltpu.HBM((z.rows, z.basis * z.columns, z.samples * z.wide), BF16)
    return pl.pallas_call(
        partial(mixed_back_body, z),
        name="mixed_back",
        grid=(z.basis,),
        in_specs=[
            pl.BlockSpec((1, z.width, z.joined), lambda i: (i, 0, 0)),
            full((z.pixels, z.width)),
        ],
        out_specs=[out, out],
        out_shape=[shape, shape],
        scratch_shapes=[pltpu.VMEM((z.pixels, 3 * z.main), BF16)],
        compiler_params=params(56),
        cost_estimate=cost(z.pixels * z.depth * z.width, 4 * z.depth * z.width),
    )(weight, d_middle)


def outer_columns(z, value):
    return jnp.concatenate([value[z.columns + LON_HALO : z.columns + 2 * LON_HALO], value[:LON_HALO]], axis=0)


def band_back_body(z, high_ref, low_ref, band_ref, out_ref, top_ref, bottom_ref, sides_ref):
    row_at = pl.program_id(0)
    columns = z.columns

    @pl.when(row_at == 0)
    def _():
        out_ref[...] = jnp.zeros_like(out_ref)

    spread = [band(band_ref[0, k : k + 1, :], columns) for k in range(z.basis)]
    spread = jnp.transpose(jnp.concatenate(spread, axis=0))[: z.taps]
    high, low = split(spread)
    top, rest = high_ref[0], low_ref[0]
    value = nn(high, top) + nn(high, rest) + nn(low, top)
    place = pl.ds(pl.multiple_of(row_at * z.span, 8), z.taps)
    for b in range(z.samples):
        out_ref[b, place, :] += value[:, b * z.wide : b * z.wide + z.joined]

    @pl.when(row_at == z.rows - 1)
    def _():
        for b in range(z.samples):
            for r in range(z.rows + 2 * LAT_HALO):
                value = out_ref[b, r * z.span : r * z.span + columns + 2 * LON_HALO, :]
                if r < LAT_HALO:
                    top_ref[b, r] = value
                elif r < z.rows + LAT_HALO:
                    sides_ref[b, r - LAT_HALO] = outer_columns(z, value)
                else:
                    bottom_ref[b, r - z.rows - LAT_HALO] = value


def band_back(z, high, low, bands):
    lanes = bands.shape[2]
    height = (z.rows + 2 * LAT_HALO) * z.span
    rim = (z.samples, LAT_HALO, z.columns + 2 * LON_HALO, z.joined)
    shapes = [(z.samples, height, z.joined), rim, rim, (z.samples, z.rows, 2 * LON_HALO, z.joined)]
    part = pl.BlockSpec((1,) + high.shape[1:], lambda i: (i, 0, 0))
    return pl.pallas_call(
        partial(band_back_body, z),
        name="band_back",
        grid=(z.rows,),
        in_specs=[part, part, pl.BlockSpec((1, z.basis, lanes), lambda i: (i, 0, 0))],
        out_specs=[full(shape) for shape in shapes],
        out_shape=[jax.ShapeDtypeStruct(shape, F32) for shape in shapes],
        compiler_params=params(56),
        cost_estimate=cost(z.pixels * z.basis * z.taps * z.joined, 8 * z.pixels * z.depth),
    )(high, low, bands)


def edge_body(z, sides_ref, above_ref, below_ref, out_ref):
    for b in range(z.samples):
        for r in range(z.rows):
            value = sides_ref[b, r]
            if r < LAT_HALO:
                value = value + outer_columns(z, above_ref[b, r])
            if r >= z.rows - LAT_HALO:
                value = value + outer_columns(z, below_ref[b, r - z.rows + LAT_HALO])
            out_ref[b, r] = value


def edge(z, sides, above, below):
    return pl.pallas_call(
        partial(edge_body, z),
        name="edge",
        out_shape=jax.ShapeDtypeStruct(sides.shape, F32),
        compiler_params=params(16),
        cost_estimate=cost(2**30, 2**24),
    )(sides, above, below)


def finish_body(
    z, padded_ref, above_ref, below_ref, sides_ref, inputs_ref, d_middle_ref, gain_ref, sums_ref, d_bias_ref, out_ref, vectors_ref, own
):
    sample = pl.program_id(0)

    @pl.when(sample == 0)
    def _():
        own[...] = jnp.zeros_like(own)

    for r in range(z.rows):
        start = (r + LAT_HALO) * z.span
        value = padded_ref[0, start : start + z.columns + 2 * LON_HALO, :]
        if r < LAT_HALO:
            value = value + above_ref[0, r]
        if r >= z.rows - LAT_HALO:
            value = value + below_ref[0, r - z.rows + LAT_HALO]
        middle = value[2 * LON_HALO : z.columns]
        low = value[LON_HALO : 2 * LON_HALO] + sides_ref[0, r, :LON_HALO]
        high = value[z.columns : z.columns + LON_HALO] + sides_ref[0, r, LON_HALO:]
        grad = jnp.concatenate([low, middle, high], axis=0)[:, : z.width]
        norm, inverse = normalize(inputs_ref[0, r])
        own[0:1, :] += jnp.sum(grad * norm, axis=0, keepdims=True)
        own[1:2, :] += jnp.sum(grad, axis=0, keepdims=True)
        grad = norm_back(grad * row(gain_ref), norm, inverse)
        out_ref[0, r] = d_middle_ref[0, r] + grad

    @pl.when(sample == pl.num_programs(0) - 1)
    def _():
        vectors_ref[...] = jnp.zeros_like(vectors_ref)
        row = 0
        rows = [(sums_ref, 2), (own, 0), (own, 1), (sums_ref, 0), (sums_ref, 1), (d_bias_ref, 0), (sums_ref, 3)]
        for ref, at in rows:
            size = ref.shape[1]
            for i in range(0, size, LANES):
                end = min(i + LANES, size)
                vectors_ref[row : row + 1, : end - i] = ref[at : at + 1, i:end]
                row += 1


def finish(z, padded, above, below, sides, inputs, d_middle, gain, sums, d_bias):
    shape = (z.samples, z.rows, z.columns, z.width)
    count = round_up(6 * pl.cdiv(z.width, LANES) + pl.cdiv(z.hidden, LANES), 16)

    def part(array):
        size = array.shape[1:]
        return pl.BlockSpec((1,) + size, lambda b: (b,) + (0,) * len(size))

    d_middle = d_middle.reshape(shape)
    arrays = [padded, above, below, sides, inputs, d_middle]
    return pl.pallas_call(
        partial(finish_body, z),
        name="finish",
        grid=(z.samples,),
        in_specs=[part(a) for a in arrays] + [full(gain.shape), full(sums.shape), full(d_bias.shape)],
        out_specs=[part(inputs), full((count, LANES))],
        out_shape=[jax.ShapeDtypeStruct(shape, F32), jax.ShapeDtypeStruct((count, LANES), F32)],
        scratch_shapes=[pltpu.VMEM((8, z.width), F32)],
        compiler_params=params(60),
        cost_estimate=cost(2**30, 2**24),
    )(*arrays, gain, sums, d_bias)


def conv_place_body(z, which, first, count, info_ref, *refs):
    number = len(which)
    pieces, (out_ref, held, narrow, sems) = refs[:number], refs[-4:]
    main_tiles = z.basis * z.tiles
    with_extra = first + 2 * count == z.half // LANES
    used = count * z.high

    def get(i):
        return pltpu.make_async_copy(pieces[i].at[pl.ds(0, used), :], held.at[i], sems.at[i])

    def tile(i, t):
        return (info_ref[which[i]] // 2) * (z.half // LANES) + first + (info_ref[which[i]] % 2) * count + t

    def put(i, t):
        at = tile(i, t)
        lanes = pl.ds(pl.multiple_of(at % z.tiles * LANES, LANES), LANES)
        return pltpu.make_async_copy(
            held.at[i, pl.ds(t * z.high, z.width), :],
            out_ref.at[at // z.tiles, :, lanes],
            sems.at[number + i * count + t],
        )

    def put_extra(k):
        return pltpu.make_async_copy(
            narrow.at[k], out_ref.at[k, :, pl.ds(z.main, z.extra)], sems.at[number * (1 + count) + k]
        )

    for i in range(number):
        get(i).start()
    for i in range(number):
        get(i).wait()
        for t in range(count):
            is_main = tile(i, t) < main_tiles

            @pl.when(is_main)
            def _():
                put(i, t).start()

            if with_extra and t == count - 1:

                @pl.when(jnp.logical_not(is_main))
                def _():
                    for k in range(z.basis):
                        value = held[i, t * z.high : (t + 1) * z.high, :]
                        value = value if k == 0 else pltpu.roll(value, LANES - z.extra * k, 1)
                        narrow[k] = value[: z.width, : z.extra]
                        put_extra(k).start()

    for i in range(number):
        if with_extra:

            @pl.when(tile(i, count - 1) >= main_tiles)
            def _():
                for k in range(z.basis):
                    put_extra(k).wait()

        for t in range(count):

            @pl.when(tile(i, t) < main_tiles)
            def _():
                put(i, t).wait()


def conv_place(z, places, which, first, count, pieces, onto):
    anywhere = pl.BlockSpec(memory_space=pl.ANY)
    operands = [places, *pieces]
    aliases = {}
    if onto is not None:
        operands.append(onto)
        aliases = {1 + len(which): 0}
    return pl.pallas_call(
        partial(conv_place_body, z, which, first, count),
        name="conv_place",
        grid_spec=pltpu.PrefetchScalarGridSpec(
            num_scalar_prefetch=1,
            grid=(),
            in_specs=[anywhere] * (len(operands) - 1),
            out_specs=anywhere,
            scratch_shapes=[
                pltpu.VMEM((len(which), count * z.high, LANES), F32),
                pltpu.VMEM((z.basis, z.width, z.extra), F32),
                pltpu.SemaphoreType.DMA((len(which) * (1 + count) + z.basis,)),
            ],
        ),
        out_shape=jax.ShapeDtypeStruct((z.basis, z.width, z.joined), F32),
        input_output_aliases=aliases,
        compiler_params=params(16),
        cost_estimate=cost(2**30, 2**24),
    )(*operands)


def mlp_place_body(z, info_ref, own_ref, far_ref, output_ref, hidden_ref, held, narrow, sems):
    main_tiles = 2 * z.tiles

    def place(refs):
        gets = []
        for i, ref in enumerate(refs):
            for half in range(2):
                rows = pl.ds(half * z.mlp_half, z.mlp_half)
                gets.append(pltpu.make_async_copy(ref.at[rows, :], held.at[i, half], sems.at[2 * i + half]))
                gets[-1].start()
        puts = []
        for i, out_ref in enumerate((output_ref, hidden_ref)):
            for t in range(main_tiles):
                half = t // z.tiles
                if t % z.tiles == 0:
                    gets[2 * i + half].wait()
                puts.append(
                    pltpu.make_async_copy(
                        held.at[i, half, pl.ds(t % z.tiles * z.high, z.width), :],
                        out_ref.at[:, pl.ds(t * LANES, LANES)],
                        sems.at[8 + i * main_tiles + t],
                    )
                )
                puts[-1].start()
            start = z.tiles * z.high
            parts = [
                held[i, half, start + 8 * j : start + 8 * j + 8, :] for half in range(2) for j in range(z.parts // 2)
            ]
            value = jnp.concatenate([jnp.concatenate(parts, axis=1)] * (LANES // 8), axis=0)
            narrow[i] = jnp.transpose(value)[: z.width, : z.rest]
            puts.append(
                pltpu.make_async_copy(
                    narrow.at[i],
                    out_ref.at[:, pl.ds(main_tiles * LANES, z.rest)],
                    sems.at[8 + 2 * main_tiles + i],
                )
            )
            puts[-1].start()
        for c in puts:
            c.wait()

    pl.when(info_ref[0] == 0)(lambda: place((own_ref, far_ref)))
    pl.when(info_ref[0] != 0)(lambda: place((far_ref, own_ref)))


def mlp_place(z, info, own, far):
    shape = jax.ShapeDtypeStruct((z.width, z.hidden), F32)
    anywhere = pl.BlockSpec(memory_space=pl.ANY)
    return pl.pallas_call(
        partial(mlp_place_body, z),
        name="mlp_place",
        grid_spec=pltpu.PrefetchScalarGridSpec(
            num_scalar_prefetch=1,
            grid=(),
            in_specs=[anywhere, anywhere],
            out_specs=[anywhere, anywhere],
            scratch_shapes=[
                pltpu.VMEM((2, 2, z.mlp_half, LANES), F32),
                pltpu.VMEM((2, z.width, z.rest), F32),
                pltpu.SemaphoreType.DMA((4 * z.tiles + 10,)),
            ],
        ),
        out_shape=[shape, shape],
        compiler_params=params(16),
        cost_estimate=cost(2**30, 2**22),
    )(info, own, far)


def axis_size(axes):
    size = 1
    for axis in axes:
        size *= lax.axis_size(axis)
    return size


def pairs(lats, lons, target):
    found = []
    for lat in range(lats):
        for lon in range(lons):
            to_lat, to_lon = target(lat, lon)
            found.append((lat * lons + lon, to_lat * lons + to_lon))
    return found


class GridSum:
    def __init__(self):
        lats, lons = axis_size(LAT), axis_size(LON)
        lat, lon = lax.axis_index(LAT), lax.axis_index(LON)
        over = partial(pairs, lats, lons)
        self.core = lat % 2
        self.cores = over(lambda a, o: (a ^ 1, o))
        self.first = over(lambda a, o: (a ^ 2, o) if a % 2 else (a, o ^ 1))
        self.second = over(lambda a, o: (a, o ^ 1) if a % 2 else (a ^ 2, o))
        self.third = over(lambda a, o: (a ^ 4, o))
        lon_bit, lat_bit = lon % 2, lat // 2 % 2
        self.first_bit = jnp.where(self.core == 0, lon_bit, lat_bit)
        self.second_bit = jnp.where(self.core == 0, lat_bit, lon_bit)
        self.third_bit = lat // 4 % 2
        far_bit = jnp.where(self.core == 0, lat_bit, lon_bit)
        mine, other = 2 * self.core, 2 * (1 - self.core)
        self.places = jnp.stack(
            [mine + self.first_bit, mine + 1 - self.first_bit, other + far_bit, other + 1 - far_bit]
        ).astype(jnp.int32)
        self.others = []
        bit = 8
        while bit < lats:
            self.others.append(over(lambda a, o, bit=bit: (a ^ bit, o)))
            bit *= 2
        bit = 2
        while bit < lons:
            self.others.append(over(lambda a, o, bit=bit: (a, o ^ bit)))
            bit *= 2

    def swap(self, value, where):
        return lax.ppermute(value, AXES, where)

    def all(self, value, where):
        return value + self.swap(value, where)


class Order:
    def __init__(self):
        self.last = ()
        self.held = True

    def use(self, value):
        if not self.held:
            return value
        value, self.last = lax.optimization_barrier((value, self.last))
        return value

    def mark(self, value):
        if self.held:
            self.last = (value,)
        return value

    def wait(self, value):
        return self.mark(self.use(value))

    def run(self, function, *values):
        return self.mark(function(*self.use(values)))


def sum_rows(size, index, arrays, vectors):
    count = 0 if vectors is None else vectors.shape[0]

    def body(index_ref, *refs):
        out_ref = refs[-1]
        total = refs[0][...]
        for ref in refs[1 : len(arrays)]:
            total = total + ref[...]
        out_ref[:size, :] = total
        if vectors is not None:
            out_ref[size:, :] = refs[len(arrays)][...]

    more = [] if vectors is None else [vectors]
    blocks = [pl.BlockSpec((size, LANES), lambda g, p, i=i: (p[i], 0)) for i in range(len(arrays))]
    return pl.pallas_call(
        body,
        name="sum_rows",
        grid_spec=pltpu.PrefetchScalarGridSpec(
            num_scalar_prefetch=1,
            grid=(1,),
            in_specs=blocks + [full(v.shape) for v in more],
            out_specs=full((size + count, LANES)),
        ),
        out_shape=jax.ShapeDtypeStruct((size + count, LANES), F32),
        compiler_params=params(16),
        cost_estimate=cost(2**30, 2**24),
    )(index, *arrays, *more)


def join_rows(size, bit, value, far):
    rows = value.shape[0] + size

    def body(bit_ref, value_ref, far_ref, out_ref):
        at = bit_ref[0]
        out_ref[pl.ds(pl.multiple_of(at * size, 8), size), :] = value_ref[:size, :]
        out_ref[pl.ds(pl.multiple_of((1 - at) * size, 8), size), :] = far_ref[:size, :]
        if rows > 2 * size:
            out_ref[2 * size :, :] = value_ref[size:, :] + far_ref[size:, :]

    return pl.pallas_call(
        body,
        name="join_rows",
        grid_spec=pltpu.PrefetchScalarGridSpec(
            num_scalar_prefetch=1,
            grid=(1,),
            in_specs=[full(value.shape), full(far.shape)],
            out_specs=full((rows, LANES)),
        ),
        out_shape=jax.ShapeDtypeStruct((rows, LANES), F32),
        compiler_params=params(16),
        cost_estimate=cost(2**30, 2**24),
    )(bit.reshape(1).astype(jnp.int32), value, far)


def add_rows(value, far, start=0):
    def body(value_ref, far_ref, out_ref):
        out_ref[...] = value_ref[...] + far_ref[start:, :]

    return pl.pallas_call(
        body,
        name="add_rows",
        out_shape=jax.ShapeDtypeStruct(value.shape, F32),
        compiler_params=params(16),
        cost_estimate=cost(2**30, 2**24),
    )(value, far)


def sum_tails(start, arrays):
    rows = arrays[0].shape[0] - start
    blocks = start % rows == 0

    def body(*refs):
        total = 0.0
        for ref in refs[:-1]:
            total = total + (ref[...] if blocks else ref[start:, :])
        refs[-1][...] = total

    spec = pl.BlockSpec((rows, LANES), lambda i: (start // rows, 0)) if blocks else full(arrays[0].shape)
    return pl.pallas_call(
        body,
        name="sum_tails",
        grid=(1,),
        in_specs=[spec] * len(arrays),
        out_specs=full((rows, LANES)),
        out_shape=jax.ShapeDtypeStruct((rows, LANES), F32),
        compiler_params=params(24),
        cost_estimate=cost(2**30, 2**22),
    )(*arrays)


class Chunk:
    def __init__(self, total, order, name, sent, kept):
        self.total, self.order, self.name = total, order, name
        self.terms, self.size = [(kept, 0)], sent.shape[0]
        self.vectors = None
        self.send("scatter_first", order.wait(sent), total.first)

    def send(self, step, value, where):
        with jax.named_scope(f"{self.name}_{step}"):
            self.value, self.far = value, self.total.swap(value, where)

    def take(self, index):
        arrays = [value for value, _ in self.terms]
        at = jnp.stack([jnp.asarray(index(at), jnp.int32) for _, at in self.terms])
        return self.order.run(partial(sum_rows, self.size), at, arrays, None)

    def halve(self, step, where, bit):
        self.terms.append((self.far, 0))
        self.size //= 2
        sent = self.take(lambda at: 2 * at + 1 - bit)
        self.terms = [(value, 2 * at + bit) for value, at in self.terms]
        self.send(step, sent, where)

    def join(self, bit):
        self.value = self.order.run(partial(join_rows, self.size), bit, self.value, self.far)
        self.size *= 2

    def scatter_second(self):
        self.halve("scatter_second", self.total.second, self.total.second_bit)

    def across_first(self):
        self.halve("across_first", self.total.third, self.total.third_bit)

    def across_second(self):
        self.terms.append((self.far, 0))
        self.value = self.take(lambda at: at)
        for where in self.total.others[:-1]:
            self.send("across", self.value, where)
            self.value = self.order.run(add_rows, self.value, self.far)
        self.send("across_second", self.value, self.total.others[-1])

    def across_third(self):
        both = [self.value, self.far]
        value = self.order.run(partial(sum_rows, self.size), jnp.zeros((2,), jnp.int32), both, self.vectors)
        self.send("across_third", value, self.total.third)

    def gather_second(self):
        self.join(self.total.third_bit)
        self.send("gather_second", self.value, self.total.second)

    def gather_first(self):
        self.join(self.total.second_bit)
        self.send("gather_first", self.value, self.total.first)
        with jax.named_scope(f"{self.name}_near_core"):
            self.near = self.total.swap(self.value, self.total.cores)

    def gather_whole(self):
        self.join(self.total.first_bit)
        with jax.named_scope(f"{self.name}_near_core"):
            self.near = self.total.swap(self.value, self.total.cores)

    def gather_core(self):
        self.far = self.order.wait(self.far)
        with jax.named_scope(f"{self.name}_gather_core"):
            self.last = self.total.swap(self.far, self.total.cores)

    def pieces(self):
        return self.value, self.far, self.near, self.last


def after(value, *others):
    return lax.optimization_barrier((value, others))[0]


def rows_of(vector):
    size = round_up(vector.shape[0], LANES)
    return jnp.pad(vector, (0, size - vector.shape[0])).reshape(-1, LANES)


def moved(value, axis, steps, cycle):
    count = axis_size(axis)
    if cycle:
        where = [(i, (i + steps) % count) for i in range(count)]
    else:
        where = [(i, i + steps) for i in range(max(0, -steps), min(count, count - steps))]
    return lax.ppermute(value, axis, where)


def edges(sides, down):
    lats, lons = axis_size(LAT), axis_size(LON)

    def shifted(value, steps):
        where = [
            (lat * lons + lon, (lat + down) * lons + (lon + steps) % lons)
            for lat in range(max(0, -down), min(lats, lats - down))
            for lon in range(lons)
        ]
        return lax.ppermute(value, AXES, where)

    if lons == 2:
        return shifted(sides, 1)
    return jnp.concatenate([shifted(sides[:, :, :LON_HALO], 1), shifted(sides[:, :, LON_HALO:], -1)], axis=2)


def local(
    inputs,
    noise_field,
    basis_values,
    row_reach,
    conv_weight,
    conv_bias,
    first_gain,
    first_shift,
    second_gain,
    second_shift,
    hidden_weight,
    hidden_bias,
    output_weight,
    output_bias,
    cotangent,
):
    z = Sizes(inputs, noise_field, conv_weight, hidden_weight)
    total = GridSum()
    lat, lats = lax.axis_index(LAT), axis_size(LAT)
    info = jnp.stack([total.core, (lat > 0).astype(jnp.int32), (lat < lats - 1).astype(jnp.int32)])
    rows, columns, width = z.rows, z.columns, z.width
    flat = (z.pixels, width)
    cot = cotangent.reshape(flat)
    conv_weight = jnp.transpose(conv_weight, (0, 2, 1))
    output_weight = jnp.transpose(output_weight)

    noise = jnp.transpose(noise_field, (0, 1, 3, 2))
    top, bottom, top_sides, bottom_sides, sides = cut(z, inputs, noise)
    below, above = moved(top, LAT, -1, False), moved(bottom, LAT, 1, False)
    sides = [edges(bottom_sides, 1), edges(top_sides, -1), edges(sides, 0)]
    d_active = active_back(z, cot, output_weight)
    bands, plain_bands = band_rows(z, basis_values, row_reach)
    above, below, sides = after((above, below, sides), d_active)
    mixed, other = mix(z, info, bands, inputs, noise, above, below, sides, first_gain, first_shift)
    far_mixed = total.swap(other, total.cores)
    middle = conv(z, mixed, conv_weight, inputs.reshape(flat), conv_bias)
    kept, sent, active_high, active_low, d_pre_high, d_pre_low, d_hidden_bias = mlp(
        z, info, middle, cot, d_active, hidden_weight, hidden_bias, second_gain, second_shift
    )
    order = Order()
    arrived = total.swap(sent, total.cores)

    d_middle, d_middle_t, sums = order.run(
        partial(middle_back, z), d_pre_high, d_pre_low, hidden_weight, middle, cot, second_gain
    )
    far_t = total.swap(d_middle_t, total.cores)

    bit = total.first_bit
    kept, arrived = kept.reshape(-1, LANES), arrived.reshape(-1, LANES)
    add_half = lambda k, r, w: sum_rows(z.mlp_half, jnp.stack([w, w]).astype(jnp.int32), [k, r], None)
    m = Chunk(total, order, "m", order.run(add_half, kept, arrived, 1 - bit), None)
    m.terms = [(kept, bit), (arrived, bit)]
    half = lambda which: order.run(
        lambda *v: conv_grad(z, jnp.stack([total.core, which]), *v), mixed, far_mixed, d_middle_t, far_t
    )
    c = Chunk(total, order, "c", half(1 - bit), None)
    c.terms = [(half(bit), 0)]
    m.scatter_second()
    d_mixed = order.run(partial(mixed_back, z), conv_weight, d_middle)
    m.across_first()
    c.scatter_second()
    m.across_second()
    d_padded, top, bottom, sides = order.run(partial(band_back, z), *d_mixed, plain_bands)
    c.across_first()
    m.across_third()
    top, bottom = order.wait((top, bottom))
    from_below = moved(top, LAT, -1, False)
    from_above = moved(bottom, LAT, 1, False)
    block_output = order.run(
        partial(output, z), active_high, active_low, output_weight, middle, output_bias
    )
    m.gather_second()
    c.across_second()
    outer = order.run(partial(edge, z), sides, from_above, from_below)
    from_sides = edges(outer, 0)
    input_grad, vectors = order.run(
        partial(finish, z), d_padded, from_above, from_below, from_sides, inputs, d_middle, first_gain, sums, d_hidden_bias
    )

    c.vectors = vectors
    c.across_third()
    m.gather_first()
    c.gather_second()
    m.gather_whole()
    output_weight_grad, hidden_weight_grad = order.run(lambda *v: mlp_place(z, info, *v), m.value, m.near)
    c.gather_first()
    place = partial(conv_place, z, total.places)
    count = z.half // LANES // 2
    conv_weight_grad = order.run(lambda *v: place((0, 2), 0, count, v, None), c.value, c.near)
    c.gather_core()
    place_far = lambda *v: place((1,), 0, count, v[:1], v[1])
    place_last = lambda *v: place((3,), 0, count, v[:1], v[1])
    conv_weight_grad = order.run(place_far, c.far, conv_weight_grad)
    vectors = order.run(lambda *v: sum_tails(c.size, v), *c.pieces())
    far_vectors = total.swap(vectors, total.others[0])
    conv_weight_grad = order.run(place_last, c.last, conv_weight_grad)
    vectors = order.run(add_rows, vectors, far_vectors)
    for where in total.others[1:]:
        vectors = order.run(add_rows, vectors, total.swap(vectors, where))
    found, start = [], 0
    for size in (width,) * 5 + (z.hidden, width):
        count = pl.cdiv(size, LANES)
        found.append(vectors[start : start + count].reshape(-1)[:size])
        start += count
    conv_weight_grad = jnp.transpose(conv_weight_grad, (0, 2, 1))
    output_weight_grad = jnp.transpose(output_weight_grad)
    conv_bias_grad, first_gain_grad, first_shift_grad, second_gain_grad, second_shift_grad = found[:5]
    hidden_bias_grad, output_bias_grad = found[5:]
    return (
        block_output.reshape(inputs.shape),
        input_grad,
        conv_weight_grad,
        conv_bias_grad,
        first_gain_grad,
        first_shift_grad,
        second_gain_grad,
        second_shift_grad,
        hidden_weight_grad,
        hidden_bias_grad,
        output_weight_grad,
        output_bias_grad,
    )


def solution(mesh):
    lats, lons = mesh.shape["lat"], mesh.shape["lon"]
    fine = Mesh(mesh.devices.reshape(lats // 4, 2, 2, lons // 2, 2), AXES)
    grid = P(None, LAT, LON, None)
    weights = (P(),) * 10
    in_specs = (grid, grid, P(LAT, None, None, None), P(LAT)) + weights + (grid,)
    out_specs = (grid, grid) + weights
    return jax.shard_map(local, mesh=fine, in_specs=in_specs, out_specs=out_specs, check_vma=False)
```

```python
from functools import partial

import jax
import jax.numpy as jnp
import numpy as np
from jax import lax
from jax.experimental import pallas as pl
from jax.experimental.pallas import tpu as pltpu
from jax.sharding import Mesh, PartitionSpec as P

LAT_HALO = 2
LON_HALO = 4
EPSILON = 1e-05
F32 = jnp.float32
BF16 = jnp.bfloat16
LAT = ("z", "y", "core")
LON = ("w", "x")
AXES = LAT + LON
LANES = 128
STEP = 256


def split(value):
    high = value.astype(BF16)
    return high, (value - high.astype(F32)).astype(BF16)


def left(value):
    high, low = split(value)
    return jnp.concatenate([high, high, low], axis=1)


def right(value):
    high, low = split(value)
    return jnp.concatenate([high, low, high], axis=0)


def right_t(value):
    high, low = split(value)
    return jnp.concatenate([high, low, high], axis=1)


def nn(a, b):
    return lax.dot_general(a, b, (((1,), (0,)), ((), ())), preferred_element_type=F32)


def nt(a, b):
    return lax.dot_general(a, b, (((1,), (1,)), ((), ())), preferred_element_type=F32)


def params(megabytes=30):
    return pltpu.CompilerParams(vmem_limit_bytes=megabytes * 1024 * 1024)


def cost(macs, moved):
    return pl.CostEstimate(flops=12 * macs, bytes_accessed=moved, transcendentals=0)


def full(shape):
    return pl.BlockSpec(shape, lambda *_: (0,) * len(shape), pipeline_mode=pl.Buffered(1))


def result(shape):
    return pl.BlockSpec(shape, lambda *_: (0,) * len(shape))


def row(ref):
    return ref[...].reshape(1, ref.shape[0])


def round_up(value, to):
    return -(-value // to) * to


def normalize(field):
    average = jnp.mean(field, axis=-1, keepdims=True)
    centered = field - average
    variance = jnp.mean(centered * centered, axis=-1, keepdims=True)
    inverse = lax.rsqrt(variance + EPSILON)
    return centered * inverse, inverse


def norm_back(grad_norm, normalized, inverse):
    first_term = jnp.mean(grad_norm, axis=-1, keepdims=True)
    second_term = jnp.mean(grad_norm * normalized, axis=-1, keepdims=True)
    return inverse * (grad_norm - first_term - normalized * second_term)


def padded_t(value, size):
    return jnp.transpose(
        jnp.concatenate(
            [value, jnp.zeros((value.shape[0], size - value.shape[1]), value.dtype)], axis=1
        )
    )


class Sizes:
    def __init__(self, inputs, noise_field, conv_weight, hidden_weight):
        self.samples, self.rows, self.columns, self.width = inputs.shape
        self.joined = self.width + noise_field.shape[-1]
        self.basis = conv_weight.shape[0]
        self.hidden = hidden_weight.shape[1]
        self.pixels = self.samples * self.rows * self.columns
        self.main = self.width // LANES * LANES
        self.tiles = self.main // LANES
        self.extra = self.joined - self.main
        self.span = round_up(self.columns + 2 * LON_HALO, 16)
        self.taps = (2 * LAT_HALO + 1) * self.span
        self.depth = self.basis * self.main + LANES
        self.half = self.depth // 2
        self.wide = self.main + LANES
        self.high = round_up(self.width, 8)
        self.steps = self.hidden // self.main
        self.rest = self.hidden - self.steps * self.main
        self.parts = self.wide // LANES
        self.mlp_half = self.tiles * self.high + 8 * self.parts // 2


def hidden_steps(z, body):
    step = pl.program_id(0)
    pl.when(step < z.steps)(lambda: body(z.main, False))
    pl.when(step == z.steps)(lambda: body(LANES, True))


def only(z, value, last):
    if not last:
        return value
    valid = lax.broadcasted_iota(jnp.int32, (1, LANES), 1) < z.rest
    return jnp.where(valid, value.astype(F32), 0.0).astype(value.dtype)


def active_back_body(z, cot_ref, weight_ref, out_ref, lhs):
    main = z.main

    @pl.when(pl.program_id(0) == 0)
    def _():
        lhs[...] = left(cot_ref[:, :main])

    def body(width, last):
        product = nn(lhs[...], right(weight_ref[:main, :width]))
        out_ref[:, :width] = product + cot_ref[:, main : main + 1] * weight_ref[main : main + 1, :width]

    hidden_steps(z, body)


def active_back(z, cot, weight):
    return pl.pallas_call(
        partial(active_back_body, z),
        name="active_back",
        grid=(z.steps + 1,),
        in_specs=[
            full((z.pixels, z.width)),
            pl.BlockSpec((z.width, z.main), lambda i: (0, i)),
        ],
        out_specs=pl.BlockSpec((z.pixels, z.main), lambda i: (0, i)),
        out_shape=pltpu.HBM((z.pixels, z.hidden), F32),
        scratch_shapes=[pltpu.VMEM((z.pixels, 3 * z.main), BF16)],
        compiler_params=params(60),
        cost_estimate=cost(z.pixels * z.width * z.hidden, 8 * z.width * z.hidden),
    )(cot, weight)


def band_rows_body(z, reach_ref, basis_ref, stacked_ref, plain_ref):
    width = 2 * LON_HALO + 1
    height = 2 * LAT_HALO + 1
    offset = lax.broadcasted_iota(jnp.int32, (1, height * width), 1) % width - LON_HALO
    row_at = lax.broadcasted_iota(jnp.int32, (z.rows, 1), 0)
    reach = jnp.zeros((z.rows, 1), jnp.int32)
    for r in range(z.rows):
        reach = jnp.where(row_at == r, reach_ref[r], reach)
    values = [
        jnp.where(
            jnp.abs(offset) <= reach, jnp.concatenate([basis_ref[k, a] for a in range(height)], axis=1), 0.0
        )
        for k in range(z.basis)
    ]
    values = jnp.concatenate(values, axis=0)
    source = lax.broadcasted_iota(jnp.int32, (values.shape[1], z.taps), 0)
    target = lax.broadcasted_iota(jnp.int32, (values.shape[1], z.taps), 1)
    place = source // width * z.span + source % width
    onehot = (place == target).astype(BF16)
    high = values.astype(BF16)
    rest = values - high.astype(F32)
    low = rest.astype(BF16)
    last = (rest - low.astype(F32)).astype(BF16)
    high, low, last = nn(high, onehot), nn(low, onehot), nn(last, onehot)
    rest = low + last
    fill = jnp.zeros((values.shape[0], stacked_ref.shape[2] - 3 * z.taps), F32)
    stacked = jnp.concatenate([high, high, rest, fill], axis=1)
    fill = jnp.zeros((values.shape[0], plain_ref.shape[2] - z.taps), F32)
    plain = jnp.concatenate([high + rest, fill], axis=1)
    for r in range(z.rows):
        for k in range(z.basis):
            at = k * z.rows + r
            stacked_ref[r, k : k + 1, :] = stacked[at : at + 1]
            plain_ref[r, k : k + 1, :] = plain[at : at + 1]


def band_rows(z, basis_values, row_reach):
    flat = jnp.transpose(basis_values, (1, 2, 0, 3))
    shapes = [(z.rows, z.basis, round_up(3 * z.taps, LANES)), (z.rows, z.basis, round_up(z.taps, LANES))]
    return pl.pallas_call(
        partial(band_rows_body, z),
        name="band_rows",
        grid_spec=pltpu.PrefetchScalarGridSpec(
            num_scalar_prefetch=1,
            grid=(1,),
            in_specs=[full(flat.shape)],
            out_specs=[full(shape) for shape in shapes],
        ),
        out_shape=[jax.ShapeDtypeStruct(shape, F32) for shape in shapes],
        compiler_params=params(16),
    )(row_reach, flat)


def band(row, columns):
    spread = jnp.broadcast_to(row, (columns, row.shape[1]))
    return pltpu.roll(spread, 0, 1, stride=1, stride_axis=0)


def cut_body(z, inputs_ref, noise_ref, top_ref, bottom_ref, top_sides_ref, bottom_sides_ref, sides_ref):
    for b in range(z.samples):
        for i in range(z.rows):
            value = jnp.concatenate([inputs_ref[b, i], jnp.transpose(noise_ref[b, i])], axis=1)
            side = jnp.concatenate([value[z.columns - LON_HALO :], value[:LON_HALO]], axis=0)
            sides_ref[b, i] = side
            if i < LAT_HALO:
                top_ref[b, i] = value
                top_sides_ref[b, i] = side
            if i >= z.rows - LAT_HALO:
                bottom_ref[b, i - z.rows + LAT_HALO] = value
                bottom_sides_ref[b, i - z.rows + LAT_HALO] = side


def cut(z, inputs, noise):
    shape = lambda rows, columns: jax.ShapeDtypeStruct((z.samples, rows, columns, z.joined), F32)
    rim, side = shape(LAT_HALO, z.columns), shape(LAT_HALO, 2 * LON_HALO)
    return pl.pallas_call(
        partial(cut_body, z),
        name="cut",
        out_shape=[rim, rim, side, side, shape(z.rows, 2 * LON_HALO)],
        compiler_params=params(60),
    )(inputs, noise)


def mix_body(z, info_ref, band_ref, inputs_ref, noise_ref, above_ref, below_ref, above_sides_ref, below_sides_ref, sides_ref, gain_ref, shift_ref, mixed_ref, other_ref, lhs, high, low):
    at_row = pl.program_id(0)
    gap = z.span - z.columns - 2 * LON_HALO

    def place(sample, at, value, sides, present, gain, shift):
        value = jnp.concatenate([sides[:LON_HALO], value, sides[LON_HALO:]], axis=0)
        channel = lax.broadcasted_iota(jnp.int32, (1, z.joined), 1)
        inside = channel < z.width
        mean = jnp.sum(jnp.where(inside, value, 0.0), axis=1, keepdims=True) / z.width
        centered = jnp.where(inside, value - mean, 0.0)
        variance = jnp.sum(centered * centered, axis=1, keepdims=True) / z.width
        normed = centered * lax.rsqrt(variance + EPSILON) * gain + shift
        value = jnp.where(inside, normed, value) * present
        value = jnp.concatenate([value, jnp.zeros((value.shape[0], z.wide - z.joined), F32)], axis=1)
        value = jnp.concatenate([value, jnp.zeros((gap, z.wide), F32)], axis=0)
        high_part, low_part = split(value)
        rows, lanes = slice(at * z.span, (at + 1) * z.span), slice(sample * z.wide, (sample + 1) * z.wide)
        high[rows, lanes] = high_part
        low[rows, lanes] = low_part

    @pl.when(at_row == 0)
    def _():
        fill = jnp.zeros((1, z.joined - z.width), F32)
        gain = jnp.concatenate([row(gain_ref), fill], axis=1)
        shift = jnp.concatenate([row(shift_ref), fill], axis=1)
        has_above = (info_ref[1] != 0).astype(F32)
        has_below = (info_ref[2] != 0).astype(F32)
        for b in range(z.samples):
            for i in range(LAT_HALO):
                place(b, i, above_ref[b, i], above_sides_ref[b, i], has_above, gain, shift)
                place(b, i + z.rows + LAT_HALO, below_ref[b, i], below_sides_ref[b, i], has_below, gain, shift)
            for i in range(z.rows):
                value = jnp.concatenate([inputs_ref[b, i], jnp.transpose(noise_ref[b, i])], axis=1)
                place(b, i + LAT_HALO, value, sides_ref[b, i], 1.0, gain, shift)

    for k in range(z.basis):
        value = band(band_ref[0, k : k + 1, :], z.columns)
        lhs[k * z.columns : (k + 1) * z.columns, :] = value.astype(BF16)

    rows = pl.ds(pl.multiple_of(at_row * z.span, 16), z.taps)
    top, rest = high[rows, :], low[rows, :]
    product = nn(lhs[:, : 3 * z.taps], jnp.concatenate([top, rest, top], axis=0))
    for b in range(z.samples):
        tail = jnp.zeros((z.columns, LANES), F32)
        for k in range(z.basis):
            part = product[k * z.columns : (k + 1) * z.columns, b * z.wide : (b + 1) * z.wide]
            mixed_ref[b, :, k * z.main : (k + 1) * z.main] = part[:, : z.main]
            last = part[:, z.main :]
            tail = tail + (last if k == 0 else pltpu.roll(last, z.extra * k, 1))
        mixed_ref[b, :, z.basis * z.main :] = tail

    @pl.when(info_ref[0] == 0)
    def _():
        other_ref[...] = mixed_ref[:, :, z.half :]

    @pl.when(info_ref[0] != 0)
    def _():
        other_ref[...] = mixed_ref[:, :, : z.half]


def mix(z, info, bands, inputs, noise, above, below, sides, gain, shift):
    height = (z.rows + 2 * LAT_HALO) * z.span
    lanes = bands.shape[2]
    arrays = [inputs, noise, above, below, *sides, gain, shift]
    mixed, other = pl.pallas_call(
        partial(mix_body, z),
        name="mix",
        grid_spec=pltpu.PrefetchScalarGridSpec(
            num_scalar_prefetch=1,
            grid=(z.rows,),
            in_specs=[
                pl.BlockSpec((1, z.basis, lanes), lambda r, *_: (r, 0, 0)),
                *(full(a.shape) for a in arrays),
            ],
            out_specs=[
                pl.BlockSpec((z.samples, z.columns, z.depth), lambda r, *_: (0, r, 0)),
                pl.BlockSpec((z.samples, z.columns, z.half), lambda r, *_: (0, r, 0)),
            ],
            scratch_shapes=[
                pltpu.VMEM((z.basis * z.columns, lanes), BF16),
                pltpu.VMEM((height, z.samples * z.wide), BF16),
                pltpu.VMEM((height, z.samples * z.wide), BF16),
            ],
        ),
        out_shape=[
            pltpu.HBM((z.samples, z.rows * z.columns, z.depth), F32),
            pltpu.HBM((z.samples, z.rows * z.columns, z.half), F32),
        ],
        compiler_params=params(34),
        cost_estimate=cost(z.pixels * z.basis * z.taps * z.joined, 8 * z.pixels * z.depth),
    )(info, bands, *arrays)
    return mixed.reshape(z.pixels, z.depth), other.reshape(z.pixels, z.half)


def conv_body(z, mixed_ref, tail_ref, weight_ref, base_ref, bias_ref, out_ref, tail_weight):
    step = pl.program_id(0)

    @pl.when(step == 0)
    def _():
        out_ref[...] = base_ref[...] + row(bias_ref)
        tail_weight[...] = jnp.zeros_like(tail_weight)

    out_ref[...] += nt(left(mixed_ref[...]), right_t(weight_ref[0, :, : z.main]))
    last = weight_ref[0, :, z.main :]
    last = jnp.concatenate([last, jnp.zeros((last.shape[0], LANES - z.extra), F32)], axis=1)
    tail_weight[...] += pltpu.roll(last, z.extra * step, 1)

    @pl.when(step == z.basis - 1)
    def _():
        out_ref[...] += nt(left(tail_ref[...]), right_t(tail_weight[...]))


def conv(z, mixed, weight, base, bias):
    return pl.pallas_call(
        partial(conv_body, z),
        name="conv",
        grid=(z.basis,),
        in_specs=[
            pl.BlockSpec((z.pixels, z.main), lambda k: (0, k)),
            pl.BlockSpec((z.pixels, LANES), lambda k: (0, z.basis * z.tiles)),
            pl.BlockSpec((1, z.width, z.joined), lambda k: (k, 0, 0)),
            full((z.pixels, z.width)),
            full(bias.shape),
        ],
        out_specs=result((z.pixels, z.width)),
        out_shape=jax.ShapeDtypeStruct((z.pixels, z.width), F32),
        scratch_shapes=[pltpu.VMEM((z.width, LANES), F32)],
        compiler_params=params(44),
        cost_estimate=cost(z.pixels * z.depth * z.width, 4 * z.depth * (z.width + z.pixels)),
    )(mixed, mixed, weight, base, bias)


def mlp_body(
    z,
    info_ref,
    middle_ref,
    cot_ref,
    d_active_ref,
    weight_ref,
    bias_ref,
    gain_ref,
    shift_ref,
    kept_ref,
    sent_ref,
    active_high_ref,
    active_low_ref,
    d_pre_high_ref,
    d_pre_low_ref,
    d_bias_ref,
    second_ref,
    second_lhs,
    second_t,
    cot_t,
    tail,
):
    step = pl.program_id(0)
    main = z.main

    @pl.when(step == 0)
    def _():
        norm, _ = normalize(middle_ref[...])
        second = norm * row(gain_ref) + row(shift_ref)
        second_ref[...] = second
        second_lhs[...] = left(second[:, :main])
        second_t[...] = left(padded_t(second, z.wide)[: z.high])
        cot_t[...] = left(padded_t(cot_ref[...], z.wide)[: z.high])

    def store(out_ref, which, value, last):
        if not last:
            for i in range(z.tiles):
                out_ref[0, i * z.high : (i + 1) * z.high, :] = value[:, i * LANES : (i + 1) * LANES]
            out_ref[0, z.tiles * z.high :, :] = tail[which, step - 1]
            return
        fill = jnp.zeros((z.wide - z.high, LANES), F32)
        value = jnp.transpose(jnp.concatenate([value, fill], axis=0))[:8]
        for i in range(z.parts):
            half, place = i // (z.parts // 2), i % (z.parts // 2)
            tail[which, half, 8 * place : 8 * place + 8, :] = value[:, i * LANES : (i + 1) * LANES]

    def body(width, last):
        weight = only(z, weight_ref[:, :width], last)
        start = z.steps * main if last else pl.multiple_of((step - 1) * main, LANES)
        bias = bias_ref[pl.ds(start, z.rest if last else width)]
        bias = bias.reshape(1, bias.shape[0])
        if last:
            bias = jnp.concatenate([bias, jnp.zeros((1, width - z.rest), F32)], axis=1)
        d_active = only(z, d_active_ref[:, :width], last)
        pre = nn(second_lhs[...], right(weight[:main]))
        pre = pre + second_ref[:, main : main + 1] * weight[main : main + 1] + bias
        cdf = 0.5 * (1.0 + lax.erf(pre * np.float32(0.5**0.5)))
        pdf = jnp.exp(pre * pre * -0.5) * np.float32(1.0 / np.sqrt(2.0 * np.pi))
        active = only(z, pre * cdf, last)
        d_pre = d_active * (cdf + pre * pdf)
        high, low = split(active)
        active_high_ref[:, :width] = high
        active_low_ref[:, :width] = low
        output_grad = nn(cot_t[...], jnp.concatenate([high, low, high], axis=0))
        high, low = split(d_pre)
        d_pre_high_ref[:, :width] = high
        d_pre_low_ref[:, :width] = low
        d_bias_ref[:, :width] = jnp.sum(d_pre, axis=0, keepdims=True)
        hidden_grad = nn(second_t[...], jnp.concatenate([high, low, high], axis=0))

        @pl.when(info_ref[0] == 0)
        def _():
            store(kept_ref, 0, output_grad, last)
            store(sent_ref, 1, hidden_grad, last)

        @pl.when(info_ref[0] != 0)
        def _():
            store(sent_ref, 0, output_grad, last)
            store(kept_ref, 1, hidden_grad, last)

    pl.when(step == 0)(lambda: body(LANES, True))
    pl.when(step > 0)(lambda: body(z.main, False))


def mlp(z, info, middle, cot, d_active, weight, bias, gain, shift):
    flat = (2, z.mlp_half, LANES)
    at = lambda i: jnp.where(i == 0, z.steps, i - 1)
    hidden = pl.BlockSpec((z.pixels, z.main), lambda i, *_: (0, at(i)))
    half = pl.BlockSpec((1, z.mlp_half, LANES), lambda i, *_: (jnp.maximum(i - 1, 0), 0, 0))
    wide = pltpu.HBM((z.pixels, z.hidden), BF16)
    return pl.pallas_call(
        partial(mlp_body, z),
        name="mlp",
        grid_spec=pltpu.PrefetchScalarGridSpec(
            num_scalar_prefetch=1,
            grid=(z.steps + 1,),
            in_specs=[
                full((z.pixels, z.width)),
                full((z.pixels, z.width)),
                hidden,
                pl.BlockSpec((z.width, z.main), lambda i, *_: (0, at(i))),
                full(bias.shape),
                full(gain.shape),
                full(shift.shape),
            ],
            out_specs=[
                half,
                half,
                hidden,
                hidden,
                hidden,
                hidden,
                pl.BlockSpec((1, z.main), lambda i, *_: (0, at(i))),
            ],
            scratch_shapes=[
                pltpu.VMEM((z.pixels, z.width), F32),
                pltpu.VMEM((z.pixels, 3 * z.main), BF16),
                pltpu.VMEM((z.high, 3 * z.pixels), BF16),
                pltpu.VMEM((z.high, 3 * z.pixels), BF16),
                pltpu.VMEM((2, z.steps, 8 * z.parts // 2, LANES), F32),
            ],
        ),
        out_shape=[
            pltpu.HBM(flat, F32),
            pltpu.HBM(flat, F32),
            wide,
            wide,
            wide,
            wide,
            jax.ShapeDtypeStruct((1, z.hidden), F32),
        ],
        compiler_params=params(44),
        cost_estimate=cost(3 * z.pixels * z.width * z.hidden, 12 * z.width * z.hidden),
    )(info, middle, cot, d_active, weight, bias, gain, shift)


def middle_back_body(z, high_ref, low_ref, weight_ref, middle_ref, cot_ref, gain_ref, out_ref, out_t_ref, sums_ref, d_second):
    step = pl.program_id(0)

    @pl.when(step == 0)
    def _():
        d_second[...] = jnp.zeros_like(d_second)

    def body(width, last):
        high = only(z, high_ref[:, :width], last)
        low = only(z, low_ref[:, :width], last)
        weight = right_t(only(z, weight_ref[:, :width], last))
        d_second[...] += nt(jnp.concatenate([high, high, low], axis=1), weight)

    hidden_steps(z, body)

    @pl.when(step == z.steps)
    def _():
        norm, inverse = normalize(middle_ref[...])
        grad = d_second[...]
        sums_ref[0:1, :] = jnp.sum(grad * norm, axis=0, keepdims=True)
        sums_ref[1:2, :] = jnp.sum(grad, axis=0, keepdims=True)
        cot = cot_ref[...]
        sums_ref[3:4, :] = jnp.sum(cot, axis=0, keepdims=True)
        d_middle = cot + norm_back(grad * row(gain_ref), norm, inverse)
        sums_ref[2:3, :] = jnp.sum(d_middle, axis=0, keepdims=True)
        out_ref[...] = d_middle
        out_t_ref[...] = padded_t(d_middle, z.wide)[: z.high]


def middle_back(z, high, low, weight, middle, cot, gain):
    hidden = pl.BlockSpec((z.pixels, z.main), lambda i: (0, i))
    return pl.pallas_call(
        partial(middle_back_body, z),
        name="middle_back",
        grid=(z.steps + 1,),
        in_specs=[
            hidden,
            hidden,
            pl.BlockSpec((z.width, z.main), lambda i: (0, i)),
            full((z.pixels, z.width)),
            full((z.pixels, z.width)),
            full(gain.shape),
        ],
        out_specs=[
            full((z.pixels, z.width)),
            full((z.high, z.pixels)),
            full((4, z.width)),
        ],
        out_shape=[
            jax.ShapeDtypeStruct((z.pixels, z.width), F32),
            jax.ShapeDtypeStruct((z.high, z.pixels), F32),
            jax.ShapeDtypeStruct((4, z.width), F32),
        ],
        scratch_shapes=[pltpu.VMEM((z.pixels, z.width), F32)],
        compiler_params=params(58),
        cost_estimate=cost(z.pixels * z.width * z.hidden, 8 * z.width * z.hidden),
    )(high, low, weight, middle, cot, gain)


def output_body(z, high_ref, low_ref, weight_ref, middle_ref, bias_ref, out_ref):
    @pl.when(pl.program_id(0) == 0)
    def _():
        out_ref[...] = middle_ref[...] + row(bias_ref)

    def body(width, last):
        high = only(z, high_ref[:, :width], last)
        low = only(z, low_ref[:, :width], last)
        weight = right_t(only(z, weight_ref[:, :width], last))
        out_ref[...] += nt(jnp.concatenate([high, high, low], axis=1), weight)

    hidden_steps(z, body)


def output(z, high, low, weight, middle, bias):
    hidden = pl.BlockSpec((z.pixels, z.main), lambda i: (0, i))
    return pl.pallas_call(
        partial(output_body, z),
        name="output",
        grid=(z.steps + 1,),
        in_specs=[
            hidden,
            hidden,
            pl.BlockSpec((z.width, z.main), lambda i: (0, i)),
            full((z.pixels, z.width)),
            full(bias.shape),
        ],
        out_specs=full((z.pixels, z.width)),
        out_shape=jax.ShapeDtypeStruct((z.pixels, z.width), F32),
        compiler_params=params(58),
        cost_estimate=cost(z.pixels * z.width * z.hidden, 8 * z.width * z.hidden),
    )(high, low, weight, middle, bias)


def conv_grad_body(z, info_ref, own_ref, far_ref, own_t_ref, far_t_ref, out_ref, lhs):
    step = pl.program_id(0)
    tiles = own_ref.shape[1] // LANES

    @pl.when(step == 0)
    def _():
        lhs[...] = left(jnp.concatenate([own_t_ref[...], far_t_ref[...]], axis=1))
        used = pl.num_programs(0) * tiles * z.high
        out_ref[used:, :] = jnp.zeros((out_ref.shape[0] - used, LANES), F32)

    value = nn(lhs[...], right(jnp.concatenate([own_ref[...], far_ref[...]], axis=0)))
    for i in range(tiles):
        rows = pl.ds(pl.multiple_of((step * tiles + i) * z.high, 8), z.high)
        out_ref[rows, :] = value[:, i * LANES : (i + 1) * LANES]


def conv_grad(z, info, mixed, far_mixed, own_t, far_t):
    count = z.half // LANES // 2
    tiles = 3
    steps = count // tiles
    flat = round_up(count * z.high, 32)
    return pl.pallas_call(
        partial(conv_grad_body, z),
        name="conv_grad",
        grid_spec=pltpu.PrefetchScalarGridSpec(
            num_scalar_prefetch=1,
            grid=(steps,),
            in_specs=[
                pl.BlockSpec((z.pixels, tiles * LANES), lambda i, c: (0, (2 * c[0] + c[1]) * steps + i)),
                pl.BlockSpec((z.pixels, tiles * LANES), lambda i, c: (0, c[1] * steps + i)),
                full((z.high, z.pixels)),
                full((z.high, z.pixels)),
            ],
            out_specs=full((flat, LANES)),
            scratch_shapes=[pltpu.VMEM((z.high, 6 * z.pixels), BF16)],
        ),
        out_shape=jax.ShapeDtypeStruct((flat, LANES), F32),
        compiler_params=params(50),
        cost_estimate=cost(2 * z.pixels * z.width * count * LANES, 12 * z.pixels * count * LANES),
    )(info, mixed, far_mixed, own_t, far_t)


def mixed_back_body(z, weight_ref, dm_ref, high_ref, low_ref, lhs):
    columns, main = z.columns, z.main

    @pl.when(pl.program_id(0) == 0)
    def _():
        lhs[...] = left(dm_ref[:, :main])

    value = nn(lhs[...], right(weight_ref[0, :main, :]))
    value = value + dm_ref[:, main : main + 1] * weight_ref[0, main : main + 1, :]
    value_high, value_low = split(value)
    for b in range(z.samples):
        for r in range(z.rows):
            i = (b * z.rows + r) * columns
            lane = b * z.wide
            high_ref[r, :, lane : lane + z.joined] = value_high[i : i + columns]
            low_ref[r, :, lane : lane + z.joined] = value_low[i : i + columns]


def mixed_back(z, weight, d_middle):
    out = pl.BlockSpec((z.rows, z.columns, z.samples * z.wide), lambda i: (0, i, 0))
    shape = pltpu.HBM((z.rows, z.basis * z.columns, z.samples * z.wide), BF16)
    return pl.pallas_call(
        partial(mixed_back_body, z),
        name="mixed_back",
        grid=(z.basis,),
        in_specs=[
            pl.BlockSpec((1, z.width, z.joined), lambda i: (i, 0, 0)),
            full((z.pixels, z.width)),
        ],
        out_specs=[out, out],
        out_shape=[shape, shape],
        scratch_shapes=[pltpu.VMEM((z.pixels, 3 * z.main), BF16)],
        compiler_params=params(56),
        cost_estimate=cost(z.pixels * z.depth * z.width, 4 * z.depth * z.width),
    )(weight, d_middle)


def outer_columns(z, value):
    return jnp.concatenate([value[z.columns + LON_HALO : z.columns + 2 * LON_HALO], value[:LON_HALO]], axis=0)


def band_back_body(z, high_ref, low_ref, band_ref, out_ref, top_ref, bottom_ref, sides_ref):
    row_at = pl.program_id(0)
    columns = z.columns

    @pl.when(row_at == 0)
    def _():
        out_ref[...] = jnp.zeros_like(out_ref)

    spread = [band(band_ref[0, k : k + 1, :], columns) for k in range(z.basis)]
    spread = jnp.transpose(jnp.concatenate(spread, axis=0))[: z.taps]
    high, low = split(spread)
    top, rest = high_ref[0], low_ref[0]
    value = nn(high, top) + nn(high, rest) + nn(low, top)
    place = pl.ds(pl.multiple_of(row_at * z.span, 8), z.taps)
    for b in range(z.samples):
        out_ref[b, place, :] += value[:, b * z.wide : b * z.wide + z.joined]

    @pl.when(row_at == z.rows - 1)
    def _():
        for b in range(z.samples):
            for r in range(z.rows + 2 * LAT_HALO):
                value = out_ref[b, r * z.span : r * z.span + columns + 2 * LON_HALO, :]
                if r < LAT_HALO:
                    top_ref[b, r] = value
                elif r < z.rows + LAT_HALO:
                    sides_ref[b, r - LAT_HALO] = outer_columns(z, value)
                else:
                    bottom_ref[b, r - z.rows - LAT_HALO] = value


def band_back(z, high, low, bands):
    lanes = bands.shape[2]
    height = (z.rows + 2 * LAT_HALO) * z.span
    rim = (z.samples, LAT_HALO, z.columns + 2 * LON_HALO, z.joined)
    shapes = [(z.samples, height, z.joined), rim, rim, (z.samples, z.rows, 2 * LON_HALO, z.joined)]
    part = pl.BlockSpec((1,) + high.shape[1:], lambda i: (i, 0, 0))
    return pl.pallas_call(
        partial(band_back_body, z),
        name="band_back",
        grid=(z.rows,),
        in_specs=[part, part, pl.BlockSpec((1, z.basis, lanes), lambda i: (i, 0, 0))],
        out_specs=[full(shape) for shape in shapes],
        out_shape=[jax.ShapeDtypeStruct(shape, F32) for shape in shapes],
        compiler_params=params(56),
        cost_estimate=cost(z.pixels * z.basis * z.taps * z.joined, 8 * z.pixels * z.depth),
    )(high, low, bands)


def edge_body(z, sides_ref, above_ref, below_ref, out_ref):
    for b in range(z.samples):
        for r in range(z.rows):
            value = sides_ref[b, r]
            if r < LAT_HALO:
                value = value + outer_columns(z, above_ref[b, r])
            if r >= z.rows - LAT_HALO:
                value = value + outer_columns(z, below_ref[b, r - z.rows + LAT_HALO])
            out_ref[b, r] = value


def edge(z, sides, above, below):
    return pl.pallas_call(
        partial(edge_body, z),
        name="edge",
        out_shape=jax.ShapeDtypeStruct(sides.shape, F32),
        compiler_params=params(16),
        cost_estimate=cost(2**30, 2**24),
    )(sides, above, below)


def finish_body(
    z, padded_ref, above_ref, below_ref, sides_ref, inputs_ref, d_middle_ref, gain_ref, sums_ref, d_bias_ref, out_ref, vectors_ref, own
):
    sample = pl.program_id(0)

    @pl.when(sample == 0)
    def _():
        own[...] = jnp.zeros_like(own)

    for r in range(z.rows):
        start = (r + LAT_HALO) * z.span
        value = padded_ref[0, start : start + z.columns + 2 * LON_HALO, :]
        if r < LAT_HALO:
            value = value + above_ref[0, r]
        if r >= z.rows - LAT_HALO:
            value = value + below_ref[0, r - z.rows + LAT_HALO]
        middle = value[2 * LON_HALO : z.columns]
        low = value[LON_HALO : 2 * LON_HALO] + sides_ref[0, r, :LON_HALO]
        high = value[z.columns : z.columns + LON_HALO] + sides_ref[0, r, LON_HALO:]
        grad = jnp.concatenate([low, middle, high], axis=0)[:, : z.width]
        norm, inverse = normalize(inputs_ref[0, r])
        own[0:1, :] += jnp.sum(grad * norm, axis=0, keepdims=True)
        own[1:2, :] += jnp.sum(grad, axis=0, keepdims=True)
        grad = norm_back(grad * row(gain_ref), norm, inverse)
        out_ref[0, r] = d_middle_ref[0, r] + grad

    @pl.when(sample == pl.num_programs(0) - 1)
    def _():
        vectors_ref[...] = jnp.zeros_like(vectors_ref)
        row = 0
        rows = [(sums_ref, 2), (own, 0), (own, 1), (sums_ref, 0), (sums_ref, 1), (d_bias_ref, 0), (sums_ref, 3)]
        for ref, at in rows:
            size = ref.shape[1]
            for i in range(0, size, LANES):
                end = min(i + LANES, size)
                vectors_ref[row : row + 1, : end - i] = ref[at : at + 1, i:end]
                row += 1


def finish(z, padded, above, below, sides, inputs, d_middle, gain, sums, d_bias):
    shape = (z.samples, z.rows, z.columns, z.width)
    count = round_up(6 * pl.cdiv(z.width, LANES) + pl.cdiv(z.hidden, LANES), 16)

    def part(array):
        size = array.shape[1:]
        return pl.BlockSpec((1,) + size, lambda b: (b,) + (0,) * len(size))

    d_middle = d_middle.reshape(shape)
    arrays = [padded, above, below, sides, inputs, d_middle]
    return pl.pallas_call(
        partial(finish_body, z),
        name="finish",
        grid=(z.samples,),
        in_specs=[part(a) for a in arrays] + [full(gain.shape), full(sums.shape), full(d_bias.shape)],
        out_specs=[part(inputs), full((count, LANES))],
        out_shape=[jax.ShapeDtypeStruct(shape, F32), jax.ShapeDtypeStruct((count, LANES), F32)],
        scratch_shapes=[pltpu.VMEM((8, z.width), F32)],
        compiler_params=params(60),
        cost_estimate=cost(2**30, 2**24),
    )(*arrays, gain, sums, d_bias)


def conv_place_body(z, which, first, count, info_ref, *refs):
    number = len(which)
    pieces, (out_ref, held, narrow, sems) = refs[:number], refs[-4:]
    main_tiles = z.basis * z.tiles
    with_extra = first + 2 * count == z.half // LANES
    used = count * z.high

    def get(i):
        return pltpu.make_async_copy(pieces[i].at[pl.ds(0, used), :], held.at[i], sems.at[i])

    def tile(i, t):
        return (info_ref[which[i]] // 2) * (z.half // LANES) + first + (info_ref[which[i]] % 2) * count + t

    def put(i, t):
        at = tile(i, t)
        lanes = pl.ds(pl.multiple_of(at % z.tiles * LANES, LANES), LANES)
        return pltpu.make_async_copy(
            held.at[i, pl.ds(t * z.high, z.width), :],
            out_ref.at[at // z.tiles, :, lanes],
            sems.at[number + i * count + t],
        )

    def put_extra(k):
        return pltpu.make_async_copy(
            narrow.at[k], out_ref.at[k, :, pl.ds(z.main, z.extra)], sems.at[number * (1 + count) + k]
        )

    for i in range(number):
        get(i).start()
    for i in range(number):
        get(i).wait()
        for t in range(count):
            is_main = tile(i, t) < main_tiles

            @pl.when(is_main)
            def _():
                put(i, t).start()

            if with_extra and t == count - 1:

                @pl.when(jnp.logical_not(is_main))
                def _():
                    for k in range(z.basis):
                        value = held[i, t * z.high : (t + 1) * z.high, :]
                        value = value if k == 0 else pltpu.roll(value, LANES - z.extra * k, 1)
                        narrow[k] = value[: z.width, : z.extra]
                        put_extra(k).start()

    for i in range(number):
        if with_extra:

            @pl.when(tile(i, count - 1) >= main_tiles)
            def _():
                for k in range(z.basis):
                    put_extra(k).wait()

        for t in range(count):

            @pl.when(tile(i, t) < main_tiles)
            def _():
                put(i, t).wait()


def conv_place(z, places, which, first, count, pieces, onto):
    anywhere = pl.BlockSpec(memory_space=pl.ANY)
    operands = [places, *pieces]
    aliases = {}
    if onto is not None:
        operands.append(onto)
        aliases = {1 + len(which): 0}
    return pl.pallas_call(
        partial(conv_place_body, z, which, first, count),
        name="conv_place",
        grid_spec=pltpu.PrefetchScalarGridSpec(
            num_scalar_prefetch=1,
            grid=(),
            in_specs=[anywhere] * (len(operands) - 1),
            out_specs=anywhere,
            scratch_shapes=[
                pltpu.VMEM((len(which), count * z.high, LANES), F32),
                pltpu.VMEM((z.basis, z.width, z.extra), F32),
                pltpu.SemaphoreType.DMA((len(which) * (1 + count) + z.basis,)),
            ],
        ),
        out_shape=jax.ShapeDtypeStruct((z.basis, z.width, z.joined), F32),
        input_output_aliases=aliases,
        compiler_params=params(16),
        cost_estimate=cost(2**30, 2**24),
    )(*operands)


def mlp_place_body(z, info_ref, own_ref, far_ref, output_ref, hidden_ref, held, narrow, sems):
    main_tiles = 2 * z.tiles

    def place(refs):
        gets = []
        for i, ref in enumerate(refs):
            for half in range(2):
                rows = pl.ds(half * z.mlp_half, z.mlp_half)
                gets.append(pltpu.make_async_copy(ref.at[rows, :], held.at[i, half], sems.at[2 * i + half]))
                gets[-1].start()
        puts = []
        for i, out_ref in enumerate((output_ref, hidden_ref)):
            for t in range(main_tiles):
                half = t // z.tiles
                if t % z.tiles == 0:
                    gets[2 * i + half].wait()
                puts.append(
                    pltpu.make_async_copy(
                        held.at[i, half, pl.ds(t % z.tiles * z.high, z.width), :],
                        out_ref.at[:, pl.ds(t * LANES, LANES)],
                        sems.at[8 + i * main_tiles + t],
                    )
                )
                puts[-1].start()
            start = z.tiles * z.high
            parts = [
                held[i, half, start + 8 * j : start + 8 * j + 8, :] for half in range(2) for j in range(z.parts // 2)
            ]
            value = jnp.concatenate([jnp.concatenate(parts, axis=1)] * (LANES // 8), axis=0)
            narrow[i] = jnp.transpose(value)[: z.width, : z.rest]
            puts.append(
                pltpu.make_async_copy(
                    narrow.at[i],
                    out_ref.at[:, pl.ds(main_tiles * LANES, z.rest)],
                    sems.at[8 + 2 * main_tiles + i],
                )
            )
            puts[-1].start()
        for c in puts:
            c.wait()

    pl.when(info_ref[0] == 0)(lambda: place((own_ref, far_ref)))
    pl.when(info_ref[0] != 0)(lambda: place((far_ref, own_ref)))


def mlp_place(z, info, own, far):
    shape = jax.ShapeDtypeStruct((z.width, z.hidden), F32)
    anywhere = pl.BlockSpec(memory_space=pl.ANY)
    return pl.pallas_call(
        partial(mlp_place_body, z),
        name="mlp_place",
        grid_spec=pltpu.PrefetchScalarGridSpec(
            num_scalar_prefetch=1,
            grid=(),
            in_specs=[anywhere, anywhere],
            out_specs=[anywhere, anywhere],
            scratch_shapes=[
                pltpu.VMEM((2, 2, z.mlp_half, LANES), F32),
                pltpu.VMEM((2, z.width, z.rest), F32),
                pltpu.SemaphoreType.DMA((4 * z.tiles + 10,)),
            ],
        ),
        out_shape=[shape, shape],
        compiler_params=params(16),
        cost_estimate=cost(2**30, 2**22),
    )(info, own, far)


def axis_size(axes):
    size = 1
    for axis in axes:
        size *= lax.axis_size(axis)
    return size


def pairs(lats, lons, target):
    found = []
    for lat in range(lats):
        for lon in range(lons):
            to_lat, to_lon = target(lat, lon)
            found.append((lat * lons + lon, to_lat * lons + to_lon))
    return found


class GridSum:
    def __init__(self):
        lats, lons = axis_size(LAT), axis_size(LON)
        lat, lon = lax.axis_index(LAT), lax.axis_index(LON)
        over = partial(pairs, lats, lons)
        self.core = lat % 2
        self.cores = over(lambda a, o: (a ^ 1, o))
        self.first = over(lambda a, o: (a ^ 2, o) if a % 2 else (a, o ^ 1))
        self.second = over(lambda a, o: (a, o ^ 1) if a % 2 else (a ^ 2, o))
        self.third = over(lambda a, o: (a ^ 4, o))
        lon_bit, lat_bit = lon % 2, lat // 2 % 2
        self.first_bit = jnp.where(self.core == 0, lon_bit, lat_bit)
        self.second_bit = jnp.where(self.core == 0, lat_bit, lon_bit)
        self.third_bit = lat // 4 % 2
        far_bit = jnp.where(self.core == 0, lat_bit, lon_bit)
        mine, other = 2 * self.core, 2 * (1 - self.core)
        self.places = jnp.stack(
            [mine + self.first_bit, mine + 1 - self.first_bit, other + far_bit, other + 1 - far_bit]
        ).astype(jnp.int32)
        self.others = []
        bit = 8
        while bit < lats:
            self.others.append(over(lambda a, o, bit=bit: (a ^ bit, o)))
            bit *= 2
        bit = 2
        while bit < lons:
            self.others.append(over(lambda a, o, bit=bit: (a, o ^ bit)))
            bit *= 2

    def swap(self, value, where):
        return lax.ppermute(value, AXES, where)

    def all(self, value, where):
        return value + self.swap(value, where)


class Order:
    def __init__(self):
        self.last = ()
        self.held = True

    def use(self, value):
        if not self.held:
            return value
        value, self.last = lax.optimization_barrier((value, self.last))
        return value

    def mark(self, value):
        if self.held:
            self.last = (value,)
        return value

    def wait(self, value):
        return self.mark(self.use(value))

    def run(self, function, *values):
        return self.mark(function(*self.use(values)))


def sum_rows(size, index, arrays, vectors):
    count = 0 if vectors is None else vectors.shape[0]

    def body(index_ref, *refs):
        out_ref = refs[-1]
        total = refs[0][...]
        for ref in refs[1 : len(arrays)]:
            total = total + ref[...]
        out_ref[:size, :] = total
        if vectors is not None:
            out_ref[size:, :] = refs[len(arrays)][...]

    more = [] if vectors is None else [vectors]
    blocks = [pl.BlockSpec((size, LANES), lambda g, p, i=i: (p[i], 0)) for i in range(len(arrays))]
    return pl.pallas_call(
        body,
        name="sum_rows",
        grid_spec=pltpu.PrefetchScalarGridSpec(
            num_scalar_prefetch=1,
            grid=(1,),
            in_specs=blocks + [full(v.shape) for v in more],
            out_specs=full((size + count, LANES)),
        ),
        out_shape=jax.ShapeDtypeStruct((size + count, LANES), F32),
        compiler_params=params(16),
        cost_estimate=cost(2**30, 2**24),
    )(index, *arrays, *more)


def join_rows(size, bit, value, far):
    rows = value.shape[0] + size

    def body(bit_ref, value_ref, far_ref, out_ref):
        at = bit_ref[0]
        out_ref[pl.ds(pl.multiple_of(at * size, 8), size), :] = value_ref[:size, :]
        out_ref[pl.ds(pl.multiple_of((1 - at) * size, 8), size), :] = far_ref[:size, :]
        if rows > 2 * size:
            out_ref[2 * size :, :] = value_ref[size:, :] + far_ref[size:, :]

    return pl.pallas_call(
        body,
        name="join_rows",
        grid_spec=pltpu.PrefetchScalarGridSpec(
            num_scalar_prefetch=1,
            grid=(1,),
            in_specs=[full(value.shape), full(far.shape)],
            out_specs=full((rows, LANES)),
        ),
        out_shape=jax.ShapeDtypeStruct((rows, LANES), F32),
        compiler_params=params(16),
        cost_estimate=cost(2**30, 2**21),
    )(bit.reshape(1).astype(jnp.int32), value, far)


def add_rows(value, far, start=0):
    def body(value_ref, far_ref, out_ref):
        out_ref[...] = value_ref[...] + far_ref[start:, :]

    return pl.pallas_call(
        body,
        name="add_rows",
        out_shape=jax.ShapeDtypeStruct(value.shape, F32),
        compiler_params=params(16),
        cost_estimate=cost(2**30, 2**24),
    )(value, far)


def sum_tails(start, arrays):
    rows = arrays[0].shape[0] - start
    blocks = start % rows == 0

    def body(*refs):
        total = 0.0
        for ref in refs[:-1]:
            total = total + (ref[...] if blocks else ref[start:, :])
        refs[-1][...] = total

    spec = pl.BlockSpec((rows, LANES), lambda i: (start // rows, 0)) if blocks else full(arrays[0].shape)
    return pl.pallas_call(
        body,
        name="sum_tails",
        grid=(1,),
        in_specs=[spec] * len(arrays),
        out_specs=full((rows, LANES)),
        out_shape=jax.ShapeDtypeStruct((rows, LANES), F32),
        compiler_params=params(24),
        cost_estimate=cost(2**30, 2**22),
    )(*arrays)


class Chunk:
    def __init__(self, total, order, name, sent, kept):
        self.total, self.order, self.name = total, order, name
        self.terms, self.size = [(kept, 0)], sent.shape[0]
        self.vectors = None
        self.send("scatter_first", order.wait(sent), total.first)

    def send(self, step, value, where):
        with jax.named_scope(f"{self.name}_{step}"):
            self.value, self.far = value, self.total.swap(value, where)

    def take(self, index):
        arrays = [value for value, _ in self.terms]
        at = jnp.stack([jnp.asarray(index(at), jnp.int32) for _, at in self.terms])
        return self.order.run(partial(sum_rows, self.size), at, arrays, None)

    def halve(self, step, where, bit):
        self.terms.append((self.far, 0))
        self.size //= 2
        sent = self.take(lambda at: 2 * at + 1 - bit)
        self.terms = [(value, 2 * at + bit) for value, at in self.terms]
        self.send(step, sent, where)

    def join(self, bit):
        self.value = self.order.run(partial(join_rows, self.size), bit, self.value, self.far)
        self.size *= 2

    def scatter_second(self):
        self.halve("scatter_second", self.total.second, self.total.second_bit)

    def across_first(self):
        self.halve("across_first", self.total.third, self.total.third_bit)

    def across_second(self):
        self.terms.append((self.far, 0))
        self.value = self.take(lambda at: at)
        for where in self.total.others[:-1]:
            self.send("across", self.value, where)
            self.value = self.order.run(add_rows, self.value, self.far)
        self.send("across_second", self.value, self.total.others[-1])

    def across_third(self):
        both = [self.value, self.far]
        value = self.order.run(partial(sum_rows, self.size), jnp.zeros((2,), jnp.int32), both, self.vectors)
        self.send("across_third", value, self.total.third)

    def gather_second(self):
        self.join(self.total.third_bit)
        self.send("gather_second", self.value, self.total.second)

    def gather_first(self):
        self.join(self.total.second_bit)
        self.send("gather_first", self.value, self.total.first)
        with jax.named_scope(f"{self.name}_near_core"):
            self.near = self.total.swap(self.value, self.total.cores)

    def gather_whole(self):
        self.join(self.total.first_bit)
        with jax.named_scope(f"{self.name}_near_core"):
            self.near = self.total.swap(self.value, self.total.cores)

    def gather_core(self):
        self.far = self.order.wait(self.far)
        with jax.named_scope(f"{self.name}_gather_core"):
            self.last = self.total.swap(self.far, self.total.cores)

    def pieces(self):
        return self.value, self.far, self.near, self.last


def after(value, *others):
    return lax.optimization_barrier((value, others))[0]


def rows_of(vector):
    size = round_up(vector.shape[0], LANES)
    return jnp.pad(vector, (0, size - vector.shape[0])).reshape(-1, LANES)


def moved(value, axis, steps, cycle):
    count = axis_size(axis)
    if cycle:
        where = [(i, (i + steps) % count) for i in range(count)]
    else:
        where = [(i, i + steps) for i in range(max(0, -steps), min(count, count - steps))]
    return lax.ppermute(value, axis, where)


def edges(sides, down):
    lats, lons = axis_size(LAT), axis_size(LON)

    def shifted(value, steps):
        where = [
            (lat * lons + lon, (lat + down) * lons + (lon + steps) % lons)
            for lat in range(max(0, -down), min(lats, lats - down))
            for lon in range(lons)
        ]
        return lax.ppermute(value, AXES, where)

    if lons == 2:
        return shifted(sides, 1)
    return jnp.concatenate([shifted(sides[:, :, :LON_HALO], 1), shifted(sides[:, :, LON_HALO:], -1)], axis=2)


def local(
    inputs,
    noise_field,
    basis_values,
    row_reach,
    conv_weight,
    conv_bias,
    first_gain,
    first_shift,
    second_gain,
    second_shift,
    hidden_weight,
    hidden_bias,
    output_weight,
    output_bias,
    cotangent,
):
    z = Sizes(inputs, noise_field, conv_weight, hidden_weight)
    total = GridSum()
    lat, lats = lax.axis_index(LAT), axis_size(LAT)
    info = jnp.stack([total.core, (lat > 0).astype(jnp.int32), (lat < lats - 1).astype(jnp.int32)])
    rows, columns, width = z.rows, z.columns, z.width
    flat = (z.pixels, width)
    cot = cotangent.reshape(flat)
    conv_weight = jnp.transpose(conv_weight, (0, 2, 1))
    output_weight = jnp.transpose(output_weight)

    noise = jnp.transpose(noise_field, (0, 1, 3, 2))
    top, bottom, top_sides, bottom_sides, sides = cut(z, inputs, noise)
    below, above = moved(top, LAT, -1, False), moved(bottom, LAT, 1, False)
    sides = [edges(bottom_sides, 1), edges(top_sides, -1), edges(sides, 0)]
    d_active = active_back(z, cot, output_weight)
    bands, plain_bands = band_rows(z, basis_values, row_reach)
    above, below, sides = after((above, below, sides), d_active)
    mixed, other = mix(z, info, bands, inputs, noise, above, below, sides, first_gain, first_shift)
    far_mixed = total.swap(other, total.cores)
    middle = conv(z, mixed, conv_weight, inputs.reshape(flat), conv_bias)
    kept, sent, active_high, active_low, d_pre_high, d_pre_low, d_hidden_bias = mlp(
        z, info, middle, cot, d_active, hidden_weight, hidden_bias, second_gain, second_shift
    )
    order = Order()
    arrived = total.swap(sent, total.cores)

    d_middle, d_middle_t, sums = order.run(
        partial(middle_back, z), d_pre_high, d_pre_low, hidden_weight, middle, cot, second_gain
    )
    far_t = total.swap(d_middle_t, total.cores)

    bit = total.first_bit
    kept, arrived = kept.reshape(-1, LANES), arrived.reshape(-1, LANES)
    add_half = lambda k, r, w: sum_rows(z.mlp_half, jnp.stack([w, w]).astype(jnp.int32), [k, r], None)
    m = Chunk(total, order, "m", order.run(add_half, kept, arrived, 1 - bit), None)
    m.terms = [(kept, bit), (arrived, bit)]
    half = lambda which: order.run(
        lambda *v: conv_grad(z, jnp.stack([total.core, which]), *v), mixed, far_mixed, d_middle_t, far_t
    )
    c = Chunk(total, order, "c", half(1 - bit), None)
    c.terms = [(half(bit), 0)]
    m.scatter_second()
    d_mixed = order.run(partial(mixed_back, z), conv_weight, d_middle)
    m.across_first()
    c.scatter_second()
    m.across_second()
    d_padded, top, bottom, sides = order.run(partial(band_back, z), *d_mixed, plain_bands)
    c.across_first()
    m.across_third()
    top, bottom = order.wait((top, bottom))
    from_below = moved(top, LAT, -1, False)
    from_above = moved(bottom, LAT, 1, False)
    block_output = order.run(
        partial(output, z), active_high, active_low, output_weight, middle, output_bias
    )
    m.gather_second()
    c.across_second()
    outer = order.run(partial(edge, z), sides, from_above, from_below)
    from_sides = edges(outer, 0)
    input_grad, vectors = order.run(
        partial(finish, z), d_padded, from_above, from_below, from_sides, inputs, d_middle, first_gain, sums, d_hidden_bias
    )

    c.vectors = vectors
    c.across_third()
    m.gather_first()
    c.gather_second()
    m.gather_whole()
    c.gather_first()
    place = partial(conv_place, z, total.places)
    count = z.half // LANES // 2
    conv_weight_grad = order.run(lambda *v: place((0, 2), 0, count, v, None), c.value, c.near)
    output_weight_grad, hidden_weight_grad = order.run(lambda *v: mlp_place(z, info, *v), m.value, m.near)
    c.gather_core()
    place_far = lambda *v: place((1,), 0, count, v[:1], v[1])
    place_last = lambda *v: place((3,), 0, count, v[:1], v[1])
    conv_weight_grad = order.run(place_far, c.far, conv_weight_grad)
    vectors = order.run(lambda *v: sum_tails(c.size, v), *c.pieces())
    far_vectors = total.swap(vectors, total.others[0])
    conv_weight_grad = order.run(place_last, c.last, conv_weight_grad)
    vectors = order.run(add_rows, vectors, far_vectors)
    for where in total.others[1:]:
        vectors = order.run(add_rows, vectors, total.swap(vectors, where))
    found, start = [], 0
    for size in (width,) * 5 + (z.hidden, width):
        count = pl.cdiv(size, LANES)
        found.append(vectors[start : start + count].reshape(-1)[:size])
        start += count
    conv_weight_grad = jnp.transpose(conv_weight_grad, (0, 2, 1))
    output_weight_grad = jnp.transpose(output_weight_grad)
    conv_bias_grad, first_gain_grad, first_shift_grad, second_gain_grad, second_shift_grad = found[:5]
    hidden_bias_grad, output_bias_grad = found[5:]
    return (
        block_output.reshape(inputs.shape),
        input_grad,
        conv_weight_grad,
        conv_bias_grad,
        first_gain_grad,
        first_shift_grad,
        second_gain_grad,
        second_shift_grad,
        hidden_weight_grad,
        hidden_bias_grad,
        output_weight_grad,
        output_bias_grad,
    )


def solution(mesh):
    lats, lons = mesh.shape["lat"], mesh.shape["lon"]
    fine = Mesh(mesh.devices.reshape(lats // 4, 2, 2, lons // 2, 2), AXES)
    grid = P(None, LAT, LON, None)
    weights = (P(),) * 10
    in_specs = (grid, grid, P(LAT, None, None, None), P(LAT)) + weights + (grid,)
    out_specs = (grid, grid) + weights
    return jax.shard_map(local, mesh=fine, in_specs=in_specs, out_specs=out_specs, check_vma=False)
```

```python
from functools import partial

import jax
import jax.numpy as jnp
import numpy as np
from jax import lax
from jax.experimental import pallas as pl
from jax.experimental.pallas import tpu as pltpu
from jax.sharding import Mesh, PartitionSpec as P

LAT_HALO = 2
LON_HALO = 4
EPSILON = 1e-05
F32 = jnp.float32
BF16 = jnp.bfloat16
LAT = ("z", "y", "core")
LON = ("w", "x")
AXES = LAT + LON
LANES = 128
STEP = 256


def split(value):
    high = value.astype(BF16)
    return high, (value - high.astype(F32)).astype(BF16)


def left(value):
    high, low = split(value)
    return jnp.concatenate([high, high, low], axis=1)


def right(value):
    high, low = split(value)
    return jnp.concatenate([high, low, high], axis=0)


def right_t(value):
    high, low = split(value)
    return jnp.concatenate([high, low, high], axis=1)


def nn(a, b):
    return lax.dot_general(a, b, (((1,), (0,)), ((), ())), preferred_element_type=F32)


def nt(a, b):
    return lax.dot_general(a, b, (((1,), (1,)), ((), ())), preferred_element_type=F32)


def params(megabytes=30):
    return pltpu.CompilerParams(vmem_limit_bytes=megabytes * 1024 * 1024)


def cost(macs, moved):
    return pl.CostEstimate(flops=12 * macs, bytes_accessed=moved, transcendentals=0)


def full(shape):
    return pl.BlockSpec(shape, lambda *_: (0,) * len(shape), pipeline_mode=pl.Buffered(1))


def result(shape):
    return pl.BlockSpec(shape, lambda *_: (0,) * len(shape))


def row(ref):
    return ref[...].reshape(1, ref.shape[0])


def round_up(value, to):
    return -(-value // to) * to


def normalize(field):
    average = jnp.mean(field, axis=-1, keepdims=True)
    centered = field - average
    variance = jnp.mean(centered * centered, axis=-1, keepdims=True)
    inverse = lax.rsqrt(variance + EPSILON)
    return centered * inverse, inverse


def norm_back(grad_norm, normalized, inverse):
    first_term = jnp.mean(grad_norm, axis=-1, keepdims=True)
    second_term = jnp.mean(grad_norm * normalized, axis=-1, keepdims=True)
    return inverse * (grad_norm - first_term - normalized * second_term)


def padded_t(value, size):
    return jnp.transpose(
        jnp.concatenate(
            [value, jnp.zeros((value.shape[0], size - value.shape[1]), value.dtype)], axis=1
        )
    )


class Sizes:
    def __init__(self, inputs, noise_field, conv_weight, hidden_weight):
        self.samples, self.rows, self.columns, self.width = inputs.shape
        self.joined = self.width + noise_field.shape[-1]
        self.basis = conv_weight.shape[0]
        self.hidden = hidden_weight.shape[1]
        self.pixels = self.samples * self.rows * self.columns
        self.main = self.width // LANES * LANES
        self.tiles = self.main // LANES
        self.extra = self.joined - self.main
        self.span = round_up(self.columns + 2 * LON_HALO, 16)
        self.taps = (2 * LAT_HALO + 1) * self.span
        self.depth = self.basis * self.main + LANES
        self.half = self.depth // 2
        self.wide = self.main + LANES
        self.high = round_up(self.width, 8)
        self.steps = self.hidden // self.main
        self.rest = self.hidden - self.steps * self.main
        self.parts = self.wide // LANES
        self.mlp_half = self.tiles * self.high + 8 * self.parts // 2


def hidden_steps(z, body):
    step = pl.program_id(0)
    pl.when(step < z.steps)(lambda: body(z.main, False))
    pl.when(step == z.steps)(lambda: body(LANES, True))


def only(z, value, last):
    if not last:
        return value
    valid = lax.broadcasted_iota(jnp.int32, (1, LANES), 1) < z.rest
    return jnp.where(valid, value.astype(F32), 0.0).astype(value.dtype)


def active_back_body(z, cot_ref, weight_ref, out_ref, lhs):
    main = z.main

    @pl.when(pl.program_id(0) == 0)
    def _():
        lhs[...] = left(cot_ref[:, :main])

    def body(width, last):
        product = nn(lhs[...], right(weight_ref[:main, :width]))
        out_ref[:, :width] = product + cot_ref[:, main : main + 1] * weight_ref[main : main + 1, :width]

    hidden_steps(z, body)


def active_back(z, cot, weight):
    return pl.pallas_call(
        partial(active_back_body, z),
        name="active_back",
        grid=(z.steps + 1,),
        in_specs=[
            full((z.pixels, z.width)),
            pl.BlockSpec((z.width, z.main), lambda i: (0, i)),
        ],
        out_specs=pl.BlockSpec((z.pixels, z.main), lambda i: (0, i)),
        out_shape=pltpu.HBM((z.pixels, z.hidden), F32),
        scratch_shapes=[pltpu.VMEM((z.pixels, 3 * z.main), BF16)],
        compiler_params=params(60),
        cost_estimate=cost(z.pixels * z.width * z.hidden, 8 * z.width * z.hidden),
    )(cot, weight)


def band_rows_body(z, reach_ref, basis_ref, stacked_ref, plain_ref):
    width = 2 * LON_HALO + 1
    height = 2 * LAT_HALO + 1
    offset = lax.broadcasted_iota(jnp.int32, (1, height * width), 1) % width - LON_HALO
    row_at = lax.broadcasted_iota(jnp.int32, (z.rows, 1), 0)
    reach = jnp.zeros((z.rows, 1), jnp.int32)
    for r in range(z.rows):
        reach = jnp.where(row_at == r, reach_ref[r], reach)
    values = [
        jnp.where(
            jnp.abs(offset) <= reach, jnp.concatenate([basis_ref[k, a] for a in range(height)], axis=1), 0.0
        )
        for k in range(z.basis)
    ]
    values = jnp.concatenate(values, axis=0)
    source = lax.broadcasted_iota(jnp.int32, (values.shape[1], z.taps), 0)
    target = lax.broadcasted_iota(jnp.int32, (values.shape[1], z.taps), 1)
    place = source // width * z.span + source % width
    onehot = (place == target).astype(BF16)
    high = values.astype(BF16)
    rest = values - high.astype(F32)
    low = rest.astype(BF16)
    last = (rest - low.astype(F32)).astype(BF16)
    high, low, last = nn(high, onehot), nn(low, onehot), nn(last, onehot)
    rest = low + last
    fill = jnp.zeros((values.shape[0], stacked_ref.shape[2] - 3 * z.taps), F32)
    stacked = jnp.concatenate([high, high, rest, fill], axis=1)
    fill = jnp.zeros((values.shape[0], plain_ref.shape[2] - z.taps), F32)
    plain = jnp.concatenate([high + rest, fill], axis=1)
    for r in range(z.rows):
        for k in range(z.basis):
            at = k * z.rows + r
            stacked_ref[r, k : k + 1, :] = stacked[at : at + 1]
            plain_ref[r, k : k + 1, :] = plain[at : at + 1]


def band_rows(z, basis_values, row_reach):
    flat = jnp.transpose(basis_values, (1, 2, 0, 3))
    shapes = [(z.rows, z.basis, round_up(3 * z.taps, LANES)), (z.rows, z.basis, round_up(z.taps, LANES))]
    return pl.pallas_call(
        partial(band_rows_body, z),
        name="band_rows",
        grid_spec=pltpu.PrefetchScalarGridSpec(
            num_scalar_prefetch=1,
            grid=(1,),
            in_specs=[full(flat.shape)],
            out_specs=[full(shape) for shape in shapes],
        ),
        out_shape=[jax.ShapeDtypeStruct(shape, F32) for shape in shapes],
        compiler_params=params(16),
    )(row_reach, flat)


def band(row, columns):
    spread = jnp.broadcast_to(row, (columns, row.shape[1]))
    return pltpu.roll(spread, 0, 1, stride=1, stride_axis=0)


def cut_body(z, inputs_ref, noise_ref, top_ref, bottom_ref, top_sides_ref, bottom_sides_ref, sides_ref):
    for b in range(z.samples):
        for i in range(z.rows):
            value = jnp.concatenate([inputs_ref[b, i], jnp.transpose(noise_ref[b, i])], axis=1)
            side = jnp.concatenate([value[z.columns - LON_HALO :], value[:LON_HALO]], axis=0)
            sides_ref[b, i] = side
            if i < LAT_HALO:
                top_ref[b, i] = value
                top_sides_ref[b, i] = side
            if i >= z.rows - LAT_HALO:
                bottom_ref[b, i - z.rows + LAT_HALO] = value
                bottom_sides_ref[b, i - z.rows + LAT_HALO] = side


def cut(z, inputs, noise):
    shape = lambda rows, columns: jax.ShapeDtypeStruct((z.samples, rows, columns, z.joined), F32)
    rim, side = shape(LAT_HALO, z.columns), shape(LAT_HALO, 2 * LON_HALO)
    return pl.pallas_call(
        partial(cut_body, z),
        name="cut",
        out_shape=[rim, rim, side, side, shape(z.rows, 2 * LON_HALO)],
        compiler_params=params(60),
    )(inputs, noise)


def mix_body(z, info_ref, band_ref, inputs_ref, noise_ref, above_ref, below_ref, above_sides_ref, below_sides_ref, sides_ref, gain_ref, shift_ref, mixed_ref, other_ref, lhs, high, low):
    at_row = pl.program_id(0)
    gap = z.span - z.columns - 2 * LON_HALO

    def place(sample, at, value, sides, present, gain, shift):
        value = jnp.concatenate([sides[:LON_HALO], value, sides[LON_HALO:]], axis=0)
        channel = lax.broadcasted_iota(jnp.int32, (1, z.joined), 1)
        inside = channel < z.width
        mean = jnp.sum(jnp.where(inside, value, 0.0), axis=1, keepdims=True) / z.width
        centered = jnp.where(inside, value - mean, 0.0)
        variance = jnp.sum(centered * centered, axis=1, keepdims=True) / z.width
        normed = centered * lax.rsqrt(variance + EPSILON) * gain + shift
        value = jnp.where(inside, normed, value) * present
        value = jnp.concatenate([value, jnp.zeros((value.shape[0], z.wide - z.joined), F32)], axis=1)
        value = jnp.concatenate([value, jnp.zeros((gap, z.wide), F32)], axis=0)
        high_part, low_part = split(value)
        rows, lanes = slice(at * z.span, (at + 1) * z.span), slice(sample * z.wide, (sample + 1) * z.wide)
        high[rows, lanes] = high_part
        low[rows, lanes] = low_part

    @pl.when(at_row == 0)
    def _():
        fill = jnp.zeros((1, z.joined - z.width), F32)
        gain = jnp.concatenate([row(gain_ref), fill], axis=1)
        shift = jnp.concatenate([row(shift_ref), fill], axis=1)
        has_above = (info_ref[1] != 0).astype(F32)
        has_below = (info_ref[2] != 0).astype(F32)
        for b in range(z.samples):
            for i in range(LAT_HALO):
                place(b, i, above_ref[b, i], above_sides_ref[b, i], has_above, gain, shift)
                place(b, i + z.rows + LAT_HALO, below_ref[b, i], below_sides_ref[b, i], has_below, gain, shift)
            for i in range(z.rows):
                value = jnp.concatenate([inputs_ref[b, i], jnp.transpose(noise_ref[b, i])], axis=1)
                place(b, i + LAT_HALO, value, sides_ref[b, i], 1.0, gain, shift)

    for k in range(z.basis):
        value = band(band_ref[0, k : k + 1, :], z.columns)
        lhs[k * z.columns : (k + 1) * z.columns, :] = value.astype(BF16)

    rows = pl.ds(pl.multiple_of(at_row * z.span, 16), z.taps)
    top, rest = high[rows, :], low[rows, :]
    product = nn(lhs[:, : 3 * z.taps], jnp.concatenate([top, rest, top], axis=0))
    for b in range(z.samples):
        tail = jnp.zeros((z.columns, LANES), F32)
        for k in range(z.basis):
            part = product[k * z.columns : (k + 1) * z.columns, b * z.wide : (b + 1) * z.wide]
            mixed_ref[b, :, k * z.main : (k + 1) * z.main] = part[:, : z.main]
            last = part[:, z.main :]
            tail = tail + (last if k == 0 else pltpu.roll(last, z.extra * k, 1))
        mixed_ref[b, :, z.basis * z.main :] = tail

    @pl.when(info_ref[0] == 0)
    def _():
        other_ref[...] = mixed_ref[:, :, z.half :]

    @pl.when(info_ref[0] != 0)
    def _():
        other_ref[...] = mixed_ref[:, :, : z.half]


def mix(z, info, bands, inputs, noise, above, below, sides, gain, shift):
    height = (z.rows + 2 * LAT_HALO) * z.span
    lanes = bands.shape[2]
    arrays = [inputs, noise, above, below, *sides, gain, shift]
    mixed, other = pl.pallas_call(
        partial(mix_body, z),
        name="mix",
        grid_spec=pltpu.PrefetchScalarGridSpec(
            num_scalar_prefetch=1,
            grid=(z.rows,),
            in_specs=[
                pl.BlockSpec((1, z.basis, lanes), lambda r, *_: (r, 0, 0)),
                *(full(a.shape) for a in arrays),
            ],
            out_specs=[
                pl.BlockSpec((z.samples, z.columns, z.depth), lambda r, *_: (0, r, 0)),
                pl.BlockSpec((z.samples, z.columns, z.half), lambda r, *_: (0, r, 0)),
            ],
            scratch_shapes=[
                pltpu.VMEM((z.basis * z.columns, lanes), BF16),
                pltpu.VMEM((height, z.samples * z.wide), BF16),
                pltpu.VMEM((height, z.samples * z.wide), BF16),
            ],
        ),
        out_shape=[
            pltpu.HBM((z.samples, z.rows * z.columns, z.depth), F32),
            pltpu.HBM((z.samples, z.rows * z.columns, z.half), F32),
        ],
        compiler_params=params(34),
        cost_estimate=cost(z.pixels * z.basis * z.taps * z.joined, 8 * z.pixels * z.depth),
    )(info, bands, *arrays)
    return mixed.reshape(z.pixels, z.depth), other.reshape(z.pixels, z.half)


def conv_body(z, mixed_ref, tail_ref, weight_ref, base_ref, bias_ref, out_ref, tail_weight):
    step = pl.program_id(0)

    @pl.when(step == 0)
    def _():
        out_ref[...] = base_ref[...] + row(bias_ref)
        tail_weight[...] = jnp.zeros_like(tail_weight)

    out_ref[...] += nt(left(mixed_ref[...]), right_t(weight_ref[0, :, : z.main]))
    last = weight_ref[0, :, z.main :]
    last = jnp.concatenate([last, jnp.zeros((last.shape[0], LANES - z.extra), F32)], axis=1)
    tail_weight[...] += pltpu.roll(last, z.extra * step, 1)

    @pl.when(step == z.basis - 1)
    def _():
        out_ref[...] += nt(left(tail_ref[...]), right_t(tail_weight[...]))


def conv(z, mixed, weight, base, bias):
    return pl.pallas_call(
        partial(conv_body, z),
        name="conv",
        grid=(z.basis,),
        in_specs=[
            pl.BlockSpec((z.pixels, z.main), lambda k: (0, k)),
            pl.BlockSpec((z.pixels, LANES), lambda k: (0, z.basis * z.tiles)),
            pl.BlockSpec((1, z.width, z.joined), lambda k: (k, 0, 0)),
            full((z.pixels, z.width)),
            full(bias.shape),
        ],
        out_specs=result((z.pixels, z.width)),
        out_shape=jax.ShapeDtypeStruct((z.pixels, z.width), F32),
        scratch_shapes=[pltpu.VMEM((z.width, LANES), F32)],
        compiler_params=params(44),
        cost_estimate=cost(z.pixels * z.depth * z.width, 4 * z.depth * (z.width + z.pixels)),
    )(mixed, mixed, weight, base, bias)


def mlp_body(
    z,
    info_ref,
    middle_ref,
    cot_ref,
    d_active_ref,
    weight_ref,
    bias_ref,
    gain_ref,
    shift_ref,
    kept_ref,
    sent_ref,
    active_high_ref,
    active_low_ref,
    d_pre_high_ref,
    d_pre_low_ref,
    d_bias_ref,
    second_ref,
    second_lhs,
    second_t,
    cot_t,
    tail,
):
    step = pl.program_id(0)
    main = z.main

    @pl.when(step == 0)
    def _():
        norm, _ = normalize(middle_ref[...])
        second = norm * row(gain_ref) + row(shift_ref)
        second_ref[...] = second
        second_lhs[...] = left(second[:, :main])
        second_t[...] = left(padded_t(second, z.wide)[: z.high])
        cot_t[...] = left(padded_t(cot_ref[...], z.wide)[: z.high])

    def store(out_ref, which, value, last):
        if not last:
            for i in range(z.tiles):
                out_ref[0, i * z.high : (i + 1) * z.high, :] = value[:, i * LANES : (i + 1) * LANES]
            out_ref[0, z.tiles * z.high :, :] = tail[which, step - 1]
            return
        fill = jnp.zeros((z.wide - z.high, LANES), F32)
        value = jnp.transpose(jnp.concatenate([value, fill], axis=0))[:8]
        for i in range(z.parts):
            half, place = i // (z.parts // 2), i % (z.parts // 2)
            tail[which, half, 8 * place : 8 * place + 8, :] = value[:, i * LANES : (i + 1) * LANES]

    def body(width, last):
        weight = only(z, weight_ref[:, :width], last)
        start = z.steps * main if last else pl.multiple_of((step - 1) * main, LANES)
        bias = bias_ref[pl.ds(start, z.rest if last else width)]
        bias = bias.reshape(1, bias.shape[0])
        if last:
            bias = jnp.concatenate([bias, jnp.zeros((1, width - z.rest), F32)], axis=1)
        d_active = only(z, d_active_ref[:, :width], last)
        pre = nn(second_lhs[...], right(weight[:main]))
        pre = pre + second_ref[:, main : main + 1] * weight[main : main + 1] + bias
        cdf = 0.5 * (1.0 + lax.erf(pre * np.float32(0.5**0.5)))
        pdf = jnp.exp(pre * pre * -0.5) * np.float32(1.0 / np.sqrt(2.0 * np.pi))
        active = only(z, pre * cdf, last)
        d_pre = d_active * (cdf + pre * pdf)
        high, low = split(active)
        active_high_ref[:, :width] = high
        active_low_ref[:, :width] = low
        output_grad = nn(cot_t[...], jnp.concatenate([high, low, high], axis=0))
        high, low = split(d_pre)
        d_pre_high_ref[:, :width] = high
        d_pre_low_ref[:, :width] = low
        d_bias_ref[:, :width] = jnp.sum(d_pre, axis=0, keepdims=True)
        hidden_grad = nn(second_t[...], jnp.concatenate([high, low, high], axis=0))

        @pl.when(info_ref[0] == 0)
        def _():
            store(kept_ref, 0, output_grad, last)
            store(sent_ref, 1, hidden_grad, last)

        @pl.when(info_ref[0] != 0)
        def _():
            store(sent_ref, 0, output_grad, last)
            store(kept_ref, 1, hidden_grad, last)

    pl.when(step == 0)(lambda: body(LANES, True))
    pl.when(step > 0)(lambda: body(z.main, False))


def mlp(z, info, middle, cot, d_active, weight, bias, gain, shift):
    flat = (2, z.mlp_half, LANES)
    at = lambda i: jnp.where(i == 0, z.steps, i - 1)
    hidden = pl.BlockSpec((z.pixels, z.main), lambda i, *_: (0, at(i)))
    half = pl.BlockSpec((1, z.mlp_half, LANES), lambda i, *_: (jnp.maximum(i - 1, 0), 0, 0))
    wide = pltpu.HBM((z.pixels, z.hidden), BF16)
    return pl.pallas_call(
        partial(mlp_body, z),
        name="mlp",
        grid_spec=pltpu.PrefetchScalarGridSpec(
            num_scalar_prefetch=1,
            grid=(z.steps + 1,),
            in_specs=[
                full((z.pixels, z.width)),
                full((z.pixels, z.width)),
                hidden,
                pl.BlockSpec((z.width, z.main), lambda i, *_: (0, at(i))),
                full(bias.shape),
                full(gain.shape),
                full(shift.shape),
            ],
            out_specs=[
                half,
                half,
                hidden,
                hidden,
                hidden,
                hidden,
                pl.BlockSpec((1, z.main), lambda i, *_: (0, at(i))),
            ],
            scratch_shapes=[
                pltpu.VMEM((z.pixels, z.width), F32),
                pltpu.VMEM((z.pixels, 3 * z.main), BF16),
                pltpu.VMEM((z.high, 3 * z.pixels), BF16),
                pltpu.VMEM((z.high, 3 * z.pixels), BF16),
                pltpu.VMEM((2, z.steps, 8 * z.parts // 2, LANES), F32),
            ],
        ),
        out_shape=[
            pltpu.HBM(flat, F32),
            pltpu.HBM(flat, F32),
            wide,
            wide,
            wide,
            wide,
            jax.ShapeDtypeStruct((1, z.hidden), F32),
        ],
        compiler_params=params(44),
        cost_estimate=cost(3 * z.pixels * z.width * z.hidden, 12 * z.width * z.hidden),
    )(info, middle, cot, d_active, weight, bias, gain, shift)


def middle_back_body(z, high_ref, low_ref, weight_ref, middle_ref, cot_ref, gain_ref, out_ref, out_t_ref, sums_ref, d_second):
    step = pl.program_id(0)

    @pl.when(step == 0)
    def _():
        d_second[...] = jnp.zeros_like(d_second)

    def body(width, last):
        high = only(z, high_ref[:, :width], last)
        low = only(z, low_ref[:, :width], last)
        weight = right_t(only(z, weight_ref[:, :width], last))
        d_second[...] += nt(jnp.concatenate([high, high, low], axis=1), weight)

    hidden_steps(z, body)

    @pl.when(step == z.steps)
    def _():
        norm, inverse = normalize(middle_ref[...])
        grad = d_second[...]
        sums_ref[0:1, :] = jnp.sum(grad * norm, axis=0, keepdims=True)
        sums_ref[1:2, :] = jnp.sum(grad, axis=0, keepdims=True)
        cot = cot_ref[...]
        sums_ref[3:4, :] = jnp.sum(cot, axis=0, keepdims=True)
        d_middle = cot + norm_back(grad * row(gain_ref), norm, inverse)
        sums_ref[2:3, :] = jnp.sum(d_middle, axis=0, keepdims=True)
        out_ref[...] = d_middle
        out_t_ref[...] = padded_t(d_middle, z.wide)[: z.high]


def middle_back(z, high, low, weight, middle, cot, gain):
    hidden = pl.BlockSpec((z.pixels, z.main), lambda i: (0, i))
    return pl.pallas_call(
        partial(middle_back_body, z),
        name="middle_back",
        grid=(z.steps + 1,),
        in_specs=[
            hidden,
            hidden,
            pl.BlockSpec((z.width, z.main), lambda i: (0, i)),
            full((z.pixels, z.width)),
            full((z.pixels, z.width)),
            full(gain.shape),
        ],
        out_specs=[
            full((z.pixels, z.width)),
            full((z.high, z.pixels)),
            full((4, z.width)),
        ],
        out_shape=[
            jax.ShapeDtypeStruct((z.pixels, z.width), F32),
            jax.ShapeDtypeStruct((z.high, z.pixels), F32),
            jax.ShapeDtypeStruct((4, z.width), F32),
        ],
        scratch_shapes=[pltpu.VMEM((z.pixels, z.width), F32)],
        compiler_params=params(58),
        cost_estimate=cost(z.pixels * z.width * z.hidden, 8 * z.width * z.hidden),
    )(high, low, weight, middle, cot, gain)


def output_body(z, high_ref, low_ref, weight_ref, middle_ref, bias_ref, out_ref):
    @pl.when(pl.program_id(0) == 0)
    def _():
        out_ref[...] = middle_ref[...] + row(bias_ref)

    def body(width, last):
        high = only(z, high_ref[:, :width], last)
        low = only(z, low_ref[:, :width], last)
        weight = right_t(only(z, weight_ref[:, :width], last))
        out_ref[...] += nt(jnp.concatenate([high, high, low], axis=1), weight)

    hidden_steps(z, body)


def output(z, high, low, weight, middle, bias):
    hidden = pl.BlockSpec((z.pixels, z.main), lambda i: (0, i))
    return pl.pallas_call(
        partial(output_body, z),
        name="output",
        grid=(z.steps + 1,),
        in_specs=[
            hidden,
            hidden,
            pl.BlockSpec((z.width, z.main), lambda i: (0, i)),
            full((z.pixels, z.width)),
            full(bias.shape),
        ],
        out_specs=full((z.pixels, z.width)),
        out_shape=jax.ShapeDtypeStruct((z.pixels, z.width), F32),
        compiler_params=params(58),
        cost_estimate=cost(z.pixels * z.width * z.hidden, 8 * z.width * z.hidden),
    )(high, low, weight, middle, bias)


def conv_grad_body(z, info_ref, own_ref, far_ref, own_t_ref, far_t_ref, out_ref, lhs):
    step = pl.program_id(0)
    tiles = own_ref.shape[1] // LANES

    @pl.when(step == 0)
    def _():
        lhs[...] = left(jnp.concatenate([own_t_ref[...], far_t_ref[...]], axis=1))
        used = pl.num_programs(0) * tiles * z.high
        out_ref[used:, :] = jnp.zeros((out_ref.shape[0] - used, LANES), F32)

    value = nn(lhs[...], right(jnp.concatenate([own_ref[...], far_ref[...]], axis=0)))
    for i in range(tiles):
        rows = pl.ds(pl.multiple_of((step * tiles + i) * z.high, 8), z.high)
        out_ref[rows, :] = value[:, i * LANES : (i + 1) * LANES]


def conv_grad(z, info, mixed, far_mixed, own_t, far_t):
    count = z.half // LANES // 2
    tiles = 3
    steps = count // tiles
    flat = round_up(count * z.high, 32)
    return pl.pallas_call(
        partial(conv_grad_body, z),
        name="conv_grad",
        grid_spec=pltpu.PrefetchScalarGridSpec(
            num_scalar_prefetch=1,
            grid=(steps,),
            in_specs=[
                pl.BlockSpec((z.pixels, tiles * LANES), lambda i, c: (0, (2 * c[0] + c[1]) * steps + i)),
                pl.BlockSpec((z.pixels, tiles * LANES), lambda i, c: (0, c[1] * steps + i)),
                full((z.high, z.pixels)),
                full((z.high, z.pixels)),
            ],
            out_specs=full((flat, LANES)),
            scratch_shapes=[pltpu.VMEM((z.high, 6 * z.pixels), BF16)],
        ),
        out_shape=jax.ShapeDtypeStruct((flat, LANES), F32),
        compiler_params=params(50),
        cost_estimate=cost(2 * z.pixels * z.width * count * LANES, 12 * z.pixels * count * LANES),
    )(info, mixed, far_mixed, own_t, far_t)


def mixed_back_body(z, weight_ref, dm_ref, high_ref, low_ref, lhs):
    columns, main = z.columns, z.main

    @pl.when(pl.program_id(0) == 0)
    def _():
        lhs[...] = left(dm_ref[:, :main])

    value = nn(lhs[...], right(weight_ref[0, :main, :]))
    value = value + dm_ref[:, main : main + 1] * weight_ref[0, main : main + 1, :]
    value_high, value_low = split(value)
    for b in range(z.samples):
        for r in range(z.rows):
            i = (b * z.rows + r) * columns
            lane = b * z.wide
            high_ref[r, :, lane : lane + z.joined] = value_high[i : i + columns]
            low_ref[r, :, lane : lane + z.joined] = value_low[i : i + columns]


def mixed_back(z, weight, d_middle):
    out = pl.BlockSpec((z.rows, z.columns, z.samples * z.wide), lambda i: (0, i, 0))
    shape = pltpu.HBM((z.rows, z.basis * z.columns, z.samples * z.wide), BF16)
    return pl.pallas_call(
        partial(mixed_back_body, z),
        name="mixed_back",
        grid=(z.basis,),
        in_specs=[
            pl.BlockSpec((1, z.width, z.joined), lambda i: (i, 0, 0)),
            full((z.pixels, z.width)),
        ],
        out_specs=[out, out],
        out_shape=[shape, shape],
        scratch_shapes=[pltpu.VMEM((z.pixels, 3 * z.main), BF16)],
        compiler_params=params(56),
        cost_estimate=cost(z.pixels * z.depth * z.width, 4 * z.depth * z.width),
    )(weight, d_middle)


def outer_columns(z, value):
    return jnp.concatenate([value[z.columns + LON_HALO : z.columns + 2 * LON_HALO], value[:LON_HALO]], axis=0)


def band_back_body(z, high_ref, low_ref, band_ref, out_ref, top_ref, bottom_ref, sides_ref):
    row_at = pl.program_id(0)
    columns = z.columns

    @pl.when(row_at == 0)
    def _():
        out_ref[...] = jnp.zeros_like(out_ref)

    spread = [band(band_ref[0, k : k + 1, :], columns) for k in range(z.basis)]
    spread = jnp.transpose(jnp.concatenate(spread, axis=0))[: z.taps]
    high, low = split(spread)
    top, rest = high_ref[0], low_ref[0]
    value = nn(high, top) + nn(high, rest) + nn(low, top)
    place = pl.ds(pl.multiple_of(row_at * z.span, 8), z.taps)
    for b in range(z.samples):
        out_ref[b, place, :] += value[:, b * z.wide : b * z.wide + z.joined]

    @pl.when(row_at == z.rows - 1)
    def _():
        for b in range(z.samples):
            for r in range(z.rows + 2 * LAT_HALO):
                value = out_ref[b, r * z.span : r * z.span + columns + 2 * LON_HALO, :]
                if r < LAT_HALO:
                    top_ref[b, r] = value
                elif r < z.rows + LAT_HALO:
                    sides_ref[b, r - LAT_HALO] = outer_columns(z, value)
                else:
                    bottom_ref[b, r - z.rows - LAT_HALO] = value


def band_back(z, high, low, bands):
    lanes = bands.shape[2]
    height = (z.rows + 2 * LAT_HALO) * z.span
    rim = (z.samples, LAT_HALO, z.columns + 2 * LON_HALO, z.joined)
    shapes = [(z.samples, height, z.joined), rim, rim, (z.samples, z.rows, 2 * LON_HALO, z.joined)]
    part = pl.BlockSpec((1,) + high.shape[1:], lambda i: (i, 0, 0))
    return pl.pallas_call(
        partial(band_back_body, z),
        name="band_back",
        grid=(z.rows,),
        in_specs=[part, part, pl.BlockSpec((1, z.basis, lanes), lambda i: (i, 0, 0))],
        out_specs=[full(shape) for shape in shapes],
        out_shape=[jax.ShapeDtypeStruct(shape, F32) for shape in shapes],
        compiler_params=params(56),
        cost_estimate=cost(z.pixels * z.basis * z.taps * z.joined, 8 * z.pixels * z.depth),
    )(high, low, bands)


def edge_body(z, sides_ref, above_ref, below_ref, out_ref):
    for b in range(z.samples):
        for r in range(z.rows):
            value = sides_ref[b, r]
            if r < LAT_HALO:
                value = value + outer_columns(z, above_ref[b, r])
            if r >= z.rows - LAT_HALO:
                value = value + outer_columns(z, below_ref[b, r - z.rows + LAT_HALO])
            out_ref[b, r] = value


def edge(z, sides, above, below):
    return pl.pallas_call(
        partial(edge_body, z),
        name="edge",
        out_shape=jax.ShapeDtypeStruct(sides.shape, F32),
        compiler_params=params(16),
        cost_estimate=cost(2**30, 2**22),
    )(sides, above, below)


def finish_body(
    z, padded_ref, above_ref, below_ref, sides_ref, inputs_ref, d_middle_ref, gain_ref, sums_ref, d_bias_ref, out_ref, vectors_ref, own
):
    sample = pl.program_id(0)

    @pl.when(sample == 0)
    def _():
        own[...] = jnp.zeros_like(own)

    for r in range(z.rows):
        start = (r + LAT_HALO) * z.span
        value = padded_ref[0, start : start + z.columns + 2 * LON_HALO, :]
        if r < LAT_HALO:
            value = value + above_ref[0, r]
        if r >= z.rows - LAT_HALO:
            value = value + below_ref[0, r - z.rows + LAT_HALO]
        middle = value[2 * LON_HALO : z.columns]
        low = value[LON_HALO : 2 * LON_HALO] + sides_ref[0, r, :LON_HALO]
        high = value[z.columns : z.columns + LON_HALO] + sides_ref[0, r, LON_HALO:]
        grad = jnp.concatenate([low, middle, high], axis=0)[:, : z.width]
        norm, inverse = normalize(inputs_ref[0, r])
        own[0:1, :] += jnp.sum(grad * norm, axis=0, keepdims=True)
        own[1:2, :] += jnp.sum(grad, axis=0, keepdims=True)
        grad = norm_back(grad * row(gain_ref), norm, inverse)
        out_ref[0, r] = d_middle_ref[0, r] + grad

    @pl.when(sample == pl.num_programs(0) - 1)
    def _():
        vectors_ref[...] = jnp.zeros_like(vectors_ref)
        row = 0
        rows = [(sums_ref, 2), (own, 0), (own, 1), (sums_ref, 0), (sums_ref, 1), (d_bias_ref, 0), (sums_ref, 3)]
        for ref, at in rows:
            size = ref.shape[1]
            for i in range(0, size, LANES):
                end = min(i + LANES, size)
                vectors_ref[row : row + 1, : end - i] = ref[at : at + 1, i:end]
                row += 1


def finish(z, padded, above, below, sides, inputs, d_middle, gain, sums, d_bias):
    shape = (z.samples, z.rows, z.columns, z.width)
    count = round_up(6 * pl.cdiv(z.width, LANES) + pl.cdiv(z.hidden, LANES), 16)

    def part(array):
        size = array.shape[1:]
        return pl.BlockSpec((1,) + size, lambda b: (b,) + (0,) * len(size))

    d_middle = d_middle.reshape(shape)
    arrays = [padded, above, below, sides, inputs, d_middle]
    return pl.pallas_call(
        partial(finish_body, z),
        name="finish",
        grid=(z.samples,),
        in_specs=[part(a) for a in arrays] + [full(gain.shape), full(sums.shape), full(d_bias.shape)],
        out_specs=[part(inputs), full((count, LANES))],
        out_shape=[jax.ShapeDtypeStruct(shape, F32), jax.ShapeDtypeStruct((count, LANES), F32)],
        scratch_shapes=[pltpu.VMEM((8, z.width), F32)],
        compiler_params=params(60),
        cost_estimate=cost(2**30, 2**22),
    )(*arrays, gain, sums, d_bias)


def conv_place_body(z, which, first, count, info_ref, *refs):
    number = len(which)
    pieces, (out_ref, held, narrow, sems) = refs[:number], refs[-4:]
    main_tiles = z.basis * z.tiles
    with_extra = first + 2 * count == z.half // LANES
    used = count * z.high

    def get(i):
        return pltpu.make_async_copy(pieces[i].at[pl.ds(0, used), :], held.at[i], sems.at[i])

    def tile(i, t):
        return (info_ref[which[i]] // 2) * (z.half // LANES) + first + (info_ref[which[i]] % 2) * count + t

    def put(i, t):
        at = tile(i, t)
        lanes = pl.ds(pl.multiple_of(at % z.tiles * LANES, LANES), LANES)
        return pltpu.make_async_copy(
            held.at[i, pl.ds(t * z.high, z.width), :],
            out_ref.at[at // z.tiles, :, lanes],
            sems.at[number + i * count + t],
        )

    def put_extra(k):
        return pltpu.make_async_copy(
            narrow.at[k], out_ref.at[k, :, pl.ds(z.main, z.extra)], sems.at[number * (1 + count) + k]
        )

    for i in range(number):
        get(i).start()
    for i in range(number):
        get(i).wait()
        for t in range(count):
            is_main = tile(i, t) < main_tiles

            @pl.when(is_main)
            def _():
                put(i, t).start()

            if with_extra and t == count - 1:

                @pl.when(jnp.logical_not(is_main))
                def _():
                    for k in range(z.basis):
                        value = held[i, t * z.high : (t + 1) * z.high, :]
                        value = value if k == 0 else pltpu.roll(value, LANES - z.extra * k, 1)
                        narrow[k] = value[: z.width, : z.extra]
                        put_extra(k).start()

    for i in range(number):
        if with_extra:

            @pl.when(tile(i, count - 1) >= main_tiles)
            def _():
                for k in range(z.basis):
                    put_extra(k).wait()

        for t in range(count):

            @pl.when(tile(i, t) < main_tiles)
            def _():
                put(i, t).wait()


def conv_place(z, places, which, first, count, pieces, onto):
    anywhere = pl.BlockSpec(memory_space=pl.ANY)
    operands = [places, *pieces]
    aliases = {}
    if onto is not None:
        operands.append(onto)
        aliases = {1 + len(which): 0}
    return pl.pallas_call(
        partial(conv_place_body, z, which, first, count),
        name="conv_place",
        grid_spec=pltpu.PrefetchScalarGridSpec(
            num_scalar_prefetch=1,
            grid=(),
            in_specs=[anywhere] * (len(operands) - 1),
            out_specs=anywhere,
            scratch_shapes=[
                pltpu.VMEM((len(which), count * z.high, LANES), F32),
                pltpu.VMEM((z.basis, z.width, z.extra), F32),
                pltpu.SemaphoreType.DMA((len(which) * (1 + count) + z.basis,)),
            ],
        ),
        out_shape=jax.ShapeDtypeStruct((z.basis, z.width, z.joined), F32),
        input_output_aliases=aliases,
        compiler_params=params(16),
        cost_estimate=cost(2**30, 2**24),
    )(*operands)


def mlp_place_body(z, info_ref, own_ref, far_ref, output_ref, hidden_ref, held, narrow, sems):
    main_tiles = 2 * z.tiles

    def place(refs):
        gets = []
        for i, ref in enumerate(refs):
            for half in range(2):
                rows = pl.ds(half * z.mlp_half, z.mlp_half)
                gets.append(pltpu.make_async_copy(ref.at[rows, :], held.at[i, half], sems.at[2 * i + half]))
                gets[-1].start()
        puts = []
        for i, out_ref in enumerate((output_ref, hidden_ref)):
            for t in range(main_tiles):
                half = t // z.tiles
                if t % z.tiles == 0:
                    gets[2 * i + half].wait()
                puts.append(
                    pltpu.make_async_copy(
                        held.at[i, half, pl.ds(t % z.tiles * z.high, z.width), :],
                        out_ref.at[:, pl.ds(t * LANES, LANES)],
                        sems.at[8 + i * main_tiles + t],
                    )
                )
                puts[-1].start()
            start = z.tiles * z.high
            parts = [
                held[i, half, start + 8 * j : start + 8 * j + 8, :] for half in range(2) for j in range(z.parts // 2)
            ]
            value = jnp.concatenate([jnp.concatenate(parts, axis=1)] * (LANES // 8), axis=0)
            narrow[i] = jnp.transpose(value)[: z.width, : z.rest]
            puts.append(
                pltpu.make_async_copy(
                    narrow.at[i],
                    out_ref.at[:, pl.ds(main_tiles * LANES, z.rest)],
                    sems.at[8 + 2 * main_tiles + i],
                )
            )
            puts[-1].start()
        for c in puts:
            c.wait()

    pl.when(info_ref[0] == 0)(lambda: place((own_ref, far_ref)))
    pl.when(info_ref[0] != 0)(lambda: place((far_ref, own_ref)))


def mlp_place(z, info, own, far):
    shape = jax.ShapeDtypeStruct((z.width, z.hidden), F32)
    anywhere = pl.BlockSpec(memory_space=pl.ANY)
    return pl.pallas_call(
        partial(mlp_place_body, z),
        name="mlp_place",
        grid_spec=pltpu.PrefetchScalarGridSpec(
            num_scalar_prefetch=1,
            grid=(),
            in_specs=[anywhere, anywhere],
            out_specs=[anywhere, anywhere],
            scratch_shapes=[
                pltpu.VMEM((2, 2, z.mlp_half, LANES), F32),
                pltpu.VMEM((2, z.width, z.rest), F32),
                pltpu.SemaphoreType.DMA((4 * z.tiles + 10,)),
            ],
        ),
        out_shape=[shape, shape],
        compiler_params=params(16),
        cost_estimate=cost(2**30, 2**22),
    )(info, own, far)


def axis_size(axes):
    size = 1
    for axis in axes:
        size *= lax.axis_size(axis)
    return size


def pairs(lats, lons, target):
    found = []
    for lat in range(lats):
        for lon in range(lons):
            to_lat, to_lon = target(lat, lon)
            found.append((lat * lons + lon, to_lat * lons + to_lon))
    return found


class GridSum:
    def __init__(self):
        lats, lons = axis_size(LAT), axis_size(LON)
        lat, lon = lax.axis_index(LAT), lax.axis_index(LON)
        over = partial(pairs, lats, lons)
        self.core = lat % 2
        self.cores = over(lambda a, o: (a ^ 1, o))
        self.first = over(lambda a, o: (a ^ 2, o) if a % 2 else (a, o ^ 1))
        self.second = over(lambda a, o: (a, o ^ 1) if a % 2 else (a ^ 2, o))
        self.third = over(lambda a, o: (a ^ 4, o))
        lon_bit, lat_bit = lon % 2, lat // 2 % 2
        self.first_bit = jnp.where(self.core == 0, lon_bit, lat_bit)
        self.second_bit = jnp.where(self.core == 0, lat_bit, lon_bit)
        self.third_bit = lat // 4 % 2
        far_bit = jnp.where(self.core == 0, lat_bit, lon_bit)
        mine, other = 2 * self.core, 2 * (1 - self.core)
        self.places = jnp.stack(
            [mine + self.first_bit, mine + 1 - self.first_bit, other + far_bit, other + 1 - far_bit]
        ).astype(jnp.int32)
        self.others = []
        bit = 8
        while bit < lats:
            self.others.append(over(lambda a, o, bit=bit: (a ^ bit, o)))
            bit *= 2
        bit = 2
        while bit < lons:
            self.others.append(over(lambda a, o, bit=bit: (a, o ^ bit)))
            bit *= 2

    def swap(self, value, where):
        return lax.ppermute(value, AXES, where)

    def all(self, value, where):
        return value + self.swap(value, where)


class Order:
    def __init__(self):
        self.last = ()
        self.held = True

    def use(self, value):
        if not self.held:
            return value
        value, self.last = lax.optimization_barrier((value, self.last))
        return value

    def mark(self, value):
        if self.held:
            self.last = (value,)
        return value

    def wait(self, value):
        return self.mark(self.use(value))

    def run(self, function, *values):
        return self.mark(function(*self.use(values)))


def sum_rows(size, index, arrays, vectors):
    count = 0 if vectors is None else vectors.shape[0]

    def body(index_ref, *refs):
        out_ref = refs[-1]
        total = refs[0][...]
        for ref in refs[1 : len(arrays)]:
            total = total + ref[...]
        out_ref[:size, :] = total
        if vectors is not None:
            out_ref[size:, :] = refs[len(arrays)][...]

    more = [] if vectors is None else [vectors]
    blocks = [pl.BlockSpec((size, LANES), lambda g, p, i=i: (p[i], 0)) for i in range(len(arrays))]
    return pl.pallas_call(
        body,
        name="sum_rows",
        grid_spec=pltpu.PrefetchScalarGridSpec(
            num_scalar_prefetch=1,
            grid=(1,),
            in_specs=blocks + [full(v.shape) for v in more],
            out_specs=full((size + count, LANES)),
        ),
        out_shape=jax.ShapeDtypeStruct((size + count, LANES), F32),
        compiler_params=params(16),
        cost_estimate=cost(2**30, 2**24),
    )(index, *arrays, *more)


def join_rows(size, bit, value, far):
    rows = value.shape[0] + size

    def body(bit_ref, value_ref, far_ref, out_ref):
        at = bit_ref[0]
        out_ref[pl.ds(pl.multiple_of(at * size, 8), size), :] = value_ref[:size, :]
        out_ref[pl.ds(pl.multiple_of((1 - at) * size, 8), size), :] = far_ref[:size, :]
        if rows > 2 * size:
            out_ref[2 * size :, :] = value_ref[size:, :] + far_ref[size:, :]

    return pl.pallas_call(
        body,
        name="join_rows",
        grid_spec=pltpu.PrefetchScalarGridSpec(
            num_scalar_prefetch=1,
            grid=(1,),
            in_specs=[full(value.shape), full(far.shape)],
            out_specs=full((rows, LANES)),
        ),
        out_shape=jax.ShapeDtypeStruct((rows, LANES), F32),
        compiler_params=params(16),
        cost_estimate=cost(2**30, 2**21),
    )(bit.reshape(1).astype(jnp.int32), value, far)


def add_rows(value, far, start=0):
    def body(value_ref, far_ref, out_ref):
        out_ref[...] = value_ref[...] + far_ref[start:, :]

    return pl.pallas_call(
        body,
        name="add_rows",
        out_shape=jax.ShapeDtypeStruct(value.shape, F32),
        compiler_params=params(16),
        cost_estimate=cost(2**30, 2**24),
    )(value, far)


def sum_tails(start, arrays):
    rows = arrays[0].shape[0] - start
    blocks = start % rows == 0

    def body(*refs):
        total = 0.0
        for ref in refs[:-1]:
            total = total + (ref[...] if blocks else ref[start:, :])
        refs[-1][...] = total

    spec = pl.BlockSpec((rows, LANES), lambda i: (start // rows, 0)) if blocks else full(arrays[0].shape)
    return pl.pallas_call(
        body,
        name="sum_tails",
        grid=(1,),
        in_specs=[spec] * len(arrays),
        out_specs=full((rows, LANES)),
        out_shape=jax.ShapeDtypeStruct((rows, LANES), F32),
        compiler_params=params(24),
        cost_estimate=cost(2**30, 2**22),
    )(*arrays)


class Chunk:
    def __init__(self, total, order, name, sent, kept):
        self.total, self.order, self.name = total, order, name
        self.terms, self.size = [(kept, 0)], sent.shape[0]
        self.vectors = None
        self.send("scatter_first", order.wait(sent), total.first)

    def send(self, step, value, where):
        with jax.named_scope(f"{self.name}_{step}"):
            self.value, self.far = value, self.total.swap(value, where)

    def take(self, index):
        arrays = [value for value, _ in self.terms]
        at = jnp.stack([jnp.asarray(index(at), jnp.int32) for _, at in self.terms])
        return self.order.run(partial(sum_rows, self.size), at, arrays, None)

    def halve(self, step, where, bit):
        self.terms.append((self.far, 0))
        self.size //= 2
        sent = self.take(lambda at: 2 * at + 1 - bit)
        self.terms = [(value, 2 * at + bit) for value, at in self.terms]
        self.send(step, sent, where)

    def join(self, bit):
        self.value = self.order.run(partial(join_rows, self.size), bit, self.value, self.far)
        self.size *= 2

    def scatter_second(self):
        self.halve("scatter_second", self.total.second, self.total.second_bit)

    def across_first(self):
        self.halve("across_first", self.total.third, self.total.third_bit)

    def across_second(self):
        self.terms.append((self.far, 0))
        self.value = self.take(lambda at: at)
        for where in self.total.others[:-1]:
            self.send("across", self.value, where)
            self.value = self.order.run(add_rows, self.value, self.far)
        self.send("across_second", self.value, self.total.others[-1])

    def across_third(self):
        both = [self.value, self.far]
        value = self.order.run(partial(sum_rows, self.size), jnp.zeros((2,), jnp.int32), both, self.vectors)
        self.send("across_third", value, self.total.third)

    def gather_second(self):
        self.join(self.total.third_bit)
        self.send("gather_second", self.value, self.total.second)

    def gather_first(self):
        self.join(self.total.second_bit)
        self.send("gather_first", self.value, self.total.first)
        with jax.named_scope(f"{self.name}_near_core"):
            self.near = self.total.swap(self.value, self.total.cores)

    def gather_whole(self):
        self.join(self.total.first_bit)
        with jax.named_scope(f"{self.name}_near_core"):
            self.near = self.total.swap(self.value, self.total.cores)

    def gather_core(self):
        self.far = self.order.wait(self.far)
        with jax.named_scope(f"{self.name}_gather_core"):
            self.last = self.total.swap(self.far, self.total.cores)

    def pieces(self):
        return self.value, self.far, self.near, self.last


def after(value, *others):
    return lax.optimization_barrier((value, others))[0]


def rows_of(vector):
    size = round_up(vector.shape[0], LANES)
    return jnp.pad(vector, (0, size - vector.shape[0])).reshape(-1, LANES)


def moved(value, axis, steps, cycle):
    count = axis_size(axis)
    if cycle:
        where = [(i, (i + steps) % count) for i in range(count)]
    else:
        where = [(i, i + steps) for i in range(max(0, -steps), min(count, count - steps))]
    return lax.ppermute(value, axis, where)


def edges(sides, down):
    lats, lons = axis_size(LAT), axis_size(LON)

    def shifted(value, steps):
        where = [
            (lat * lons + lon, (lat + down) * lons + (lon + steps) % lons)
            for lat in range(max(0, -down), min(lats, lats - down))
            for lon in range(lons)
        ]
        return lax.ppermute(value, AXES, where)

    if lons == 2:
        return shifted(sides, 1)
    return jnp.concatenate([shifted(sides[:, :, :LON_HALO], 1), shifted(sides[:, :, LON_HALO:], -1)], axis=2)


def local(
    inputs,
    noise_field,
    basis_values,
    row_reach,
    conv_weight,
    conv_bias,
    first_gain,
    first_shift,
    second_gain,
    second_shift,
    hidden_weight,
    hidden_bias,
    output_weight,
    output_bias,
    cotangent,
):
    z = Sizes(inputs, noise_field, conv_weight, hidden_weight)
    total = GridSum()
    lat, lats = lax.axis_index(LAT), axis_size(LAT)
    info = jnp.stack([total.core, (lat > 0).astype(jnp.int32), (lat < lats - 1).astype(jnp.int32)])
    rows, columns, width = z.rows, z.columns, z.width
    flat = (z.pixels, width)
    cot = cotangent.reshape(flat)
    conv_weight = jnp.transpose(conv_weight, (0, 2, 1))
    output_weight = jnp.transpose(output_weight)

    noise = jnp.transpose(noise_field, (0, 1, 3, 2))
    top, bottom, top_sides, bottom_sides, sides = cut(z, inputs, noise)
    below, above = moved(top, LAT, -1, False), moved(bottom, LAT, 1, False)
    d_active = active_back(z, cot, output_weight)
    bottom_sides, top_sides, sides = after((bottom_sides, top_sides, sides), d_active)
    sides = [edges(bottom_sides, 1), edges(top_sides, -1), edges(sides, 0)]
    bands, plain_bands = band_rows(z, basis_values, row_reach)
    above, below, sides = after((above, below, sides), d_active)
    mixed, other = mix(z, info, bands, inputs, noise, above, below, sides, first_gain, first_shift)
    far_mixed = total.swap(other, total.cores)
    middle = conv(z, mixed, conv_weight, inputs.reshape(flat), conv_bias)
    kept, sent, active_high, active_low, d_pre_high, d_pre_low, d_hidden_bias = mlp(
        z, info, middle, cot, d_active, hidden_weight, hidden_bias, second_gain, second_shift
    )
    order = Order()
    arrived = total.swap(sent, total.cores)

    d_middle, d_middle_t, sums = order.run(
        partial(middle_back, z), d_pre_high, d_pre_low, hidden_weight, middle, cot, second_gain
    )
    far_t = total.swap(d_middle_t, total.cores)

    bit = total.first_bit
    kept, arrived = kept.reshape(-1, LANES), arrived.reshape(-1, LANES)
    add_half = lambda k, r, w: sum_rows(z.mlp_half, jnp.stack([w, w]).astype(jnp.int32), [k, r], None)
    m = Chunk(total, order, "m", order.run(add_half, kept, arrived, 1 - bit), None)
    m.terms = [(kept, bit), (arrived, bit)]
    half = lambda which: order.run(
        lambda *v: conv_grad(z, jnp.stack([total.core, which]), *v), mixed, far_mixed, d_middle_t, far_t
    )
    c = Chunk(total, order, "c", half(1 - bit), None)
    c.terms = [(half(bit), 0)]
    m.scatter_second()
    d_mixed = order.run(partial(mixed_back, z), conv_weight, d_middle)
    m.across_first()
    c.scatter_second()
    m.across_second()
    d_padded, top, bottom, sides = order.run(partial(band_back, z), *d_mixed, plain_bands)
    c.across_first()
    m.across_third()
    top, bottom = order.wait((top, bottom))
    from_below = moved(top, LAT, -1, False)
    from_above = moved(bottom, LAT, 1, False)
    block_output = order.run(
        partial(output, z), active_high, active_low, output_weight, middle, output_bias
    )
    m.gather_second()
    c.across_second()
    outer = order.run(partial(edge, z), sides, from_above, from_below)
    from_sides = edges(outer, 0)
    input_grad, vectors = order.run(
        partial(finish, z), d_padded, from_above, from_below, from_sides, inputs, d_middle, first_gain, sums, d_hidden_bias
    )

    c.vectors = vectors
    c.across_third()
    m.gather_first()
    c.gather_second()
    m.gather_whole()
    c.gather_first()
    place = partial(conv_place, z, total.places)
    count = z.half // LANES // 2
    conv_weight_grad = order.run(lambda *v: place((0, 2), 0, count, v, None), c.value, c.near)
    output_weight_grad, hidden_weight_grad = order.run(lambda *v: mlp_place(z, info, *v), m.value, m.near)
    c.gather_core()
    place_far = lambda *v: place((1,), 0, count, v[:1], v[1])
    place_last = lambda *v: place((3,), 0, count, v[:1], v[1])
    conv_weight_grad = order.run(place_far, c.far, conv_weight_grad)
    vectors = order.run(lambda *v: sum_tails(c.size, v), *c.pieces())
    far_vectors = total.swap(vectors, total.others[0])
    conv_weight_grad = order.run(place_last, c.last, conv_weight_grad)
    vectors = order.run(add_rows, vectors, far_vectors)
    for where in total.others[1:]:
        vectors = order.run(add_rows, vectors, total.swap(vectors, where))
    found, start = [], 0
    for size in (width,) * 5 + (z.hidden, width):
        count = pl.cdiv(size, LANES)
        found.append(vectors[start : start + count].reshape(-1)[:size])
        start += count
    conv_weight_grad = jnp.transpose(conv_weight_grad, (0, 2, 1))
    output_weight_grad = jnp.transpose(output_weight_grad)
    conv_bias_grad, first_gain_grad, first_shift_grad, second_gain_grad, second_shift_grad = found[:5]
    hidden_bias_grad, output_bias_grad = found[5:]
    return (
        block_output.reshape(inputs.shape),
        input_grad,
        conv_weight_grad,
        conv_bias_grad,
        first_gain_grad,
        first_shift_grad,
        second_gain_grad,
        second_shift_grad,
        hidden_weight_grad,
        hidden_bias_grad,
        output_weight_grad,
        output_bias_grad,
    )


def solution(mesh):
    lats, lons = mesh.shape["lat"], mesh.shape["lon"]
    fine = Mesh(mesh.devices.reshape(lats // 4, 2, 2, lons // 2, 2), AXES)
    grid = P(None, LAT, LON, None)
    weights = (P(),) * 10
    in_specs = (grid, grid, P(LAT, None, None, None), P(LAT)) + weights + (grid,)
    out_specs = (grid, grid) + weights
    return jax.shard_map(local, mesh=fine, in_specs=in_specs, out_specs=out_specs, check_vma=False)
```

```python
from functools import partial

import jax
import jax.numpy as jnp
import numpy as np
from jax import lax
from jax.experimental import pallas as pl
from jax.experimental.pallas import tpu as pltpu
from jax.sharding import Mesh, PartitionSpec as P

LAT_HALO = 2
LON_HALO = 4
EPSILON = 1e-05
F32 = jnp.float32
BF16 = jnp.bfloat16
LAT = ("z", "y", "core")
LON = ("w", "x")
AXES = LAT + LON
LANES = 128
STEP = 256


def split(value):
    high = value.astype(BF16)
    return high, (value - high.astype(F32)).astype(BF16)


def left(value):
    high, low = split(value)
    return jnp.concatenate([high, high, low], axis=1)


def right(value):
    high, low = split(value)
    return jnp.concatenate([high, low, high], axis=0)


def right_t(value):
    high, low = split(value)
    return jnp.concatenate([high, low, high], axis=1)


def nn(a, b):
    return lax.dot_general(a, b, (((1,), (0,)), ((), ())), preferred_element_type=F32)


def nt(a, b):
    return lax.dot_general(a, b, (((1,), (1,)), ((), ())), preferred_element_type=F32)


def params(megabytes=30):
    return pltpu.CompilerParams(vmem_limit_bytes=megabytes * 1024 * 1024)


def cost(macs, moved):
    return pl.CostEstimate(flops=12 * macs, bytes_accessed=moved, transcendentals=0)


def full(shape):
    return pl.BlockSpec(shape, lambda *_: (0,) * len(shape), pipeline_mode=pl.Buffered(1))


def result(shape):
    return pl.BlockSpec(shape, lambda *_: (0,) * len(shape))


def row(ref):
    return ref[...].reshape(1, ref.shape[0])


def round_up(value, to):
    return -(-value // to) * to


def normalize(field):
    average = jnp.mean(field, axis=-1, keepdims=True)
    centered = field - average
    variance = jnp.mean(centered * centered, axis=-1, keepdims=True)
    inverse = lax.rsqrt(variance + EPSILON)
    return centered * inverse, inverse


def norm_back(grad_norm, normalized, inverse):
    first_term = jnp.mean(grad_norm, axis=-1, keepdims=True)
    second_term = jnp.mean(grad_norm * normalized, axis=-1, keepdims=True)
    return inverse * (grad_norm - first_term - normalized * second_term)


def padded_t(value, size):
    return jnp.transpose(
        jnp.concatenate(
            [value, jnp.zeros((value.shape[0], size - value.shape[1]), value.dtype)], axis=1
        )
    )


class Sizes:
    def __init__(self, inputs, noise_field, conv_weight, hidden_weight):
        self.samples, self.rows, self.columns, self.width = inputs.shape
        self.joined = self.width + noise_field.shape[-1]
        self.basis = conv_weight.shape[0]
        self.hidden = hidden_weight.shape[1]
        self.pixels = self.samples * self.rows * self.columns
        self.main = self.width // LANES * LANES
        self.tiles = self.main // LANES
        self.extra = self.joined - self.main
        self.span = round_up(self.columns + 2 * LON_HALO, 16)
        self.taps = (2 * LAT_HALO + 1) * self.span
        self.depth = self.basis * self.main + LANES
        self.half = self.depth // 2
        self.wide = self.main + LANES
        self.high = round_up(self.width, 8)
        self.steps = self.hidden // self.main
        self.rest = self.hidden - self.steps * self.main
        self.parts = self.wide // LANES
        self.mlp_half = self.tiles * self.high + 8 * self.parts // 2


def hidden_steps(z, body):
    step = pl.program_id(0)
    pl.when(step < z.steps)(lambda: body(z.main, False))
    pl.when(step == z.steps)(lambda: body(LANES, True))


def only(z, value, last):
    if not last:
        return value
    valid = lax.broadcasted_iota(jnp.int32, (1, LANES), 1) < z.rest
    return jnp.where(valid, value.astype(F32), 0.0).astype(value.dtype)


def active_back_body(z, cot_ref, weight_ref, out_ref, lhs):
    main = z.main

    @pl.when(pl.program_id(0) == 0)
    def _():
        lhs[...] = left(cot_ref[:, :main])

    def body(width, last):
        product = nn(lhs[...], right(weight_ref[:main, :width]))
        out_ref[:, :width] = product + cot_ref[:, main : main + 1] * weight_ref[main : main + 1, :width]

    hidden_steps(z, body)


def active_back(z, cot, weight):
    return pl.pallas_call(
        partial(active_back_body, z),
        name="active_back",
        grid=(z.steps + 1,),
        in_specs=[
            full((z.pixels, z.width)),
            pl.BlockSpec((z.width, z.main), lambda i: (0, i)),
        ],
        out_specs=pl.BlockSpec((z.pixels, z.main), lambda i: (0, i)),
        out_shape=pltpu.HBM((z.pixels, z.hidden), F32),
        scratch_shapes=[pltpu.VMEM((z.pixels, 3 * z.main), BF16)],
        compiler_params=params(60),
        cost_estimate=cost(z.pixels * z.width * z.hidden, 8 * z.width * z.hidden),
    )(cot, weight)


def band_rows_body(z, reach_ref, basis_ref, stacked_ref, plain_ref):
    width = 2 * LON_HALO + 1
    height = 2 * LAT_HALO + 1
    offset = lax.broadcasted_iota(jnp.int32, (1, height * width), 1) % width - LON_HALO
    row_at = lax.broadcasted_iota(jnp.int32, (z.rows, 1), 0)
    reach = jnp.zeros((z.rows, 1), jnp.int32)
    for r in range(z.rows):
        reach = jnp.where(row_at == r, reach_ref[r], reach)
    values = [
        jnp.where(
            jnp.abs(offset) <= reach, jnp.concatenate([basis_ref[k, a] for a in range(height)], axis=1), 0.0
        )
        for k in range(z.basis)
    ]
    values = jnp.concatenate(values, axis=0)
    source = lax.broadcasted_iota(jnp.int32, (values.shape[1], z.taps), 0)
    target = lax.broadcasted_iota(jnp.int32, (values.shape[1], z.taps), 1)
    place = source // width * z.span + source % width
    onehot = (place == target).astype(BF16)
    high = values.astype(BF16)
    rest = values - high.astype(F32)
    low = rest.astype(BF16)
    last = (rest - low.astype(F32)).astype(BF16)
    high, low, last = nn(high, onehot), nn(low, onehot), nn(last, onehot)
    rest = low + last
    fill = jnp.zeros((values.shape[0], stacked_ref.shape[2] - 3 * z.taps), F32)
    stacked = jnp.concatenate([high, high, rest, fill], axis=1)
    fill = jnp.zeros((values.shape[0], plain_ref.shape[2] - z.taps), F32)
    plain = jnp.concatenate([high + rest, fill], axis=1)
    for r in range(z.rows):
        for k in range(z.basis):
            at = k * z.rows + r
            stacked_ref[r, k : k + 1, :] = stacked[at : at + 1]
            plain_ref[r, k : k + 1, :] = plain[at : at + 1]


def band_rows(z, basis_values, row_reach):
    flat = jnp.transpose(basis_values, (1, 2, 0, 3))
    shapes = [(z.rows, z.basis, round_up(3 * z.taps, LANES)), (z.rows, z.basis, round_up(z.taps, LANES))]
    return pl.pallas_call(
        partial(band_rows_body, z),
        name="band_rows",
        grid_spec=pltpu.PrefetchScalarGridSpec(
            num_scalar_prefetch=1,
            grid=(1,),
            in_specs=[full(flat.shape)],
            out_specs=[full(shape) for shape in shapes],
        ),
        out_shape=[jax.ShapeDtypeStruct(shape, F32) for shape in shapes],
        compiler_params=params(16),
    )(row_reach, flat)


def band(row, columns):
    spread = jnp.broadcast_to(row, (columns, row.shape[1]))
    return pltpu.roll(spread, 0, 1, stride=1, stride_axis=0)


def cut_body(z, inputs_ref, noise_ref, top_ref, bottom_ref, top_sides_ref, bottom_sides_ref, sides_ref):
    for b in range(z.samples):
        for i in range(z.rows):
            value = jnp.concatenate([inputs_ref[b, i], jnp.transpose(noise_ref[b, i])], axis=1)
            side = jnp.concatenate([value[z.columns - LON_HALO :], value[:LON_HALO]], axis=0)
            sides_ref[b, i] = side
            if i < LAT_HALO:
                top_ref[b, i] = value
                top_sides_ref[b, i] = side
            if i >= z.rows - LAT_HALO:
                bottom_ref[b, i - z.rows + LAT_HALO] = value
                bottom_sides_ref[b, i - z.rows + LAT_HALO] = side


def cut(z, inputs, noise):
    shape = lambda rows, columns: jax.ShapeDtypeStruct((z.samples, rows, columns, z.joined), F32)
    rim, side = shape(LAT_HALO, z.columns), shape(LAT_HALO, 2 * LON_HALO)
    return pl.pallas_call(
        partial(cut_body, z),
        name="cut",
        out_shape=[rim, rim, side, side, shape(z.rows, 2 * LON_HALO)],
        compiler_params=params(60),
    )(inputs, noise)


def mix_body(z, info_ref, band_ref, inputs_ref, noise_ref, above_ref, below_ref, above_sides_ref, below_sides_ref, sides_ref, gain_ref, shift_ref, mixed_ref, other_ref, lhs, high, low):
    at_row = pl.program_id(0)
    gap = z.span - z.columns - 2 * LON_HALO

    def place(sample, at, value, sides, present, gain, shift):
        value = jnp.concatenate([sides[:LON_HALO], value, sides[LON_HALO:]], axis=0)
        channel = lax.broadcasted_iota(jnp.int32, (1, z.joined), 1)
        inside = channel < z.width
        mean = jnp.sum(jnp.where(inside, value, 0.0), axis=1, keepdims=True) / z.width
        centered = jnp.where(inside, value - mean, 0.0)
        variance = jnp.sum(centered * centered, axis=1, keepdims=True) / z.width
        normed = centered * lax.rsqrt(variance + EPSILON) * gain + shift
        value = jnp.where(inside, normed, value) * present
        value = jnp.concatenate([value, jnp.zeros((value.shape[0], z.wide - z.joined), F32)], axis=1)
        value = jnp.concatenate([value, jnp.zeros((gap, z.wide), F32)], axis=0)
        high_part, low_part = split(value)
        rows, lanes = slice(at * z.span, (at + 1) * z.span), slice(sample * z.wide, (sample + 1) * z.wide)
        high[rows, lanes] = high_part
        low[rows, lanes] = low_part

    @pl.when(at_row == 0)
    def _():
        fill = jnp.zeros((1, z.joined - z.width), F32)
        gain = jnp.concatenate([row(gain_ref), fill], axis=1)
        shift = jnp.concatenate([row(shift_ref), fill], axis=1)
        has_above = (info_ref[1] != 0).astype(F32)
        has_below = (info_ref[2] != 0).astype(F32)
        for b in range(z.samples):
            for i in range(LAT_HALO):
                place(b, i, above_ref[b, i], above_sides_ref[b, i], has_above, gain, shift)
                place(b, i + z.rows + LAT_HALO, below_ref[b, i], below_sides_ref[b, i], has_below, gain, shift)
            for i in range(z.rows):
                value = jnp.concatenate([inputs_ref[b, i], jnp.transpose(noise_ref[b, i])], axis=1)
                place(b, i + LAT_HALO, value, sides_ref[b, i], 1.0, gain, shift)

    for k in range(z.basis):
        value = band(band_ref[0, k : k + 1, :], z.columns)
        lhs[k * z.columns : (k + 1) * z.columns, :] = value.astype(BF16)

    rows = pl.ds(pl.multiple_of(at_row * z.span, 16), z.taps)
    top, rest = high[rows, :], low[rows, :]
    product = nn(lhs[:, : 3 * z.taps], jnp.concatenate([top, rest, top], axis=0))
    for b in range(z.samples):
        tail = jnp.zeros((z.columns, LANES), F32)
        for k in range(z.basis):
            part = product[k * z.columns : (k + 1) * z.columns, b * z.wide : (b + 1) * z.wide]
            mixed_ref[b, :, k * z.main : (k + 1) * z.main] = part[:, : z.main]
            last = part[:, z.main :]
            tail = tail + (last if k == 0 else pltpu.roll(last, z.extra * k, 1))
        mixed_ref[b, :, z.basis * z.main :] = tail

    @pl.when(info_ref[0] == 0)
    def _():
        other_ref[...] = mixed_ref[:, :, z.half :]

    @pl.when(info_ref[0] != 0)
    def _():
        other_ref[...] = mixed_ref[:, :, : z.half]


def mix(z, info, bands, inputs, noise, above, below, sides, gain, shift):
    height = (z.rows + 2 * LAT_HALO) * z.span
    lanes = bands.shape[2]
    arrays = [inputs, noise, above, below, *sides, gain, shift]
    mixed, other = pl.pallas_call(
        partial(mix_body, z),
        name="mix",
        grid_spec=pltpu.PrefetchScalarGridSpec(
            num_scalar_prefetch=1,
            grid=(z.rows,),
            in_specs=[
                pl.BlockSpec((1, z.basis, lanes), lambda r, *_: (r, 0, 0)),
                *(full(a.shape) for a in arrays),
            ],
            out_specs=[
                pl.BlockSpec((z.samples, z.columns, z.depth), lambda r, *_: (0, r, 0)),
                pl.BlockSpec((z.samples, z.columns, z.half), lambda r, *_: (0, r, 0)),
            ],
            scratch_shapes=[
                pltpu.VMEM((z.basis * z.columns, lanes), BF16),
                pltpu.VMEM((height, z.samples * z.wide), BF16),
                pltpu.VMEM((height, z.samples * z.wide), BF16),
            ],
        ),
        out_shape=[
            pltpu.HBM((z.samples, z.rows * z.columns, z.depth), F32),
            pltpu.HBM((z.samples, z.rows * z.columns, z.half), F32),
        ],
        compiler_params=params(34),
        cost_estimate=cost(z.pixels * z.basis * z.taps * z.joined, 8 * z.pixels * z.depth),
    )(info, bands, *arrays)
    return mixed.reshape(z.pixels, z.depth), other.reshape(z.pixels, z.half)


def conv_body(z, mixed_ref, tail_ref, weight_ref, base_ref, bias_ref, out_ref, tail_weight):
    step = pl.program_id(0)

    @pl.when(step == 0)
    def _():
        out_ref[...] = base_ref[...] + row(bias_ref)
        tail_weight[...] = jnp.zeros_like(tail_weight)

    out_ref[...] += nt(left(mixed_ref[...]), right_t(weight_ref[0, :, : z.main]))
    last = weight_ref[0, :, z.main :]
    last = jnp.concatenate([last, jnp.zeros((last.shape[0], LANES - z.extra), F32)], axis=1)
    tail_weight[...] += pltpu.roll(last, z.extra * step, 1)

    @pl.when(step == z.basis - 1)
    def _():
        out_ref[...] += nt(left(tail_ref[...]), right_t(tail_weight[...]))


def conv(z, mixed, weight, base, bias):
    return pl.pallas_call(
        partial(conv_body, z),
        name="conv",
        grid=(z.basis,),
        in_specs=[
            pl.BlockSpec((z.pixels, z.main), lambda k: (0, k)),
            pl.BlockSpec((z.pixels, LANES), lambda k: (0, z.basis * z.tiles)),
            pl.BlockSpec((1, z.width, z.joined), lambda k: (k, 0, 0)),
            full((z.pixels, z.width)),
            full(bias.shape),
        ],
        out_specs=result((z.pixels, z.width)),
        out_shape=jax.ShapeDtypeStruct((z.pixels, z.width), F32),
        scratch_shapes=[pltpu.VMEM((z.width, LANES), F32)],
        compiler_params=params(44),
        cost_estimate=cost(z.pixels * z.depth * z.width, 4 * z.depth * (z.width + z.pixels)),
    )(mixed, mixed, weight, base, bias)


def mlp_body(
    z,
    info_ref,
    middle_ref,
    cot_ref,
    d_active_ref,
    weight_ref,
    bias_ref,
    gain_ref,
    shift_ref,
    kept_ref,
    sent_ref,
    active_high_ref,
    active_low_ref,
    d_pre_high_ref,
    d_pre_low_ref,
    d_bias_ref,
    second_ref,
    second_lhs,
    second_t,
    cot_t,
    tail,
):
    step = pl.program_id(0)
    main = z.main

    @pl.when(step == 0)
    def _():
        norm, _ = normalize(middle_ref[...])
        second = norm * row(gain_ref) + row(shift_ref)
        second_ref[...] = second
        second_lhs[...] = left(second[:, :main])
        second_t[...] = left(padded_t(second, z.wide)[: z.high])
        cot_t[...] = left(padded_t(cot_ref[...], z.wide)[: z.high])

    def store(out_ref, which, value, last):
        if not last:
            for i in range(z.tiles):
                out_ref[0, i * z.high : (i + 1) * z.high, :] = value[:, i * LANES : (i + 1) * LANES]
            out_ref[0, z.tiles * z.high :, :] = tail[which, step - 1]
            return
        fill = jnp.zeros((z.wide - z.high, LANES), F32)
        value = jnp.transpose(jnp.concatenate([value, fill], axis=0))[:8]
        for i in range(z.parts):
            half, place = i // (z.parts // 2), i % (z.parts // 2)
            tail[which, half, 8 * place : 8 * place + 8, :] = value[:, i * LANES : (i + 1) * LANES]

    def body(width, last):
        weight = only(z, weight_ref[:, :width], last)
        start = z.steps * main if last else pl.multiple_of((step - 1) * main, LANES)
        bias = bias_ref[pl.ds(start, z.rest if last else width)]
        bias = bias.reshape(1, bias.shape[0])
        if last:
            bias = jnp.concatenate([bias, jnp.zeros((1, width - z.rest), F32)], axis=1)
        d_active = only(z, d_active_ref[:, :width], last)
        pre = nn(second_lhs[...], right(weight[:main]))
        pre = pre + second_ref[:, main : main + 1] * weight[main : main + 1] + bias
        cdf = 0.5 * (1.0 + lax.erf(pre * np.float32(0.5**0.5)))
        pdf = jnp.exp(pre * pre * -0.5) * np.float32(1.0 / np.sqrt(2.0 * np.pi))
        active = only(z, pre * cdf, last)
        d_pre = d_active * (cdf + pre * pdf)
        high, low = split(active)
        active_high_ref[:, :width] = high
        active_low_ref[:, :width] = low
        output_grad = nn(cot_t[...], jnp.concatenate([high, low, high], axis=0))
        high, low = split(d_pre)
        d_pre_high_ref[:, :width] = high
        d_pre_low_ref[:, :width] = low
        d_bias_ref[:, :width] = jnp.sum(d_pre, axis=0, keepdims=True)
        hidden_grad = nn(second_t[...], jnp.concatenate([high, low, high], axis=0))

        @pl.when(info_ref[0] == 0)
        def _():
            store(kept_ref, 0, output_grad, last)
            store(sent_ref, 1, hidden_grad, last)

        @pl.when(info_ref[0] != 0)
        def _():
            store(sent_ref, 0, output_grad, last)
            store(kept_ref, 1, hidden_grad, last)

    pl.when(step == 0)(lambda: body(LANES, True))
    pl.when(step > 0)(lambda: body(z.main, False))


def mlp(z, info, middle, cot, d_active, weight, bias, gain, shift):
    flat = (2, z.mlp_half, LANES)
    at = lambda i: jnp.where(i == 0, z.steps, i - 1)
    hidden = pl.BlockSpec((z.pixels, z.main), lambda i, *_: (0, at(i)))
    half = pl.BlockSpec((1, z.mlp_half, LANES), lambda i, *_: (jnp.maximum(i - 1, 0), 0, 0))
    wide = pltpu.HBM((z.pixels, z.hidden), BF16)
    return pl.pallas_call(
        partial(mlp_body, z),
        name="mlp",
        grid_spec=pltpu.PrefetchScalarGridSpec(
            num_scalar_prefetch=1,
            grid=(z.steps + 1,),
            in_specs=[
                full((z.pixels, z.width)),
                full((z.pixels, z.width)),
                hidden,
                pl.BlockSpec((z.width, z.main), lambda i, *_: (0, at(i))),
                full(bias.shape),
                full(gain.shape),
                full(shift.shape),
            ],
            out_specs=[
                half,
                half,
                hidden,
                hidden,
                hidden,
                hidden,
                pl.BlockSpec((1, z.main), lambda i, *_: (0, at(i))),
            ],
            scratch_shapes=[
                pltpu.VMEM((z.pixels, z.width), F32),
                pltpu.VMEM((z.pixels, 3 * z.main), BF16),
                pltpu.VMEM((z.high, 3 * z.pixels), BF16),
                pltpu.VMEM((z.high, 3 * z.pixels), BF16),
                pltpu.VMEM((2, z.steps, 8 * z.parts // 2, LANES), F32),
            ],
        ),
        out_shape=[
            pltpu.HBM(flat, F32),
            pltpu.HBM(flat, F32),
            wide,
            wide,
            wide,
            wide,
            jax.ShapeDtypeStruct((1, z.hidden), F32),
        ],
        compiler_params=params(44),
        cost_estimate=cost(3 * z.pixels * z.width * z.hidden, 12 * z.width * z.hidden),
    )(info, middle, cot, d_active, weight, bias, gain, shift)


def middle_back_body(z, high_ref, low_ref, weight_ref, middle_ref, cot_ref, gain_ref, out_ref, out_t_ref, sums_ref, d_second):
    step = pl.program_id(0)

    @pl.when(step == 0)
    def _():
        d_second[...] = jnp.zeros_like(d_second)

    def body(width, last):
        high = only(z, high_ref[:, :width], last)
        low = only(z, low_ref[:, :width], last)
        weight = right_t(only(z, weight_ref[:, :width], last))
        d_second[...] += nt(jnp.concatenate([high, high, low], axis=1), weight)

    hidden_steps(z, body)

    @pl.when(step == z.steps)
    def _():
        norm, inverse = normalize(middle_ref[...])
        grad = d_second[...]
        sums_ref[0:1, :] = jnp.sum(grad * norm, axis=0, keepdims=True)
        sums_ref[1:2, :] = jnp.sum(grad, axis=0, keepdims=True)
        cot = cot_ref[...]
        sums_ref[3:4, :] = jnp.sum(cot, axis=0, keepdims=True)
        d_middle = cot + norm_back(grad * row(gain_ref), norm, inverse)
        sums_ref[2:3, :] = jnp.sum(d_middle, axis=0, keepdims=True)
        out_ref[...] = d_middle
        out_t_ref[...] = padded_t(d_middle, z.wide)[: z.high]


def middle_back(z, high, low, weight, middle, cot, gain):
    hidden = pl.BlockSpec((z.pixels, z.main), lambda i: (0, i))
    return pl.pallas_call(
        partial(middle_back_body, z),
        name="middle_back",
        grid=(z.steps + 1,),
        in_specs=[
            hidden,
            hidden,
            pl.BlockSpec((z.width, z.main), lambda i: (0, i)),
            full((z.pixels, z.width)),
            full((z.pixels, z.width)),
            full(gain.shape),
        ],
        out_specs=[
            full((z.pixels, z.width)),
            full((z.high, z.pixels)),
            full((4, z.width)),
        ],
        out_shape=[
            jax.ShapeDtypeStruct((z.pixels, z.width), F32),
            jax.ShapeDtypeStruct((z.high, z.pixels), F32),
            jax.ShapeDtypeStruct((4, z.width), F32),
        ],
        scratch_shapes=[pltpu.VMEM((z.pixels, z.width), F32)],
        compiler_params=params(58),
        cost_estimate=cost(z.pixels * z.width * z.hidden, 8 * z.width * z.hidden),
    )(high, low, weight, middle, cot, gain)


def output_body(z, high_ref, low_ref, weight_ref, middle_ref, bias_ref, out_ref):
    @pl.when(pl.program_id(0) == 0)
    def _():
        out_ref[...] = middle_ref[...] + row(bias_ref)

    def body(width, last):
        high = only(z, high_ref[:, :width], last)
        low = only(z, low_ref[:, :width], last)
        weight = right_t(only(z, weight_ref[:, :width], last))
        out_ref[...] += nt(jnp.concatenate([high, high, low], axis=1), weight)

    hidden_steps(z, body)


def output(z, high, low, weight, middle, bias):
    hidden = pl.BlockSpec((z.pixels, z.main), lambda i: (0, i))
    return pl.pallas_call(
        partial(output_body, z),
        name="output",
        grid=(z.steps + 1,),
        in_specs=[
            hidden,
            hidden,
            pl.BlockSpec((z.width, z.main), lambda i: (0, i)),
            full((z.pixels, z.width)),
            full(bias.shape),
        ],
        out_specs=full((z.pixels, z.width)),
        out_shape=jax.ShapeDtypeStruct((z.pixels, z.width), F32),
        compiler_params=params(58),
        cost_estimate=cost(z.pixels * z.width * z.hidden, 8 * z.width * z.hidden),
    )(high, low, weight, middle, bias)


def conv_grad_body(z, info_ref, own_ref, far_ref, own_t_ref, far_t_ref, out_ref, lhs):
    step = pl.program_id(0)
    tiles = own_ref.shape[1] // LANES

    @pl.when(step == 0)
    def _():
        lhs[...] = left(jnp.concatenate([own_t_ref[...], far_t_ref[...]], axis=1))
        used = pl.num_programs(0) * tiles * z.high
        out_ref[used:, :] = jnp.zeros((out_ref.shape[0] - used, LANES), F32)

    value = nn(lhs[...], right(jnp.concatenate([own_ref[...], far_ref[...]], axis=0)))
    for i in range(tiles):
        rows = pl.ds(pl.multiple_of((step * tiles + i) * z.high, 8), z.high)
        out_ref[rows, :] = value[:, i * LANES : (i + 1) * LANES]


def conv_grad(z, info, mixed, far_mixed, own_t, far_t):
    count = z.half // LANES // 2
    tiles = 3
    steps = count // tiles
    flat = round_up(count * z.high, 32)
    return pl.pallas_call(
        partial(conv_grad_body, z),
        name="conv_grad",
        grid_spec=pltpu.PrefetchScalarGridSpec(
            num_scalar_prefetch=1,
            grid=(steps,),
            in_specs=[
                pl.BlockSpec((z.pixels, tiles * LANES), lambda i, c: (0, (2 * c[0] + c[1]) * steps + i)),
                pl.BlockSpec((z.pixels, tiles * LANES), lambda i, c: (0, c[1] * steps + i)),
                full((z.high, z.pixels)),
                full((z.high, z.pixels)),
            ],
            out_specs=full((flat, LANES)),
            scratch_shapes=[pltpu.VMEM((z.high, 6 * z.pixels), BF16)],
        ),
        out_shape=jax.ShapeDtypeStruct((flat, LANES), F32),
        compiler_params=params(50),
        cost_estimate=cost(2 * z.pixels * z.width * count * LANES, 12 * z.pixels * count * LANES),
    )(info, mixed, far_mixed, own_t, far_t)


def mixed_back_body(z, weight_ref, dm_ref, high_ref, low_ref, lhs):
    columns, main = z.columns, z.main

    @pl.when(pl.program_id(0) == 0)
    def _():
        lhs[...] = left(dm_ref[:, :main])

    value = nn(lhs[...], right(weight_ref[0, :main, :]))
    value = value + dm_ref[:, main : main + 1] * weight_ref[0, main : main + 1, :]
    value_high, value_low = split(value)
    for b in range(z.samples):
        for r in range(z.rows):
            i = (b * z.rows + r) * columns
            lane = b * z.wide
            high_ref[r, :, lane : lane + z.joined] = value_high[i : i + columns]
            low_ref[r, :, lane : lane + z.joined] = value_low[i : i + columns]


def mixed_back(z, weight, d_middle):
    out = pl.BlockSpec((z.rows, z.columns, z.samples * z.wide), lambda i: (0, i, 0))
    shape = pltpu.HBM((z.rows, z.basis * z.columns, z.samples * z.wide), BF16)
    return pl.pallas_call(
        partial(mixed_back_body, z),
        name="mixed_back",
        grid=(z.basis,),
        in_specs=[
            pl.BlockSpec((1, z.width, z.joined), lambda i: (i, 0, 0)),
            full((z.pixels, z.width)),
        ],
        out_specs=[out, out],
        out_shape=[shape, shape],
        scratch_shapes=[pltpu.VMEM((z.pixels, 3 * z.main), BF16)],
        compiler_params=params(56),
        cost_estimate=cost(z.pixels * z.depth * z.width, 4 * z.depth * z.width),
    )(weight, d_middle)


def outer_columns(z, value):
    return jnp.concatenate([value[z.columns + LON_HALO : z.columns + 2 * LON_HALO], value[:LON_HALO]], axis=0)


def band_back_body(z, high_ref, low_ref, band_ref, out_ref, top_ref, bottom_ref, sides_ref):
    row_at = pl.program_id(0)
    columns = z.columns

    @pl.when(row_at == 0)
    def _():
        out_ref[...] = jnp.zeros_like(out_ref)

    spread = [band(band_ref[0, k : k + 1, :], columns) for k in range(z.basis)]
    spread = jnp.transpose(jnp.concatenate(spread, axis=0))[: z.taps]
    high, low = split(spread)
    top, rest = high_ref[0], low_ref[0]
    value = nn(high, top) + nn(high, rest) + nn(low, top)
    place = pl.ds(pl.multiple_of(row_at * z.span, 8), z.taps)
    for b in range(z.samples):
        out_ref[b, place, :] += value[:, b * z.wide : b * z.wide + z.joined]

    @pl.when(row_at == z.rows - 1)
    def _():
        for b in range(z.samples):
            for r in range(z.rows + 2 * LAT_HALO):
                value = out_ref[b, r * z.span : r * z.span + columns + 2 * LON_HALO, :]
                if r < LAT_HALO:
                    top_ref[b, r] = value
                elif r < z.rows + LAT_HALO:
                    sides_ref[b, r - LAT_HALO] = outer_columns(z, value)
                else:
                    bottom_ref[b, r - z.rows - LAT_HALO] = value


def band_back(z, high, low, bands):
    lanes = bands.shape[2]
    height = (z.rows + 2 * LAT_HALO) * z.span
    rim = (z.samples, LAT_HALO, z.columns + 2 * LON_HALO, z.joined)
    shapes = [(z.samples, height, z.joined), rim, rim, (z.samples, z.rows, 2 * LON_HALO, z.joined)]
    part = pl.BlockSpec((1,) + high.shape[1:], lambda i: (i, 0, 0))
    return pl.pallas_call(
        partial(band_back_body, z),
        name="band_back",
        grid=(z.rows,),
        in_specs=[part, part, pl.BlockSpec((1, z.basis, lanes), lambda i: (i, 0, 0))],
        out_specs=[full(shape) for shape in shapes],
        out_shape=[jax.ShapeDtypeStruct(shape, F32) for shape in shapes],
        compiler_params=params(56),
        cost_estimate=cost(z.pixels * z.basis * z.taps * z.joined, 8 * z.pixels * z.depth),
    )(high, low, bands)


def edge_body(z, sides_ref, above_ref, below_ref, out_ref):
    for b in range(z.samples):
        for r in range(z.rows):
            value = sides_ref[b, r]
            if r < LAT_HALO:
                value = value + outer_columns(z, above_ref[b, r])
            if r >= z.rows - LAT_HALO:
                value = value + outer_columns(z, below_ref[b, r - z.rows + LAT_HALO])
            out_ref[b, r] = value


def edge(z, sides, above, below):
    return pl.pallas_call(
        partial(edge_body, z),
        name="edge",
        out_shape=jax.ShapeDtypeStruct(sides.shape, F32),
        compiler_params=params(16),
        cost_estimate=cost(2**30, 2**22),
    )(sides, above, below)


def finish_body(
    z, padded_ref, above_ref, below_ref, sides_ref, inputs_ref, d_middle_ref, gain_ref, sums_ref, d_bias_ref, out_ref, vectors_ref, own
):
    sample = pl.program_id(0)

    @pl.when(sample == 0)
    def _():
        own[...] = jnp.zeros_like(own)

    for r in range(z.rows):
        start = (r + LAT_HALO) * z.span
        value = padded_ref[0, start : start + z.columns + 2 * LON_HALO, :]
        if r < LAT_HALO:
            value = value + above_ref[0, r]
        if r >= z.rows - LAT_HALO:
            value = value + below_ref[0, r - z.rows + LAT_HALO]
        middle = value[2 * LON_HALO : z.columns]
        low = value[LON_HALO : 2 * LON_HALO] + sides_ref[0, r, :LON_HALO]
        high = value[z.columns : z.columns + LON_HALO] + sides_ref[0, r, LON_HALO:]
        grad = jnp.concatenate([low, middle, high], axis=0)[:, : z.width]
        norm, inverse = normalize(inputs_ref[0, r])
        own[0:1, :] += jnp.sum(grad * norm, axis=0, keepdims=True)
        own[1:2, :] += jnp.sum(grad, axis=0, keepdims=True)
        grad = norm_back(grad * row(gain_ref), norm, inverse)
        out_ref[0, r] = d_middle_ref[0, r] + grad

    @pl.when(sample == pl.num_programs(0) - 1)
    def _():
        vectors_ref[...] = jnp.zeros_like(vectors_ref)
        row = 0
        rows = [(sums_ref, 2), (own, 0), (own, 1), (sums_ref, 0), (sums_ref, 1), (d_bias_ref, 0), (sums_ref, 3)]
        for ref, at in rows:
            size = ref.shape[1]
            for i in range(0, size, LANES):
                end = min(i + LANES, size)
                vectors_ref[row : row + 1, : end - i] = ref[at : at + 1, i:end]
                row += 1


def finish(z, padded, above, below, sides, inputs, d_middle, gain, sums, d_bias):
    shape = (z.samples, z.rows, z.columns, z.width)
    count = round_up(6 * pl.cdiv(z.width, LANES) + pl.cdiv(z.hidden, LANES), 16)

    def part(array):
        size = array.shape[1:]
        return pl.BlockSpec((1,) + size, lambda b: (b,) + (0,) * len(size))

    d_middle = d_middle.reshape(shape)
    arrays = [padded, above, below, sides, inputs, d_middle]
    return pl.pallas_call(
        partial(finish_body, z),
        name="finish",
        grid=(z.samples,),
        in_specs=[part(a) for a in arrays] + [full(gain.shape), full(sums.shape), full(d_bias.shape)],
        out_specs=[part(inputs), full((count, LANES))],
        out_shape=[jax.ShapeDtypeStruct(shape, F32), jax.ShapeDtypeStruct((count, LANES), F32)],
        scratch_shapes=[pltpu.VMEM((8, z.width), F32)],
        compiler_params=params(60),
        cost_estimate=cost(2**30, 2**22),
    )(*arrays, gain, sums, d_bias)


def conv_place_body(z, which, first, count, info_ref, *refs):
    number = len(which)
    pieces, (out_ref, held, narrow, sems) = refs[:number], refs[-4:]
    main_tiles = z.basis * z.tiles
    with_extra = first + 2 * count == z.half // LANES
    used = count * z.high

    def get(i):
        return pltpu.make_async_copy(pieces[i].at[pl.ds(0, used), :], held.at[i], sems.at[i])

    def tile(i, t):
        return (info_ref[which[i]] // 2) * (z.half // LANES) + first + (info_ref[which[i]] % 2) * count + t

    def put(i, t):
        at = tile(i, t)
        lanes = pl.ds(pl.multiple_of(at % z.tiles * LANES, LANES), LANES)
        return pltpu.make_async_copy(
            held.at[i, pl.ds(t * z.high, z.width), :],
            out_ref.at[at // z.tiles, :, lanes],
            sems.at[number + i * count + t],
        )

    def put_extra(k):
        return pltpu.make_async_copy(
            narrow.at[k], out_ref.at[k, :, pl.ds(z.main, z.extra)], sems.at[number * (1 + count) + k]
        )

    for i in range(number):
        get(i).start()
    for i in range(number):
        get(i).wait()
        for t in range(count):
            is_main = tile(i, t) < main_tiles

            @pl.when(is_main)
            def _():
                put(i, t).start()

            if with_extra and t == count - 1:

                @pl.when(jnp.logical_not(is_main))
                def _():
                    for k in range(z.basis):
                        value = held[i, t * z.high : (t + 1) * z.high, :]
                        value = value if k == 0 else pltpu.roll(value, LANES - z.extra * k, 1)
                        narrow[k] = value[: z.width, : z.extra]
                        put_extra(k).start()

    for i in range(number):
        if with_extra:

            @pl.when(tile(i, count - 1) >= main_tiles)
            def _():
                for k in range(z.basis):
                    put_extra(k).wait()

        for t in range(count):

            @pl.when(tile(i, t) < main_tiles)
            def _():
                put(i, t).wait()


def conv_place(z, places, which, first, count, pieces, onto):
    anywhere = pl.BlockSpec(memory_space=pl.ANY)
    operands = [places, *pieces]
    aliases = {}
    if onto is not None:
        operands.append(onto)
        aliases = {1 + len(which): 0}
    return pl.pallas_call(
        partial(conv_place_body, z, which, first, count),
        name="conv_place",
        grid_spec=pltpu.PrefetchScalarGridSpec(
            num_scalar_prefetch=1,
            grid=(),
            in_specs=[anywhere] * (len(operands) - 1),
            out_specs=anywhere,
            scratch_shapes=[
                pltpu.VMEM((len(which), count * z.high, LANES), F32),
                pltpu.VMEM((z.basis, z.width, z.extra), F32),
                pltpu.SemaphoreType.DMA((len(which) * (1 + count) + z.basis,)),
            ],
        ),
        out_shape=jax.ShapeDtypeStruct((z.basis, z.width, z.joined), F32),
        input_output_aliases=aliases,
        compiler_params=params(16),
        cost_estimate=cost(2**30, 2**24),
    )(*operands)


def mlp_place_body(z, info_ref, own_ref, far_ref, output_ref, hidden_ref, held, narrow, sems):
    main_tiles = 2 * z.tiles

    def place(refs):
        gets = []
        for i, ref in enumerate(refs):
            for half in range(2):
                rows = pl.ds(half * z.mlp_half, z.mlp_half)
                gets.append(pltpu.make_async_copy(ref.at[rows, :], held.at[i, half], sems.at[2 * i + half]))
                gets[-1].start()
        puts = []
        for i, out_ref in enumerate((output_ref, hidden_ref)):
            for t in range(main_tiles):
                half = t // z.tiles
                if t % z.tiles == 0:
                    gets[2 * i + half].wait()
                puts.append(
                    pltpu.make_async_copy(
                        held.at[i, half, pl.ds(t % z.tiles * z.high, z.width), :],
                        out_ref.at[:, pl.ds(t * LANES, LANES)],
                        sems.at[8 + i * main_tiles + t],
                    )
                )
                puts[-1].start()
            start = z.tiles * z.high
            parts = [
                held[i, half, start + 8 * j : start + 8 * j + 8, :] for half in range(2) for j in range(z.parts // 2)
            ]
            value = jnp.concatenate([jnp.concatenate(parts, axis=1)] * (LANES // 8), axis=0)
            narrow[i] = jnp.transpose(value)[: z.width, : z.rest]
            puts.append(
                pltpu.make_async_copy(
                    narrow.at[i],
                    out_ref.at[:, pl.ds(main_tiles * LANES, z.rest)],
                    sems.at[8 + 2 * main_tiles + i],
                )
            )
            puts[-1].start()
        for c in puts:
            c.wait()

    pl.when(info_ref[0] == 0)(lambda: place((own_ref, far_ref)))
    pl.when(info_ref[0] != 0)(lambda: place((far_ref, own_ref)))


def mlp_place(z, info, own, far):
    shape = jax.ShapeDtypeStruct((z.width, z.hidden), F32)
    anywhere = pl.BlockSpec(memory_space=pl.ANY)
    return pl.pallas_call(
        partial(mlp_place_body, z),
        name="mlp_place",
        grid_spec=pltpu.PrefetchScalarGridSpec(
            num_scalar_prefetch=1,
            grid=(),
            in_specs=[anywhere, anywhere],
            out_specs=[anywhere, anywhere],
            scratch_shapes=[
                pltpu.VMEM((2, 2, z.mlp_half, LANES), F32),
                pltpu.VMEM((2, z.width, z.rest), F32),
                pltpu.SemaphoreType.DMA((4 * z.tiles + 10,)),
            ],
        ),
        out_shape=[shape, shape],
        compiler_params=params(16),
        cost_estimate=cost(2**30, 2**22),
    )(info, own, far)


def axis_size(axes):
    size = 1
    for axis in axes:
        size *= lax.axis_size(axis)
    return size


def pairs(lats, lons, target):
    found = []
    for lat in range(lats):
        for lon in range(lons):
            to_lat, to_lon = target(lat, lon)
            found.append((lat * lons + lon, to_lat * lons + to_lon))
    return found


class GridSum:
    def __init__(self):
        lats, lons = axis_size(LAT), axis_size(LON)
        lat, lon = lax.axis_index(LAT), lax.axis_index(LON)
        over = partial(pairs, lats, lons)
        self.core = lat % 2
        self.cores = over(lambda a, o: (a ^ 1, o))
        self.first = over(lambda a, o: (a ^ 2, o) if a % 2 else (a, o ^ 1))
        self.second = over(lambda a, o: (a, o ^ 1) if a % 2 else (a ^ 2, o))
        self.third = over(lambda a, o: (a ^ 4, o))
        lon_bit, lat_bit = lon % 2, lat // 2 % 2
        self.first_bit = jnp.where(self.core == 0, lon_bit, lat_bit)
        self.second_bit = jnp.where(self.core == 0, lat_bit, lon_bit)
        self.third_bit = lat // 4 % 2
        far_bit = jnp.where(self.core == 0, lat_bit, lon_bit)
        mine, other = 2 * self.core, 2 * (1 - self.core)
        self.places = jnp.stack(
            [mine + self.first_bit, mine + 1 - self.first_bit, other + far_bit, other + 1 - far_bit]
        ).astype(jnp.int32)
        self.others = []
        bit = 8
        while bit < lats:
            self.others.append(over(lambda a, o, bit=bit: (a ^ bit, o)))
            bit *= 2
        bit = 2
        while bit < lons:
            self.others.append(over(lambda a, o, bit=bit: (a, o ^ bit)))
            bit *= 2

    def swap(self, value, where):
        return lax.ppermute(value, AXES, where)

    def all(self, value, where):
        return value + self.swap(value, where)


class Order:
    def __init__(self):
        self.last = ()
        self.held = True

    def use(self, value):
        if not self.held:
            return value
        value, self.last = lax.optimization_barrier((value, self.last))
        return value

    def mark(self, value):
        if self.held:
            self.last = (value,)
        return value

    def wait(self, value):
        return self.mark(self.use(value))

    def run(self, function, *values):
        return self.mark(function(*self.use(values)))


def sum_rows(size, index, arrays, vectors):
    count = 0 if vectors is None else vectors.shape[0]

    def body(index_ref, *refs):
        out_ref = refs[-1]
        total = refs[0][...]
        for ref in refs[1 : len(arrays)]:
            total = total + ref[...]
        out_ref[:size, :] = total
        if vectors is not None:
            out_ref[size:, :] = refs[len(arrays)][...]

    more = [] if vectors is None else [vectors]
    blocks = [pl.BlockSpec((size, LANES), lambda g, p, i=i: (p[i], 0)) for i in range(len(arrays))]
    return pl.pallas_call(
        body,
        name="sum_rows",
        grid_spec=pltpu.PrefetchScalarGridSpec(
            num_scalar_prefetch=1,
            grid=(1,),
            in_specs=blocks + [full(v.shape) for v in more],
            out_specs=full((size + count, LANES)),
        ),
        out_shape=jax.ShapeDtypeStruct((size + count, LANES), F32),
        compiler_params=params(16),
        cost_estimate=cost(2**30, 2**24),
    )(index, *arrays, *more)


def join_rows(size, bit, value, far):
    rows = value.shape[0] + size

    def body(bit_ref, value_ref, far_ref, out_ref):
        at = bit_ref[0]
        out_ref[pl.ds(pl.multiple_of(at * size, 8), size), :] = value_ref[:size, :]
        out_ref[pl.ds(pl.multiple_of((1 - at) * size, 8), size), :] = far_ref[:size, :]
        if rows > 2 * size:
            out_ref[2 * size :, :] = value_ref[size:, :] + far_ref[size:, :]

    return pl.pallas_call(
        body,
        name="join_rows",
        grid_spec=pltpu.PrefetchScalarGridSpec(
            num_scalar_prefetch=1,
            grid=(1,),
            in_specs=[full(value.shape), full(far.shape)],
            out_specs=full((rows, LANES)),
        ),
        out_shape=jax.ShapeDtypeStruct((rows, LANES), F32),
        compiler_params=params(16),
        cost_estimate=cost(2**30, 2**21),
    )(bit.reshape(1).astype(jnp.int32), value, far)


def add_rows(value, far, start=0):
    def body(value_ref, far_ref, out_ref):
        out_ref[...] = value_ref[...] + far_ref[start:, :]

    return pl.pallas_call(
        body,
        name="add_rows",
        out_shape=jax.ShapeDtypeStruct(value.shape, F32),
        compiler_params=params(16),
        cost_estimate=cost(2**30, 2**24),
    )(value, far)


def sum_tails(start, arrays):
    rows = arrays[0].shape[0] - start
    blocks = start % rows == 0

    def body(*refs):
        total = 0.0
        for ref in refs[:-1]:
            total = total + (ref[...] if blocks else ref[start:, :])
        refs[-1][...] = total

    spec = pl.BlockSpec((rows, LANES), lambda i: (start // rows, 0)) if blocks else full(arrays[0].shape)
    return pl.pallas_call(
        body,
        name="sum_tails",
        grid=(1,),
        in_specs=[spec] * len(arrays),
        out_specs=full((rows, LANES)),
        out_shape=jax.ShapeDtypeStruct((rows, LANES), F32),
        compiler_params=params(24),
        cost_estimate=cost(2**30, 2**22),
    )(*arrays)


class Chunk:
    def __init__(self, total, order, name, sent, kept):
        self.total, self.order, self.name = total, order, name
        self.terms, self.size = [(kept, 0)], sent.shape[0]
        self.vectors = None
        self.send("scatter_first", order.wait(sent), total.first)

    def send(self, step, value, where):
        with jax.named_scope(f"{self.name}_{step}"):
            self.value, self.far = value, self.total.swap(value, where)

    def take(self, index):
        arrays = [value for value, _ in self.terms]
        at = jnp.stack([jnp.asarray(index(at), jnp.int32) for _, at in self.terms])
        return self.order.run(partial(sum_rows, self.size), at, arrays, None)

    def halve(self, step, where, bit):
        self.terms.append((self.far, 0))
        self.size //= 2
        sent = self.take(lambda at: 2 * at + 1 - bit)
        self.terms = [(value, 2 * at + bit) for value, at in self.terms]
        self.send(step, sent, where)

    def join(self, bit):
        self.value = self.order.run(partial(join_rows, self.size), bit, self.value, self.far)
        self.size *= 2

    def scatter_second(self):
        self.halve("scatter_second", self.total.second, self.total.second_bit)

    def across_first(self):
        self.halve("across_first", self.total.third, self.total.third_bit)

    def across_second(self):
        self.terms.append((self.far, 0))
        self.value = self.take(lambda at: at)
        for where in self.total.others[:-1]:
            self.send("across", self.value, where)
            self.value = self.order.run(add_rows, self.value, self.far)
        self.send("across_second", self.value, self.total.others[-1])

    def across_third(self):
        both = [self.value, self.far]
        value = self.order.run(partial(sum_rows, self.size), jnp.zeros((2,), jnp.int32), both, self.vectors)
        self.send("across_third", value, self.total.third)

    def gather_second(self):
        self.join(self.total.third_bit)
        self.send("gather_second", self.value, self.total.second)

    def gather_first(self):
        self.join(self.total.second_bit)
        self.send("gather_first", self.value, self.total.first)
        with jax.named_scope(f"{self.name}_near_core"):
            self.near = self.total.swap(self.value, self.total.cores)

    def gather_whole(self):
        self.join(self.total.first_bit)
        with jax.named_scope(f"{self.name}_near_core"):
            self.near = self.total.swap(self.value, self.total.cores)

    def gather_core(self):
        self.far = self.order.wait(self.far)
        with jax.named_scope(f"{self.name}_gather_core"):
            self.last = self.total.swap(self.far, self.total.cores)

    def pieces(self):
        return self.value, self.far, self.near, self.last


def after(value, *others):
    return lax.optimization_barrier((value, others))[0]


def rows_of(vector):
    size = round_up(vector.shape[0], LANES)
    return jnp.pad(vector, (0, size - vector.shape[0])).reshape(-1, LANES)


def moved(value, axis, steps, cycle):
    count = axis_size(axis)
    if cycle:
        where = [(i, (i + steps) % count) for i in range(count)]
    else:
        where = [(i, i + steps) for i in range(max(0, -steps), min(count, count - steps))]
    return lax.ppermute(value, axis, where)


def edges(sides, down):
    lats, lons = axis_size(LAT), axis_size(LON)

    def shifted(value, steps):
        where = [
            (lat * lons + lon, (lat + down) * lons + (lon + steps) % lons)
            for lat in range(max(0, -down), min(lats, lats - down))
            for lon in range(lons)
        ]
        return lax.ppermute(value, AXES, where)

    if lons == 2:
        return shifted(sides, 1)
    return jnp.concatenate([shifted(sides[:, :, :LON_HALO], 1), shifted(sides[:, :, LON_HALO:], -1)], axis=2)


def local(
    inputs,
    noise_field,
    basis_values,
    row_reach,
    conv_weight,
    conv_bias,
    first_gain,
    first_shift,
    second_gain,
    second_shift,
    hidden_weight,
    hidden_bias,
    output_weight,
    output_bias,
    cotangent,
):
    z = Sizes(inputs, noise_field, conv_weight, hidden_weight)
    total = GridSum()
    lat, lats = lax.axis_index(LAT), axis_size(LAT)
    info = jnp.stack([total.core, (lat > 0).astype(jnp.int32), (lat < lats - 1).astype(jnp.int32)])
    rows, columns, width = z.rows, z.columns, z.width
    flat = (z.pixels, width)
    cot = cotangent.reshape(flat)
    conv_weight = jnp.transpose(conv_weight, (0, 2, 1))
    output_weight = jnp.transpose(output_weight)

    noise = jnp.transpose(noise_field, (0, 1, 3, 2))
    top, bottom, top_sides, bottom_sides, sides = cut(z, inputs, noise)
    below, above = moved(top, LAT, -1, False), moved(bottom, LAT, 1, False)
    sides = [edges(bottom_sides, 1), edges(top_sides, -1), edges(sides, 0)]
    d_active = active_back(z, cot, output_weight)
    bands, plain_bands = band_rows(z, basis_values, row_reach)
    above, below, sides = after((above, below, sides), d_active)
    mixed, other = mix(z, info, bands, inputs, noise, above, below, sides, first_gain, first_shift)
    far_mixed = total.swap(other, total.cores)
    middle = conv(z, mixed, conv_weight, inputs.reshape(flat), conv_bias)
    kept, sent, active_high, active_low, d_pre_high, d_pre_low, d_hidden_bias = mlp(
        z, info, middle, cot, d_active, hidden_weight, hidden_bias, second_gain, second_shift
    )
    order = Order()
    arrived = total.swap(sent, total.cores)

    d_middle, d_middle_t, sums = order.run(
        partial(middle_back, z), d_pre_high, d_pre_low, hidden_weight, middle, cot, second_gain
    )
    far_t = total.swap(d_middle_t, total.cores)

    bit = total.first_bit
    kept, arrived = kept.reshape(-1, LANES), arrived.reshape(-1, LANES)
    add_half = lambda k, r, w: sum_rows(z.mlp_half, jnp.stack([w, w]).astype(jnp.int32), [k, r], None)
    m = Chunk(total, order, "m", order.run(add_half, kept, arrived, 1 - bit), None)
    m.terms = [(kept, bit), (arrived, bit)]
    half = lambda which: order.run(
        lambda *v: conv_grad(z, jnp.stack([total.core, which]), *v), mixed, far_mixed, d_middle_t, far_t
    )
    c = Chunk(total, order, "c", half(1 - bit), None)
    c.terms = [(half(bit), 0)]
    m.scatter_second()
    d_mixed = order.run(partial(mixed_back, z), conv_weight, d_middle)
    m.across_first()
    c.scatter_second()
    m.across_second()
    d_padded, top, bottom, sides = order.run(partial(band_back, z), *d_mixed, plain_bands)
    c.across_first()
    m.across_third()
    top, bottom = order.wait((top, bottom))
    from_below = moved(top, LAT, -1, False)
    from_above = moved(bottom, LAT, 1, False)
    block_output = order.run(
        partial(output, z), active_high, active_low, output_weight, middle, output_bias
    )
    m.gather_second()
    c.across_second()
    outer = order.run(partial(edge, z), sides, from_above, from_below)
    from_sides = edges(outer, 0)
    input_grad, vectors = order.run(
        partial(finish, z), d_padded, from_above, from_below, from_sides, inputs, d_middle, first_gain, sums, d_hidden_bias
    )

    c.vectors = vectors
    c.across_third()
    m.gather_first()
    c.gather_second()
    m.gather_whole()
    c.gather_first()
    place = partial(conv_place, z, total.places)
    count = z.half // LANES // 2
    conv_weight_grad = order.run(lambda *v: place((0, 2), 0, count, v, None), c.value, c.near)
    output_weight_grad, hidden_weight_grad = order.run(lambda *v: mlp_place(z, info, *v), m.value, m.near)
    c.gather_core()
    place_far = lambda *v: place((1,), 0, count, v[:1], v[1])
    place_last = lambda *v: place((3,), 0, count, v[:1], v[1])
    conv_weight_grad = order.run(place_far, c.far, conv_weight_grad)
    vectors = order.run(lambda *v: sum_tails(c.size, v), *c.pieces())
    far_vectors = total.swap(vectors, total.others[0])
    conv_weight_grad = order.run(place_last, c.last, conv_weight_grad)
    vectors = order.run(add_rows, vectors, far_vectors)
    for where in total.others[1:]:
        vectors = order.run(add_rows, vectors, total.swap(vectors, where))
    found, start = [], 0
    for size in (width,) * 5 + (z.hidden, width):
        count = pl.cdiv(size, LANES)
        found.append(vectors[start : start + count].reshape(-1)[:size])
        start += count
    conv_weight_grad = jnp.transpose(conv_weight_grad, (0, 2, 1))
    output_weight_grad = jnp.transpose(output_weight_grad)
    conv_bias_grad, first_gain_grad, first_shift_grad, second_gain_grad, second_shift_grad = found[:5]
    hidden_bias_grad, output_bias_grad = found[5:]
    return (
        block_output.reshape(inputs.shape),
        input_grad,
        conv_weight_grad,
        conv_bias_grad,
        first_gain_grad,
        first_shift_grad,
        second_gain_grad,
        second_shift_grad,
        hidden_weight_grad,
        hidden_bias_grad,
        output_weight_grad,
        output_bias_grad,
    )


def solution(mesh):
    lats, lons = mesh.shape["lat"], mesh.shape["lon"]
    fine = Mesh(mesh.devices.reshape(lats // 4, 2, 2, lons // 2, 2), AXES)
    grid = P(None, LAT, LON, None)
    weights = (P(),) * 10
    in_specs = (grid, grid, P(LAT, None, None, None), P(LAT)) + weights + (grid,)
    out_specs = (grid, grid) + weights
    return jax.shard_map(local, mesh=fine, in_specs=in_specs, out_specs=out_specs, check_vma=False)
```
